32 devices in a mesh: ep: 16 (over z, x, core), dp: 2 (over y).
Axes of the slice: x: 2, y: 2, z: 4, core: 2. Of those that a mesh axis runs over, the one named last changes fastest.
Arguments:
- tokens: bfloat16 [4096, 2048], P(('ep', 'dp')), may hold values from -6 to 6
- routes: int32 [4096, 8], P(('ep', 'dp')), may hold values from 0 to 15, as said below
- gates: bfloat16 [4096, 8], P(('ep', 'dp')), may hold values from 0.19921875 to 1
- w_gate: bfloat16 [16, 2048, 768], P('ep'), may hold values from -0.125 to 0.125
- w_up: bfloat16 [16, 2048, 768], P('ep'), may hold values from -0.125 to 0.125
- w_down: bfloat16 [16, 768, 2048], P('ep'), may hold values from -0.21875 to 0.21875
- score_head: float32 [2048], replicated, may hold values from -0.125 to 0.125
- doc_ids: int32 [32], P(('ep', 'dp')), may hold values from 0 to 7, never falling along the last dimension, each value on 1 to 8 neighbouring positions
Outputs:
- mixed: bfloat16 [4096, 2048], P(('ep', 'dp'))
- doc_scores: float32 [3, 8], replicated
The draws below stay inside these ranges and needn't reach their ends.
Inputs may be any that keep to these rules, and one draw needn't show every extreme that they name: `routes`: each row names 8 different experts; among the rows of one device no expert is named more than 96 times. `doc_ids`: never falling along the passages; every document has 1 to 8 passages.
All inputs are finite; a program needn't handle non-finite values.
Results may differ from the reference program's by a relative error of at most 0.0058.
Values may be sent and summed in bfloat16 or wider, within the bound.
No kernel may reach another device: no remote copies, remote signals or barrier semaphores. Data moves between devices by JAX's collectives and lax.ppermute only.
A program may use at most 64 MiB of HBM per device.

```python
import math
import jax
import jax.numpy as jnp
import numpy as np
from jax import lax

D = 2048
FF = 768
TOP = 8
PASSAGE = 128
DOC_MOST = 8
TOK_DEV = 128
EXPERTS = 16
CAP = 96
TOKENS = 4096
PASSAGES = 32
DOCS = 8
N_EP = 16
N_DP = 2


def route_block(block_key, hot):
    row_pos = jnp.arange(TOK_DEV, dtype=jnp.int32)[:, None]
    column_pos = jnp.arange(TOP, dtype=jnp.int32)[None, :]
    lower = jnp.where(column_pos == 0, -1, row_pos * (TOP - 1) + column_pos - 1)
    upper = CAP * (TOP - 1) + (row_pos - CAP) * TOP + column_pos
    position = jnp.where(row_pos < CAP, lower, upper).astype(jnp.int32)
    others = jax.random.permutation(jax.random.fold_in(block_key, 1), EXPERTS - 1).astype(jnp.int32)
    listed = (others + (others >= hot).astype(jnp.int32)).astype(jnp.int32)
    picks = listed[jnp.maximum(position, 0) % (EXPERTS - 1)]
    picks = jnp.where(position < 0, hot, picks).astype(jnp.int32)
    row_order = jax.random.permutation(jax.random.fold_in(block_key, 2), TOK_DEV).astype(jnp.int32)
    picks = picks[row_order]
    column_keys = jax.random.split(jax.random.fold_in(block_key, 3), TOK_DEV)
    column_order = jax.vmap(lambda one_key: jax.random.permutation(one_key, TOP))(column_keys).astype(jnp.int32)
    return jnp.take_along_axis(picks, column_order, axis=1).astype(jnp.int32)


def draw_routes(key, part):
    block_count = TOKENS // TOK_DEV
    first_hot = jax.random.randint(jax.random.fold_in(key, 11), (), 0, EXPERTS).astype(jnp.int32)
    block_index = jnp.arange(block_count, dtype=jnp.int32)
    group = block_index % N_DP
    hot_list = ((first_hot + group * (EXPERTS // N_DP)) % EXPERTS).astype(jnp.int32)
    block_keys = jax.vmap(lambda index: jax.random.fold_in(jax.random.fold_in(key, 17), index))(block_index)
    blocks = jax.vmap(route_block)(block_keys, hot_list)
    return blocks.reshape(TOKENS, TOP).astype(jnp.int32)


def levels(rng, extent, pieces, least, high):
    def one(dim, blocks):
        draws = jax.random.uniform(jax.random.fold_in(jax.random.fold_in(rng, 6), dim), (blocks,), jnp.float32, least / len(pieces), high / len(pieces))
        return jnp.repeat(jnp.exp(draws), extent[dim] // blocks).reshape((-1,) + (1,) * (len(extent) - dim - 1))

    factor_of = one(*pieces[0])
    for cut in pieces[1:]:
        factor_of = factor_of * one(*cut)
    return factor_of


def profile(amount, total, most, skew):
    weights = [(1 << 20) // math.isqrt(rank ** skew) + 1 for rank in range(2, amount + 1)]
    rest, counts = total - most - (amount - 1), [1] * (amount - 1)
    while rest > 0:
        candidates = [i for i in range(amount - 1) if counts[i] < most]
        pool, left = sum([weights[i] for i in candidates]), rest
        for i in candidates:
            more = min(most - counts[i], max(1, left * weights[i] // pool), rest)
            counts[i] = counts[i] + more
            rest = rest - more
    return np.array([most] + counts)


def ragged(rng, amount, total, reach, skew):
    if amount == 2:
        one = jax.random.randint(rng, (), max(1, total - reach), min(reach, total - 1) + 1)
        return jnp.stack([one, total - one])
    tallies = jnp.asarray(profile(amount, total, reach, skew), jnp.int32)
    couples = (amount - 1) // 2
    source_of, sink = tallies[1:1 + 2 * couples:2], tallies[2:2 + 2 * couples:2]
    slack = jnp.minimum(source_of - 1, reach - sink)
    shifted = jax.random.randint(jax.random.fold_in(rng, 1), (couples,), 0, 1 << 20) % (slack + 1)
    tallies = tallies.at[1:1 + 2 * couples:2].set(source_of - shifted).at[2:2 + 2 * couples:2].set(sink + shifted)
    return tallies[jax.random.permutation(jax.random.fold_in(rng, 2), amount)]


def noise(stream_key, dims, spread, most, cuts=(), held_as=jnp.bfloat16):
    array = jax.random.normal(stream_key, dims, jnp.float32) * spread
    if len(cuts) > 0:
        array = levels(stream_key, dims, cuts, -0.22, 0.18) * array
    return jnp.clip(array, min=-most, max=most).astype(held_as)


def setup_inputs(seed: int = 0) -> dict:
    arg_keys = jax.random.split(jax.random.key(seed), 9)
    return {
        "tokens": noise(arg_keys[0], (TOKENS, D), 1.0, 6.0, ((0, 32),)),
        "routes": draw_routes(jax.random.fold_in(arg_keys[8], 71), 0),
        "gates": jnp.clip(jnp.exp(math.log(1.0) - 1.6133518 * jax.random.uniform(arg_keys[2], (TOKENS, TOP), jnp.float32) ** levels(arg_keys[2], (TOKENS, TOP), ((0, 32),), -0.2, 0.2)), 0.19921875, 1.0).astype(jnp.bfloat16),
        "w_gate": noise(arg_keys[3], (EXPERTS, D, FF), D ** -0.5, 0.125, ((0, 16),)),
        "w_up": noise(arg_keys[4], (EXPERTS, D, FF), D ** -0.5, 0.125, ((0, 16),)),
        "w_down": noise(arg_keys[5], (EXPERTS, FF, D), FF ** -0.5, 0.21875, ((0, 16),)),
        "score_head": noise(arg_keys[6], (D,), D ** -0.5, 0.125, (), jnp.float32),
        "doc_ids": jnp.searchsorted(jnp.cumsum(ragged(arg_keys[7], DOCS, PASSAGES, DOC_MOST, 2)), jnp.arange(PASSAGES), side="right").astype(jnp.int32),
    }


block_rows = 256

def expert_rows(rows, gate_rows, wg_single, wu_single, wd_single):
    gate_part = jnp.dot(rows, wg_single, preferred_element_type=jnp.float32)
    up_part = jnp.dot(rows, wu_single, preferred_element_type=jnp.float32)
    hidden = (jax.nn.silu(gate_part) * up_part).astype(jnp.bfloat16)
    result = jnp.dot(hidden, wd_single, preferred_element_type=jnp.float32)
    return (gate_rows.astype(jnp.float32)[:, None] * result).astype(jnp.bfloat16)

def reference(tokens, routes, gates, w_gate, w_up, w_down, score_head, doc_ids):
    flat_routes = routes.reshape(-1)
    flat_gates = gates.reshape(-1)
    span = -(-(CAP * N_EP * N_DP) // block_rows) * block_rows

    def per_expert(total, expert):
        chosen_mask = flat_routes == expert
        live_count = jnp.sum(chosen_mask.astype(jnp.int32))
        chosen = jnp.nonzero(chosen_mask, size=span, fill_value=0)[0].astype(jnp.int32)
        wg_single = w_gate[expert]
        wu_single = w_up[expert]
        wd_single = w_down[expert]

        def keep_going(state):
            return state[0] * block_rows < live_count

        def one_block(state):
            block_index, running = state
            pair_index = lax.dynamic_slice_in_dim(chosen, block_index * block_rows, block_rows)
            valid = block_index * block_rows + jnp.arange(block_rows, dtype=jnp.int32) < live_count
            token_index = (pair_index // TOP).astype(jnp.int32)
            weighted = expert_rows(tokens[token_index], flat_gates[pair_index], wg_single, wu_single, wd_single)
            addend = jnp.where(valid[:, None], weighted.astype(jnp.float32), jnp.float32(0.0))
            return (block_index + 1, running.at[token_index].add(addend))
        _, total = lax.while_loop(keep_going, one_block, (jnp.int32(0), total))
        return (total, None)
    start_total = jnp.zeros((TOKENS, D), jnp.float32)
    total, _ = lax.scan(per_expert, start_total, jnp.arange(EXPERTS, dtype=jnp.int32))
    mixed = total.astype(jnp.bfloat16)
    token_score = jnp.dot(mixed.astype(jnp.float32), score_head, precision=lax.Precision.HIGHEST)
    passage_score = token_score.reshape(-1, PASSAGE).sum(axis=1) / math.sqrt(PASSAGE)
    member = doc_ids[:, None] == jnp.arange(DOCS, dtype=jnp.int32)[None, :]
    column = passage_score[:, None]
    max_score = jnp.where(member, column, -1e+30).max(axis=0)
    sum_score = jnp.where(member, column, 0.0).sum(axis=0)
    passage_index = jnp.arange(PASSAGES, dtype=jnp.int32)[:, None]
    first_index = jnp.where(member, passage_index, PASSAGES).min(axis=0)
    first_score = jnp.where(member & (passage_index == first_index[None, :]), column, 0.0).sum(axis=0)
    return (mixed, jnp.stack([max_score, first_score, sum_score]))
```

```python
import math

import jax
import jax.numpy as jnp
from jax import lax
from jax.sharding import PartitionSpec as P

TOP = 8
PASSAGE = 128


def expert_rows(rows, gate_rows, wg_single, wu_single, wd_single):
    gate_part = jnp.dot(rows, wg_single, preferred_element_type=jnp.float32)
    up_part = jnp.dot(rows, wu_single, preferred_element_type=jnp.float32)
    hidden = (jax.nn.silu(gate_part) * up_part).astype(jnp.bfloat16)
    result = jnp.dot(hidden, wd_single, preferred_element_type=jnp.float32)
    return (gate_rows.astype(jnp.float32)[:, None] * result).astype(jnp.bfloat16)


def run_expert(slot_rows, slot_gates, wg_single, wu_single, wd_single):
    width = slot_rows.shape[-1]
    rows = slot_rows.reshape(-1, width)
    gate_rows = slot_gates.reshape(-1)
    result = expert_rows(rows, gate_rows, wg_single, wu_single, wd_single)
    return result.reshape(slot_rows.shape)


def slot_shards(tokens, routes, gates, w_gate, w_up, w_down, score_head, doc_ids):
    tok_dev, width = tokens.shape
    experts = lax.axis_size("ep")
    capacity = min(tok_dev, 3 * tok_dev * TOP // (2 * experts))
    flat_routes = routes.reshape(-1)
    onehot = (flat_routes[:, None] == jnp.arange(experts, dtype=jnp.int32)[None, :]).astype(
        jnp.int32
    )
    ranked = jnp.cumsum(onehot, axis=0)
    slot = jnp.sum(ranked * onehot, axis=1) - 1
    destination = flat_routes * capacity + slot
    repeated = jnp.repeat(tokens, TOP, axis=0)
    send_rows = jnp.zeros((experts * capacity, width), jnp.bfloat16).at[destination].set(repeated)
    send_gates = (
        jnp.zeros((experts * capacity,), jnp.bfloat16).at[destination].set(gates.reshape(-1))
    )
    recv_rows, recv_gates = (
        lax.all_to_all(
            send_rows.reshape(experts, capacity, width),
            "ep",
            split_axis=0,
            concat_axis=0,
            tiled=True,
        ),
        lax.all_to_all(
            send_gates.reshape(experts, capacity), "ep", split_axis=0, concat_axis=0, tiled=True
        ),
    )
    wg_single = w_gate[0]
    wu_single = w_up[0]
    wd_single = w_down[0]
    results = run_expert(recv_rows, recv_gates, wg_single, wu_single, wd_single)
    returned = lax.all_to_all(results, "ep", split_axis=0, concat_axis=0, tiled=True)
    returned_flat = returned.reshape(experts * capacity, width)
    gathered = returned_flat[destination].astype(jnp.float32).reshape(tok_dev, TOP, width)
    mixed = jnp.sum(gathered, axis=1).astype(jnp.bfloat16)
    token_score = jnp.dot(mixed.astype(jnp.float32), score_head, precision=lax.Precision.HIGHEST)
    passage_score = token_score.reshape(-1, PASSAGE).sum(axis=1) / math.sqrt(PASSAGE)
    doc_count = lax.axis_size("ep") * lax.axis_size("dp") * tok_dev // PASSAGE // 4
    doc_range = jnp.arange(doc_count, dtype=jnp.int32)[None, :]
    all_scores, all_docs = (
        lax.all_gather(passage_score, ("ep", "dp"), axis=0, tiled=True),
        lax.all_gather(doc_ids.astype(jnp.float32), ("ep", "dp"), axis=0, tiled=True),
    )
    member = all_docs[:, None] == doc_range.astype(jnp.float32)
    column = all_scores[:, None]
    passage_index = jnp.arange(all_scores.shape[0], dtype=jnp.int32)[:, None]
    max_score = jnp.where(member, column, -1e30).max(axis=0)
    sum_score = jnp.where(member, column, 0.0).sum(axis=0)
    first_index = jnp.where(member, passage_index, all_scores.shape[0]).min(axis=0)
    first_score = jnp.where(member & (passage_index == first_index[None, :]), column, 0.0).sum(
        axis=0
    )
    return (mixed, jnp.stack([max_score, first_score, sum_score]))


def pool(all_scores, all_docs, doc_count):
    doc_range = jnp.arange(doc_count, dtype=jnp.int32)[None, :]
    member = all_docs[:, None] == doc_range.astype(jnp.float32)
    column = all_scores[:, None]
    passage_index = jnp.arange(all_scores.shape[0], dtype=jnp.int32)[:, None]
    max_score = jnp.where(member, column, -1e30).max(axis=0)
    sum_score = jnp.where(member, column, 0.0).sum(axis=0)
    first_index = jnp.where(member, passage_index, all_scores.shape[0]).min(axis=0)
    first_score = jnp.where(member & (passage_index == first_index[None, :]), column, 0.0).sum(
        axis=0
    )
    return jnp.stack([max_score, first_score, sum_score])


def dense_shards(tokens, routes, gates, w_gate, w_up, w_down, score_head, doc_ids):
    tok_dev, width = tokens.shape
    experts = lax.axis_size("ep")
    groups = lax.axis_size("dp")
    local = tok_dev // PASSAGE
    me = lax.axis_index("ep")
    chosen = routes[:, :, None] == jnp.arange(experts, dtype=jnp.int32)[None, None, :]
    dense_gates = jnp.where(chosen, gates[:, :, None], jnp.bfloat16(0)).sum(axis=1)
    rows, gate_table = (
        lax.all_gather(tokens, "ep", axis=0, tiled=True),
        lax.all_gather(dense_gates, "ep", axis=0, tiled=True),
    )
    gate_rows = lax.dynamic_slice_in_dim(gate_table, me, 1, axis=1)
    gate_part = jnp.dot(rows, w_gate[0], preferred_element_type=jnp.float32)
    up_part = jnp.dot(rows, w_up[0], preferred_element_type=jnp.float32)
    hidden = (jax.nn.silu(gate_part) * up_part).astype(jnp.bfloat16)
    result = jnp.dot(hidden, w_down[0], preferred_element_type=jnp.float32)
    weighted = (gate_rows.astype(jnp.float32) * result).astype(jnp.bfloat16)
    mixed = lax.psum_scatter(weighted, "ep", scatter_dimension=0, tiled=True)
    head_part = jnp.dot(
        w_down[0].astype(jnp.float32), score_head, precision=lax.Precision.HIGHEST
    )
    pooled = jnp.einsum(
        "pt,ptf->pf",
        gate_rows.reshape(experts * local, PASSAGE),
        hidden.reshape(experts * local, PASSAGE, -1),
        preferred_element_type=jnp.float32,
    )
    part_score = (pooled * head_part[None, :]).sum(axis=1) / math.sqrt(PASSAGE)
    group = lax.axis_index("dp")
    here = (jnp.arange(groups) == group).astype(jnp.float32)[None, :, None]
    spread_scores = part_score.reshape(experts, 1, local) * here
    mine = (jnp.arange(experts) == me).astype(jnp.float32)[:, None, None]
    spread_docs = doc_ids.astype(jnp.float32).reshape(1, 1, local) * here * mine
    totals = lax.psum(
        jnp.stack([spread_scores.reshape(-1), spread_docs.reshape(-1)]), ("ep", "dp")
    )
    doc_count = experts * groups * local // 4
    return (mixed, pool(totals[0], totals[1], doc_count))


def shards(tokens, *rest):
    tok_dev = tokens.shape[0]
    capacity = min(tok_dev, 3 * tok_dev * TOP // (2 * lax.axis_size("ep")))
    plan = dense_shards if 2 * capacity >= tok_dev else slot_shards
    return plan(tokens, *rest)


def solution(mesh):
    return jax.shard_map(
        shards,
        mesh=mesh,
        in_specs=(
            P(("ep", "dp"), None),
            P(("ep", "dp"), None),
            P(("ep", "dp"), None),
            P("ep", None, None),
            P("ep", None, None),
            P("ep", None, None),
            P(),
            P(("ep", "dp")),
        ),
        out_specs=(P(("ep", "dp"), None), P()),
        check_vma=False,
    )
```

```python
import math

import jax
import jax.numpy as jnp
from jax import lax
from jax.experimental import pallas as pl
from jax.experimental.pallas import tpu as pltpu
from jax.sharding import PartitionSpec as P

TOP = 8
PASSAGE = 128


def expert_rows(rows, gate_rows, wg_single, wu_single, wd_single):
    gate_part = jnp.dot(rows, wg_single, preferred_element_type=jnp.float32)
    up_part = jnp.dot(rows, wu_single, preferred_element_type=jnp.float32)
    hidden = (jax.nn.silu(gate_part) * up_part).astype(jnp.bfloat16)
    result = jnp.dot(hidden, wd_single, preferred_element_type=jnp.float32)
    return (gate_rows.astype(jnp.float32)[:, None] * result).astype(jnp.bfloat16)


def run_expert(slot_rows, slot_gates, wg_single, wu_single, wd_single):
    width = slot_rows.shape[-1]
    rows = slot_rows.reshape(-1, width)
    gate_rows = slot_gates.reshape(-1)
    result = expert_rows(rows, gate_rows, wg_single, wu_single, wd_single)
    return result.reshape(slot_rows.shape)


def slot_shards(tokens, routes, gates, w_gate, w_up, w_down, score_head, doc_ids):
    tok_dev, width = tokens.shape
    experts = lax.axis_size("ep")
    capacity = min(tok_dev, 3 * tok_dev * TOP // (2 * experts))
    flat_routes = routes.reshape(-1)
    onehot = (flat_routes[:, None] == jnp.arange(experts, dtype=jnp.int32)[None, :]).astype(
        jnp.int32
    )
    ranked = jnp.cumsum(onehot, axis=0)
    slot = jnp.sum(ranked * onehot, axis=1) - 1
    destination = flat_routes * capacity + slot
    repeated = jnp.repeat(tokens, TOP, axis=0)
    send_rows = jnp.zeros((experts * capacity, width), jnp.bfloat16).at[destination].set(repeated)
    send_gates = (
        jnp.zeros((experts * capacity,), jnp.bfloat16).at[destination].set(gates.reshape(-1))
    )
    recv_rows, recv_gates = (
        lax.all_to_all(
            send_rows.reshape(experts, capacity, width),
            "ep",
            split_axis=0,
            concat_axis=0,
            tiled=True,
        ),
        lax.all_to_all(
            send_gates.reshape(experts, capacity), "ep", split_axis=0, concat_axis=0, tiled=True
        ),
    )
    wg_single = w_gate[0]
    wu_single = w_up[0]
    wd_single = w_down[0]
    results = run_expert(recv_rows, recv_gates, wg_single, wu_single, wd_single)
    returned = lax.all_to_all(results, "ep", split_axis=0, concat_axis=0, tiled=True)
    returned_flat = returned.reshape(experts * capacity, width)
    gathered = returned_flat[destination].astype(jnp.float32).reshape(tok_dev, TOP, width)
    mixed = jnp.sum(gathered, axis=1).astype(jnp.bfloat16)
    token_score = jnp.dot(mixed.astype(jnp.float32), score_head, precision=lax.Precision.HIGHEST)
    passage_score = token_score.reshape(-1, PASSAGE).sum(axis=1) / math.sqrt(PASSAGE)
    doc_count = lax.axis_size("ep") * lax.axis_size("dp") * tok_dev // PASSAGE // 4
    doc_range = jnp.arange(doc_count, dtype=jnp.int32)[None, :]
    all_scores, all_docs = (
        lax.all_gather(passage_score, ("ep", "dp"), axis=0, tiled=True),
        lax.all_gather(doc_ids.astype(jnp.float32), ("ep", "dp"), axis=0, tiled=True),
    )
    member = all_docs[:, None] == doc_range.astype(jnp.float32)
    column = all_scores[:, None]
    passage_index = jnp.arange(all_scores.shape[0], dtype=jnp.int32)[:, None]
    max_score = jnp.where(member, column, -1e30).max(axis=0)
    sum_score = jnp.where(member, column, 0.0).sum(axis=0)
    first_index = jnp.where(member, passage_index, all_scores.shape[0]).min(axis=0)
    first_score = jnp.where(member & (passage_index == first_index[None, :]), column, 0.0).sum(
        axis=0
    )
    return (mixed, jnp.stack([max_score, first_score, sum_score]))


def pool(all_scores, all_docs, doc_count):
    doc_range = jnp.arange(doc_count, dtype=jnp.int32)[None, :]
    member = all_docs[:, None] == doc_range.astype(jnp.float32)
    column = all_scores[:, None]
    passage_index = jnp.arange(all_scores.shape[0], dtype=jnp.int32)[:, None]
    max_score = jnp.where(member, column, -1e30).max(axis=0)
    sum_score = jnp.where(member, column, 0.0).sum(axis=0)
    first_index = jnp.where(member, passage_index, all_scores.shape[0]).min(axis=0)
    first_score = jnp.where(member & (passage_index == first_index[None, :]), column, 0.0).sum(
        axis=0
    )
    return jnp.stack([max_score, first_score, sum_score])


FF_TILE = 256


def expert_kernel(xa, xb, xc, xd, gate, head, wg, wu, wd, keep, send, score, rows, scale, acc):
    step = pl.program_id(0)
    tok = xa.shape[0]
    local = tok // PASSAGE

    @pl.when(step == 0)
    def _():
        for n, ref in enumerate((xa, xb, xc, xd)):
            rows[pl.ds(n * tok, tok), :] = ref[...]
        diagonal = lax.broadcasted_iota(jnp.int32, (tok, tok), 0) == lax.broadcasted_iota(
            jnp.int32, (tok, tok), 1
        )
        for n in range(4):
            row = gate[pl.ds(n, 1), :]
            scale[pl.ds(n * tok, tok), :] = jnp.sum(
                jnp.where(diagonal, row, 0.0), axis=1, keepdims=True
            )

    x = rows[...]
    gate_part = jnp.dot(x, wg[...], preferred_element_type=jnp.float32)
    up_part = jnp.dot(x, wu[...], preferred_element_type=jnp.float32)
    hidden = (gate_part / (1.0 + jnp.exp(-gate_part)) * up_part).astype(jnp.bfloat16)
    part = jnp.dot(hidden, wd[...], preferred_element_type=jnp.float32)

    weighed = hidden.astype(jnp.float32) * head[...] * scale[...]
    summed = jnp.sum(weighed.reshape(4 * local, PASSAGE, weighed.shape[1]), axis=1)

    @pl.when(step == 0)
    def _():
        acc[...] = part
        score[...] = summed

    @pl.when(step > 0)
    def _():
        acc[...] += part
        score[...] += summed

    @pl.when(step == pl.num_programs(0) - 1)
    def _():
        half = 2 * tok
        weighted = (acc[...] * scale[...]).astype(jnp.bfloat16)
        keep[...] = weighted[:half]
        send[...] = weighted[half:]


def expert_call(blocks, gate, head, wg, wu, wd):
    tok, width = blocks[0].shape
    ff = wg.shape[1]
    tile = FF_TILE if ff % FF_TILE == 0 else ff
    local = tok // PASSAGE
    whole = lambda shape: pl.BlockSpec(shape, lambda j: (0,) * len(shape))
    return pl.pallas_call(
        expert_kernel,
        grid=(ff // tile,),
        in_specs=[whole((tok, width))] * 4
        + [
            whole((4, tok)),
            pl.BlockSpec((1, tile), lambda j: (0, j)),
            pl.BlockSpec((width, tile), lambda j: (0, j)),
            pl.BlockSpec((width, tile), lambda j: (0, j)),
            pl.BlockSpec((tile, width), lambda j: (j, 0)),
        ],
        out_specs=[
            whole((2 * tok, width)),
            whole((2 * tok, width)),
            whole((4 * local, tile)),
        ],
        out_shape=[
            jax.ShapeDtypeStruct((2 * tok, width), jnp.bfloat16),
            jax.ShapeDtypeStruct((2 * tok, width), jnp.bfloat16),
            jax.ShapeDtypeStruct((4 * local, tile), jnp.float32),
        ],
        scratch_shapes=[
            pltpu.VMEM((4 * tok, width), jnp.bfloat16),
            pltpu.VMEM((4 * tok, 1), jnp.float32),
            pltpu.VMEM((4 * tok, width), jnp.float32),
        ],
        compiler_params=pltpu.CompilerParams(vmem_limit_bytes=48 * 2**20),
        cost_estimate=pl.CostEstimate(
            flops=24 * tok * width * ff,
            bytes_accessed=2 * (3 * width * ff + 8 * tok * width),
            transcendentals=4 * tok * ff,
        ),
        name="expert",
    )(*blocks, gate, head, wg, wu, wd)


def add_rounded(left, right):
    return (left.astype(jnp.float32) + right.astype(jnp.float32)).astype(jnp.bfloat16)


def spread_total(value, axis):
    size = lax.axis_size(axis)
    if size & (size - 1):
        return lax.psum(value, axis)
    step = 1
    while step < size:
        value = value + lax.ppermute(value, axis, [(i, i ^ step) for i in range(size)])
        step *= 2
    return value


def dense_shards(tokens, routes, gates, w_gate, w_up, w_down, score_head, doc_ids):
    tok_dev, width = tokens.shape
    experts = lax.axis_size("ep")
    groups = lax.axis_size("dp")
    local = tok_dev // PASSAGE
    ring = experts // 4
    me = lax.axis_index("ep")
    group = lax.axis_index("dp")
    onward = lambda v: lax.ppermute(
        v, "ep", [(i, (i + 4) % experts) for i in range(experts)]
    )
    across = lambda v: lax.ppermute(v, "ep", [(i, i ^ 2) for i in range(experts)])
    sibling = lambda v: lax.ppermute(v, "ep", [(i, i ^ 1) for i in range(experts)])

    near = [tokens]
    for s in range(1, ring):
        near.append(onward(near[-1]))
    far = [across(v) for v in near]
    blocks = [(near[s], far[s], sibling(near[s]), sibling(far[s])) for s in range(ring)]

    chosen = routes[:, None, :] == jnp.arange(experts, dtype=jnp.int32)[None, :, None]
    dense_gates = jnp.where(chosen, gates[:, None, :], jnp.bfloat16(0)).sum(axis=2).T
    gate_rows = lax.all_to_all(dense_gates, "ep", split_axis=0, concat_axis=0, tiled=True)
    place = (me // 4 - jnp.arange(ring, dtype=jnp.int32)) % ring
    order = (place[:, None] * 4 + (me % 4 ^ jnp.array([0, 2, 1, 3], jnp.int32))[None, :]).reshape(-1)
    position = order[:, None] == jnp.arange(experts, dtype=jnp.int32)[None, :]
    slot_gates = gate_rows.astype(jnp.float32)[order].reshape(ring, 4, tok_dev)
    head = jnp.sum(w_down[0].astype(jnp.float32) * score_head[None, :], axis=1)[None, :]

    scores = [None] * ring
    merged = [None] * ring
    for s in range(ring):
        keep, send, scores[s] = expert_call(
            blocks[s], slot_gates[s], head, w_gate[0], w_up[0], w_down[0]
        )
        pair = add_rounded(keep, sibling(send))
        merged[s] = (pair[:tok_dev], across(pair[tok_dev:]))
    carried = None
    for s in [*range(1, ring), 0]:
        own, other = merged[s]
        total = own.astype(jnp.float32) + other.astype(jnp.float32)
        if carried is not None:
            total = total + carried.astype(jnp.float32)
        total = total.astype(jnp.bfloat16)
        if s > 0:
            carried = onward(total)
    mixed = total

    slot_scores = jnp.stack(scores).reshape(experts, local, -1).sum(axis=2) / math.sqrt(PASSAGE)
    part_score = jnp.where(position[:, :, None], slot_scores[:, None, :], 0.0).sum(axis=0)
    here = (jnp.arange(groups) == group)[None, :, None]
    mine = (jnp.arange(experts) == me)[:, None, None]
    spread_scores = jnp.where(here, part_score[:, None, :], 0.0)
    spread_docs = jnp.where(
        here & mine, doc_ids.astype(jnp.float32).reshape(1, 1, local), 0.0
    )
    totals = jnp.stack([spread_scores.reshape(-1), spread_docs.reshape(-1)])
    totals = spread_total(spread_total(totals, "dp"), "ep")
    doc_count = experts * groups * local // 4
    return (mixed, pool(totals[0], totals[1], doc_count))


def shards(tokens, *rest):
    tok_dev = tokens.shape[0]
    experts = lax.axis_size("ep")
    capacity = min(tok_dev, 3 * tok_dev * TOP // (2 * experts))
    dense = 2 * capacity >= tok_dev and experts % 4 == 0 and tok_dev % PASSAGE == 0
    return (dense_shards if dense else slot_shards)(tokens, *rest)


def solution(mesh):
    return jax.shard_map(
        shards,
        mesh=mesh,
        in_specs=(
            P(("ep", "dp"), None),
            P(("ep", "dp"), None),
            P(("ep", "dp"), None),
            P("ep", None, None),
            P("ep", None, None),
            P("ep", None, None),
            P(),
            P(("ep", "dp")),
        ),
        out_specs=(P(("ep", "dp"), None), P()),
        check_vma=False,
    )
```

```python
import math

import jax
import jax.numpy as jnp
from jax import lax
from jax.experimental import pallas as pl
from jax.experimental.pallas import tpu as pltpu
from jax.sharding import PartitionSpec as P

TOP = 8
PASSAGE = 128


def expert_rows(rows, gate_rows, wg_single, wu_single, wd_single):
    gate_part = jnp.dot(rows, wg_single, preferred_element_type=jnp.float32)
    up_part = jnp.dot(rows, wu_single, preferred_element_type=jnp.float32)
    hidden = (jax.nn.silu(gate_part) * up_part).astype(jnp.bfloat16)
    result = jnp.dot(hidden, wd_single, preferred_element_type=jnp.float32)
    return (gate_rows.astype(jnp.float32)[:, None] * result).astype(jnp.bfloat16)


def run_expert(slot_rows, slot_gates, wg_single, wu_single, wd_single):
    width = slot_rows.shape[-1]
    rows = slot_rows.reshape(-1, width)
    gate_rows = slot_gates.reshape(-1)
    result = expert_rows(rows, gate_rows, wg_single, wu_single, wd_single)
    return result.reshape(slot_rows.shape)


def slot_shards(tokens, routes, gates, w_gate, w_up, w_down, score_head, doc_ids):
    tok_dev, width = tokens.shape
    experts = lax.axis_size("ep")
    capacity = min(tok_dev, 3 * tok_dev * TOP // (2 * experts))
    flat_routes = routes.reshape(-1)
    onehot = (flat_routes[:, None] == jnp.arange(experts, dtype=jnp.int32)[None, :]).astype(
        jnp.int32
    )
    ranked = jnp.cumsum(onehot, axis=0)
    slot = jnp.sum(ranked * onehot, axis=1) - 1
    destination = flat_routes * capacity + slot
    repeated = jnp.repeat(tokens, TOP, axis=0)
    send_rows = jnp.zeros((experts * capacity, width), jnp.bfloat16).at[destination].set(repeated)
    send_gates = (
        jnp.zeros((experts * capacity,), jnp.bfloat16).at[destination].set(gates.reshape(-1))
    )
    recv_rows, recv_gates = (
        lax.all_to_all(
            send_rows.reshape(experts, capacity, width),
            "ep",
            split_axis=0,
            concat_axis=0,
            tiled=True,
        ),
        lax.all_to_all(
            send_gates.reshape(experts, capacity), "ep", split_axis=0, concat_axis=0, tiled=True
        ),
    )
    wg_single = w_gate[0]
    wu_single = w_up[0]
    wd_single = w_down[0]
    results = run_expert(recv_rows, recv_gates, wg_single, wu_single, wd_single)
    returned = lax.all_to_all(results, "ep", split_axis=0, concat_axis=0, tiled=True)
    returned_flat = returned.reshape(experts * capacity, width)
    gathered = returned_flat[destination].astype(jnp.float32).reshape(tok_dev, TOP, width)
    mixed = jnp.sum(gathered, axis=1).astype(jnp.bfloat16)
    token_score = jnp.dot(mixed.astype(jnp.float32), score_head, precision=lax.Precision.HIGHEST)
    passage_score = token_score.reshape(-1, PASSAGE).sum(axis=1) / math.sqrt(PASSAGE)
    doc_count = lax.axis_size("ep") * lax.axis_size("dp") * tok_dev // PASSAGE // 4
    doc_range = jnp.arange(doc_count, dtype=jnp.int32)[None, :]
    all_scores, all_docs = (
        lax.all_gather(passage_score, ("ep", "dp"), axis=0, tiled=True),
        lax.all_gather(doc_ids.astype(jnp.float32), ("ep", "dp"), axis=0, tiled=True),
    )
    member = all_docs[:, None] == doc_range.astype(jnp.float32)
    column = all_scores[:, None]
    passage_index = jnp.arange(all_scores.shape[0], dtype=jnp.int32)[:, None]
    max_score = jnp.where(member, column, -1e30).max(axis=0)
    sum_score = jnp.where(member, column, 0.0).sum(axis=0)
    first_index = jnp.where(member, passage_index, all_scores.shape[0]).min(axis=0)
    first_score = jnp.where(member & (passage_index == first_index[None, :]), column, 0.0).sum(
        axis=0
    )
    return (mixed, jnp.stack([max_score, first_score, sum_score]))


def pool(all_scores, all_docs, doc_count):
    doc_range = jnp.arange(doc_count, dtype=jnp.int32)[None, :]
    member = all_docs[:, None] == doc_range.astype(jnp.float32)
    column = all_scores[:, None]
    passage_index = jnp.arange(all_scores.shape[0], dtype=jnp.int32)[:, None]
    max_score = jnp.where(member, column, -1e30).max(axis=0)
    sum_score = jnp.where(member, column, 0.0).sum(axis=0)
    first_index = jnp.where(member, passage_index, all_scores.shape[0]).min(axis=0)
    first_score = jnp.where(member & (passage_index == first_index[None, :]), column, 0.0).sum(
        axis=0
    )
    return jnp.stack([max_score, first_score, sum_score])


LANES = 128


def tile_of(extent, most):
    return most if extent % most == 0 else extent


def expert_kernel(
    xa, xb, wg0, wu0, wd0, wg1, wu1, wd1, gate, head, after,
    outa, outb, score,
    rows, wg, wu, wd, hidden, scale, out, x_sem, up_sem, down_sem, out_sem,
):
    tok, width = xa.shape
    ff = wg0.shape[1]
    local = tok // PASSAGE
    ff_tile = tile_of(ff, 256)
    out_tile = tile_of(width, 512)
    blocks = [pl.ds(n * tok, tok) for n in range(2)]
    x_copies = [
        pltpu.make_async_copy(ref, rows.at[blocks[n], :], x_sem.at[n])
        for n, ref in enumerate((xa, xb))
    ]
    up_copies = []
    for e, pair in enumerate(((wg0, wu0), (wg1, wu1))):
        for j in range(ff // ff_tile):
            columns = pl.ds(j * ff_tile, ff_tile)
            up_copies.append(
                [
                    pltpu.make_async_copy(
                        src.at[:, columns], dst.at[e, :, columns], up_sem.at[e, j, m]
                    )
                    for m, (src, dst) in enumerate(zip(pair, (wg, wu)))
                ]
            )
    down_copies = [
        pltpu.make_async_copy(src, wd.at[e], down_sem.at[e]) for e, src in enumerate((wd0, wd1))
    ]
    for copy in x_copies + [c for pair in up_copies for c in pair] + down_copies:
        copy.start()

    diagonal = lax.broadcasted_iota(jnp.int32, (tok, tok), 0) == lax.broadcasted_iota(
        jnp.int32, (tok, tok), 1
    )
    for n in range(2):
        for e in range(2):
            row = gate[pl.ds(2 * n + e, 1), :]
            scale[e, blocks[n], :] = jnp.sum(
                jnp.where(diagonal, row, 0.0), axis=1, keepdims=True
            )

    for copy in x_copies:
        copy.wait()
    for e in range(2):
        for j in range(ff // ff_tile):
            columns = pl.ds(j * ff_tile, ff_tile)
            for copy in up_copies[e * (ff // ff_tile) + j]:
                copy.wait()
            gate_part = jnp.dot(
                rows[...], wg[e, :, columns], preferred_element_type=jnp.float32
            )
            up_part = jnp.dot(rows[...], wu[e, :, columns], preferred_element_type=jnp.float32)
            value = gate_part / (1.0 + jnp.exp(-gate_part)) * up_part
            hidden[e, :, columns] = value.astype(jnp.bfloat16)

    for copy in down_copies:
        copy.wait()
    totals = [jnp.zeros((1, LANES), jnp.float32) for _ in range(2 * local)]
    out_copies = []
    for j in range(width // out_tile):
        columns = pl.ds(j * out_tile, out_tile)
        weighted = sum(
            scale[e]
            * jnp.dot(hidden[e], wd[e, :, columns], preferred_element_type=jnp.float32)
            for e in range(2)
        )
        out[:, columns] = weighted.astype(jnp.bfloat16)
        scored = weighted * head[:, columns]
        lanes = sum(
            scored[:, k * LANES : (k + 1) * LANES] for k in range(out_tile // LANES)
        )
        for p in range(2 * local):
            totals[p] += jnp.sum(lanes[p * PASSAGE : (p + 1) * PASSAGE], axis=0, keepdims=True)
        for n, ref in enumerate((outa, outb)):
            copy = pltpu.make_async_copy(
                out.at[blocks[n], columns], ref.at[:, columns], out_sem.at[n, j]
            )
            copy.start()
            out_copies.append(copy)
    for p in range(2 * local):
        score[pl.ds(p, 1), :] = totals[p]
    for copy in out_copies:
        copy.wait()


def expert_call(blocks, weights, gate, head, after):
    tok, width = blocks[0].shape
    ff = weights[0].shape[1]
    local = tok // PASSAGE
    anywhere = pl.BlockSpec(memory_space=pl.ANY)
    vmem = pl.BlockSpec(memory_space=pltpu.VMEM)
    bf16 = jnp.bfloat16
    return pl.pallas_call(
        expert_kernel,
        in_specs=[anywhere] * 8 + [vmem, vmem, anywhere],
        out_specs=[anywhere, anywhere, vmem],
        out_shape=[
            jax.ShapeDtypeStruct((tok, width), bf16),
            jax.ShapeDtypeStruct((tok, width), bf16),
            jax.ShapeDtypeStruct((2 * local, LANES), jnp.float32),
        ],
        scratch_shapes=[
            pltpu.VMEM((2 * tok, width), bf16),
            pltpu.VMEM((2, width, ff), bf16),
            pltpu.VMEM((2, width, ff), bf16),
            pltpu.VMEM((2, ff, width), bf16),
            pltpu.VMEM((2, 2 * tok, ff), bf16),
            pltpu.VMEM((2, 2 * tok, 1), jnp.float32),
            pltpu.VMEM((2 * tok, width), bf16),
            pltpu.SemaphoreType.DMA((2,)),
            pltpu.SemaphoreType.DMA((2, ff // tile_of(ff, 256), 2)),
            pltpu.SemaphoreType.DMA((2,)),
            pltpu.SemaphoreType.DMA((2, width // tile_of(width, 512))),
        ],
        compiler_params=pltpu.CompilerParams(vmem_limit_bytes=28 * 2**20),
        cost_estimate=pl.CostEstimate(
            flops=24 * tok * width * ff,
            bytes_accessed=2 * (6 * width * ff + 4 * tok * width),
            transcendentals=4 * tok * ff,
        ),
        name="expert",
    )(*blocks, *weights, gate, head, after)


def dense_shards(tokens, routes, gates, w_gate, w_up, w_down, score_head, doc_ids):
    tok_dev, width = tokens.shape
    experts = lax.axis_size("ep")
    groups = lax.axis_size("dp")
    local = tok_dev // PASSAGE
    ring = experts // 4
    me = lax.axis_index("ep")
    onward = lambda v: lax.ppermute(
        v, "ep", [(i, (i + 4) % experts) for i in range(experts)]
    )
    across = lambda v: lax.ppermute(v, "ep", [(i, i ^ 2) for i in range(experts)])
    sibling = lambda v: lax.ppermute(v, "ep", [(i, i ^ 1) for i in range(experts)])

    near = [tokens]
    for s in range(1, ring):
        near.append(onward(near[-1]))
    far = [across(v) for v in near]
    own = (w_gate[0], w_up[0], w_down[0])
    weights = own + tuple(sibling(w) for w in own)

    chosen = routes[:, None, :] == jnp.arange(experts, dtype=jnp.int32)[None, :, None]
    dense_gates = jnp.where(chosen, gates[:, None, :], jnp.bfloat16(0)).sum(axis=2).T
    chip_gates = dense_gates.reshape(experts // 2, 2, tok_dev)
    sent_gates = jnp.stack([chip_gates, chip_gates[:, ::-1]], axis=1)
    gate_rows = lax.all_to_all(
        sent_gates.reshape(experts, 2 * tok_dev), "ep", split_axis=0, concat_axis=0, tiled=True
    )
    place = (me // 4 - jnp.arange(ring, dtype=jnp.int32)) % ring
    order = (place[:, None] * 4 + (me % 4 ^ jnp.array([0, 2], jnp.int32))[None, :]).reshape(-1)
    position = order[:, None] == jnp.arange(experts, dtype=jnp.int32)[None, :]
    slot_gates = gate_rows.astype(jnp.float32)[order].reshape(ring, 4, tok_dev)

    head = score_head[None, :]
    scores = [None] * ring
    mine = [None] * ring
    other = [None] * ring
    after = far[0]
    turns = [*range(1, ring), 0]
    for s in turns:
        mine[s], other[s], scores[s] = expert_call(
            (near[s], far[s]), weights, slot_gates[s], head, after
        )
        after = scores[s]
    carried = None
    for s in turns:
        total = mine[s].astype(jnp.float32) + across(other[s]).astype(jnp.float32)
        if carried is not None:
            total = total + carried.astype(jnp.float32)
        total = total.astype(jnp.bfloat16)
        if s > 0:
            carried = onward(total)
    mixed = total

    slot_scores = jnp.stack(scores).sum(axis=2).reshape(2 * ring, local) / math.sqrt(PASSAGE)
    part_score = jnp.where(position[:, :, None], slot_scores[:, None, :], 0.0).sum(axis=0)
    told = jnp.concatenate([part_score.reshape(-1), doc_ids.astype(jnp.float32)])
    told = jnp.pad(told, (0, -told.shape[0] % LANES))
    heard = lax.all_to_all(
        jnp.broadcast_to(told[None, :], (experts * groups, told.shape[0])),
        ("ep", "dp"),
        split_axis=0,
        concat_axis=0,
        tiled=True,
    )
    count = experts * local
    all_scores = heard[:, :count].reshape(experts, groups, experts, local).sum(axis=0)
    all_scores = all_scores.transpose(1, 0, 2).reshape(-1)
    all_docs = heard[:, count : count + local].reshape(-1)
    return (mixed, pool(all_scores, all_docs, count * groups // 4))


def shards(tokens, *rest):
    tok_dev = tokens.shape[0]
    experts = lax.axis_size("ep")
    capacity = min(tok_dev, 3 * tok_dev * TOP // (2 * experts))
    dense = 2 * capacity >= tok_dev and experts % 4 == 0 and tok_dev % PASSAGE == 0
    return (dense_shards if dense else slot_shards)(tokens, *rest)


def solution(mesh):
    return jax.shard_map(
        shards,
        mesh=mesh,
        in_specs=(
            P(("ep", "dp"), None),
            P(("ep", "dp"), None),
            P(("ep", "dp"), None),
            P("ep", None, None),
            P("ep", None, None),
            P("ep", None, None),
            P(),
            P(("ep", "dp")),
        ),
        out_specs=(P(("ep", "dp"), None), P()),
        check_vma=False,
    )
```

```python
import math

import jax
import jax.numpy as jnp
from jax import lax
from jax.experimental import pallas as pl
from jax.experimental.pallas import tpu as pltpu
from jax.sharding import PartitionSpec as P

TOP = 8
PASSAGE = 128


def expert_rows(rows, gate_rows, wg_single, wu_single, wd_single):
    gate_part = jnp.dot(rows, wg_single, preferred_element_type=jnp.float32)
    up_part = jnp.dot(rows, wu_single, preferred_element_type=jnp.float32)
    hidden = (jax.nn.silu(gate_part) * up_part).astype(jnp.bfloat16)
    result = jnp.dot(hidden, wd_single, preferred_element_type=jnp.float32)
    return (gate_rows.astype(jnp.float32)[:, None] * result).astype(jnp.bfloat16)


def run_expert(slot_rows, slot_gates, wg_single, wu_single, wd_single):
    width = slot_rows.shape[-1]
    rows = slot_rows.reshape(-1, width)
    gate_rows = slot_gates.reshape(-1)
    result = expert_rows(rows, gate_rows, wg_single, wu_single, wd_single)
    return result.reshape(slot_rows.shape)


def slot_shards(tokens, routes, gates, w_gate, w_up, w_down, score_head, doc_ids):
    tok_dev, width = tokens.shape
    experts = lax.axis_size("ep")
    capacity = min(tok_dev, 3 * tok_dev * TOP // (2 * experts))
    flat_routes = routes.reshape(-1)
    onehot = (flat_routes[:, None] == jnp.arange(experts, dtype=jnp.int32)[None, :]).astype(
        jnp.int32
    )
    ranked = jnp.cumsum(onehot, axis=0)
    slot = jnp.sum(ranked * onehot, axis=1) - 1
    destination = flat_routes * capacity + slot
    repeated = jnp.repeat(tokens, TOP, axis=0)
    send_rows = jnp.zeros((experts * capacity, width), jnp.bfloat16).at[destination].set(repeated)
    send_gates = (
        jnp.zeros((experts * capacity,), jnp.bfloat16).at[destination].set(gates.reshape(-1))
    )
    recv_rows, recv_gates = (
        lax.all_to_all(
            send_rows.reshape(experts, capacity, width),
            "ep",
            split_axis=0,
            concat_axis=0,
            tiled=True,
        ),
        lax.all_to_all(
            send_gates.reshape(experts, capacity), "ep", split_axis=0, concat_axis=0, tiled=True
        ),
    )
    wg_single = w_gate[0]
    wu_single = w_up[0]
    wd_single = w_down[0]
    results = run_expert(recv_rows, recv_gates, wg_single, wu_single, wd_single)
    returned = lax.all_to_all(results, "ep", split_axis=0, concat_axis=0, tiled=True)
    returned_flat = returned.reshape(experts * capacity, width)
    gathered = returned_flat[destination].astype(jnp.float32).reshape(tok_dev, TOP, width)
    mixed = jnp.sum(gathered, axis=1).astype(jnp.bfloat16)
    token_score = jnp.dot(mixed.astype(jnp.float32), score_head, precision=lax.Precision.HIGHEST)
    passage_score = token_score.reshape(-1, PASSAGE).sum(axis=1) / math.sqrt(PASSAGE)
    doc_count = lax.axis_size("ep") * lax.axis_size("dp") * tok_dev // PASSAGE // 4
    doc_range = jnp.arange(doc_count, dtype=jnp.int32)[None, :]
    all_scores, all_docs = (
        lax.all_gather(passage_score, ("ep", "dp"), axis=0, tiled=True),
        lax.all_gather(doc_ids.astype(jnp.float32), ("ep", "dp"), axis=0, tiled=True),
    )
    member = all_docs[:, None] == doc_range.astype(jnp.float32)
    column = all_scores[:, None]
    passage_index = jnp.arange(all_scores.shape[0], dtype=jnp.int32)[:, None]
    max_score = jnp.where(member, column, -1e30).max(axis=0)
    sum_score = jnp.where(member, column, 0.0).sum(axis=0)
    first_index = jnp.where(member, passage_index, all_scores.shape[0]).min(axis=0)
    first_score = jnp.where(member & (passage_index == first_index[None, :]), column, 0.0).sum(
        axis=0
    )
    return (mixed, jnp.stack([max_score, first_score, sum_score]))


def pool(all_scores, all_docs, doc_count):
    doc_range = jnp.arange(doc_count, dtype=jnp.int32)[None, :]
    member = all_docs[:, None] == doc_range.astype(jnp.float32)
    column = all_scores[:, None]
    passage_index = jnp.arange(all_scores.shape[0], dtype=jnp.int32)[:, None]
    max_score = jnp.where(member, column, -1e30).max(axis=0)
    sum_score = jnp.where(member, column, 0.0).sum(axis=0)
    first_index = jnp.where(member, passage_index, all_scores.shape[0]).min(axis=0)
    first_score = jnp.where(member & (passage_index == first_index[None, :]), column, 0.0).sum(
        axis=0
    )
    return jnp.stack([max_score, first_score, sum_score])


LANES = 128


def tile_of(extent, most):
    return most if extent % most == 0 else extent


def expert_kernel(
    xa, xb, wg0, wu0, wd0, wg1, wu1, wd1, gate, head, after,
    outa, outb, score,
    rows, wg, wu, wd, hidden, scale, out, x_sem, up_sem, down_sem, out_sem,
):
    tok, width = xa.shape
    ff = wg0.shape[1]
    local = tok // PASSAGE
    ff_tile = tile_of(ff, 256)
    out_tile = tile_of(width, 512)
    blocks = [pl.ds(n * tok, tok) for n in range(2)]
    x_copies = [
        pltpu.make_async_copy(ref, rows.at[blocks[n], :], x_sem.at[n])
        for n, ref in enumerate((xa, xb))
    ]
    up_copies = []
    for e, pair in enumerate(((wg0, wu0), (wg1, wu1))):
        for j in range(ff // ff_tile):
            columns = pl.ds(j * ff_tile, ff_tile)
            up_copies.append(
                [
                    pltpu.make_async_copy(
                        src.at[:, columns], dst.at[e, :, columns], up_sem.at[e, j, m]
                    )
                    for m, (src, dst) in enumerate(zip(pair, (wg, wu)))
                ]
            )
    down_copies = [
        pltpu.make_async_copy(src, wd.at[e], down_sem.at[e]) for e, src in enumerate((wd0, wd1))
    ]
    for copy in x_copies + [c for pair in up_copies for c in pair] + down_copies:
        copy.start()

    diagonal = lax.broadcasted_iota(jnp.int32, (tok, tok), 0) == lax.broadcasted_iota(
        jnp.int32, (tok, tok), 1
    )
    for n in range(2):
        for e in range(2):
            row = gate[pl.ds(2 * n + e, 1), :]
            scale[e, blocks[n], :] = jnp.sum(
                jnp.where(diagonal, row, 0.0), axis=1, keepdims=True
            )

    for copy in x_copies:
        copy.wait()
    for e in range(2):
        for j in range(ff // ff_tile):
            columns = pl.ds(j * ff_tile, ff_tile)
            for copy in up_copies[e * (ff // ff_tile) + j]:
                copy.wait()
            gate_part = jnp.dot(
                rows[...], wg[e, :, columns], preferred_element_type=jnp.float32
            )
            up_part = jnp.dot(rows[...], wu[e, :, columns], preferred_element_type=jnp.float32)
            value = gate_part / (1.0 + jnp.exp(-gate_part)) * up_part
            hidden[e, :, columns] = value.astype(jnp.bfloat16)

    for copy in down_copies:
        copy.wait()
    totals = [jnp.zeros((1, LANES), jnp.float32) for _ in range(2 * local)]
    out_copies = []
    for j in range(width // out_tile):
        columns = pl.ds(j * out_tile, out_tile)
        weighted = sum(
            scale[e]
            * jnp.dot(hidden[e], wd[e, :, columns], preferred_element_type=jnp.float32)
            for e in range(2)
        )
        out[:, columns] = weighted.astype(jnp.bfloat16)
        scored = weighted * head[:, columns]
        lanes = sum(
            scored[:, k * LANES : (k + 1) * LANES] for k in range(out_tile // LANES)
        )
        for p in range(2 * local):
            totals[p] += jnp.sum(lanes[p * PASSAGE : (p + 1) * PASSAGE], axis=0, keepdims=True)
        for n, ref in enumerate((outa, outb)):
            copy = pltpu.make_async_copy(
                out.at[blocks[n], columns], ref.at[:, columns], out_sem.at[n, j]
            )
            copy.start()
            out_copies.append(copy)
    for p in range(2 * local):
        score[pl.ds(p, 1), :] = totals[p]
    for copy in out_copies:
        copy.wait()


def tie_kernel(value, first, passed):
    pass


def tie(value, first):
    anywhere = pl.BlockSpec(memory_space=pl.ANY)
    return pl.pallas_call(
        tie_kernel,
        in_specs=[anywhere, anywhere],
        out_specs=anywhere,
        out_shape=jax.ShapeDtypeStruct(value.shape, value.dtype),
        input_output_aliases={0: 0},
        name="tie",
    )(value, first)


def expert_call(blocks, weights, gate, head, after):
    tok, width = blocks[0].shape
    ff = weights[0].shape[1]
    local = tok // PASSAGE
    anywhere = pl.BlockSpec(memory_space=pl.ANY)
    vmem = pl.BlockSpec(memory_space=pltpu.VMEM)
    bf16 = jnp.bfloat16
    return pl.pallas_call(
        expert_kernel,
        in_specs=[anywhere] * 8 + [vmem, vmem, anywhere],
        out_specs=[anywhere, anywhere, vmem],
        out_shape=[
            jax.ShapeDtypeStruct((tok, width), bf16),
            jax.ShapeDtypeStruct((tok, width), bf16),
            jax.ShapeDtypeStruct((2 * local, LANES), jnp.float32),
        ],
        scratch_shapes=[
            pltpu.VMEM((2 * tok, width), bf16),
            pltpu.VMEM((2, width, ff), bf16),
            pltpu.VMEM((2, width, ff), bf16),
            pltpu.VMEM((2, ff, width), bf16),
            pltpu.VMEM((2, 2 * tok, ff), bf16),
            pltpu.VMEM((2, 2 * tok, 1), jnp.float32),
            pltpu.VMEM((2 * tok, width), bf16),
            pltpu.SemaphoreType.DMA((2,)),
            pltpu.SemaphoreType.DMA((2, ff // tile_of(ff, 256), 2)),
            pltpu.SemaphoreType.DMA((2,)),
            pltpu.SemaphoreType.DMA((2, width // tile_of(width, 512))),
        ],
        compiler_params=pltpu.CompilerParams(vmem_limit_bytes=60 * 2**20),
        cost_estimate=pl.CostEstimate(
            flops=24 * tok * width * ff,
            bytes_accessed=2 * (6 * width * ff + 4 * tok * width),
            transcendentals=4 * tok * ff,
        ),
        name="expert",
    )(*blocks, *weights, gate, head, after)


def dense_shards(tokens, routes, gates, w_gate, w_up, w_down, score_head, doc_ids):
    tok_dev, width = tokens.shape
    experts = lax.axis_size("ep")
    groups = lax.axis_size("dp")
    local = tok_dev // PASSAGE
    ring = experts // 4
    me = lax.axis_index("ep")
    onward = lambda v: lax.ppermute(
        v, "ep", [(i, (i + 4) % experts) for i in range(experts)]
    )
    across = lambda v: lax.ppermute(v, "ep", [(i, i ^ 2) for i in range(experts)])
    sibling = lambda v: lax.ppermute(v, "ep", [(i, i ^ 1) for i in range(experts)])

    near = [tokens]
    for s in range(1, ring):
        near.append(onward(near[-1]))
    far = [across(v) for v in near]
    own = (w_gate[0], w_up[0], w_down[0])
    weights = own + tuple(sibling(w) for w in own)

    chosen = routes[:, None, :] == jnp.arange(experts, dtype=jnp.int32)[None, :, None]
    dense_gates = jnp.where(chosen, gates[:, None, :], jnp.bfloat16(0)).sum(axis=2).T
    chip_gates = dense_gates.reshape(experts // 2, 2, tok_dev)
    sent_gates = jnp.stack([chip_gates, chip_gates[:, ::-1]], axis=1)
    gate_rows = lax.all_to_all(
        sent_gates.reshape(experts, 2 * tok_dev), "ep", split_axis=0, concat_axis=0, tiled=True
    )
    place = (me // 4 - jnp.arange(ring, dtype=jnp.int32)) % ring
    order = (place[:, None] * 4 + (me % 4 ^ jnp.array([0, 2], jnp.int32))[None, :]).reshape(-1)
    position = order[:, None] == jnp.arange(experts, dtype=jnp.int32)[None, :]
    slot_gates = gate_rows.astype(jnp.float32)[order].reshape(ring, 4, tok_dev)

    head = score_head[None, :]
    scores = [None] * ring
    mine = [None] * ring
    other = [None] * ring
    after = far[0]
    turns = [*range(1, ring), 0]
    for s in turns:
        mine[s], other[s], scores[s] = expert_call(
            (near[s], far[s]), weights, slot_gates[s], head, after
        )
        after = scores[s]
    carried = None
    for s in turns:
        total = mine[s].astype(jnp.float32) + across(other[s]).astype(jnp.float32)
        if carried is not None:
            total = total + carried.astype(jnp.float32)
        total = total.astype(jnp.bfloat16)
        if s > 0:
            carried, last_sent = onward(total), total
    mixed = total

    slot_scores = jnp.stack(scores).sum(axis=2).reshape(2 * ring, local) / math.sqrt(PASSAGE)
    part_score = jnp.where(position[:, :, None], slot_scores[:, None, :], 0.0).sum(axis=0)
    told = jnp.concatenate([part_score.reshape(-1), doc_ids.astype(jnp.float32)])
    told = jnp.pad(told, (0, -told.shape[0] % LANES))[None, :]
    told = tie(told, last_sent)
    heard = lax.all_to_all(
        jnp.broadcast_to(told, (experts * groups, told.shape[1])),
        ("ep", "dp"),
        split_axis=0,
        concat_axis=0,
        tiled=True,
    )
    count = experts * local
    all_scores = heard[:, :count].reshape(experts, groups, experts, local).sum(axis=0)
    all_scores = all_scores.transpose(1, 0, 2).reshape(-1)
    all_docs = heard[:, count : count + local].reshape(-1)
    return (mixed, pool(all_scores, all_docs, count * groups // 4))


def shards(tokens, *rest):
    tok_dev = tokens.shape[0]
    experts = lax.axis_size("ep")
    capacity = min(tok_dev, 3 * tok_dev * TOP // (2 * experts))
    dense = 2 * capacity >= tok_dev and experts % 4 == 0 and tok_dev % PASSAGE == 0
    return (dense_shards if dense else slot_shards)(tokens, *rest)


def solution(mesh):
    return jax.shard_map(
        shards,
        mesh=mesh,
        in_specs=(
            P(("ep", "dp"), None),
            P(("ep", "dp"), None),
            P(("ep", "dp"), None),
            P("ep", None, None),
            P("ep", None, None),
            P("ep", None, None),
            P(),
            P(("ep", "dp")),
        ),
        out_specs=(P(("ep", "dp"), None), P()),
        check_vma=False,
    )
```

```python
import math

import jax
import jax.numpy as jnp
from jax import lax
from jax.experimental import pallas as pl
from jax.experimental.pallas import tpu as pltpu
from jax.sharding import PartitionSpec as P

TOP = 8
PASSAGE = 128


def expert_rows(rows, gate_rows, wg_single, wu_single, wd_single):
    gate_part = jnp.dot(rows, wg_single, preferred_element_type=jnp.float32)
    up_part = jnp.dot(rows, wu_single, preferred_element_type=jnp.float32)
    hidden = (jax.nn.silu(gate_part) * up_part).astype(jnp.bfloat16)
    result = jnp.dot(hidden, wd_single, preferred_element_type=jnp.float32)
    return (gate_rows.astype(jnp.float32)[:, None] * result).astype(jnp.bfloat16)


def run_expert(slot_rows, slot_gates, wg_single, wu_single, wd_single):
    width = slot_rows.shape[-1]
    rows = slot_rows.reshape(-1, width)
    gate_rows = slot_gates.reshape(-1)
    result = expert_rows(rows, gate_rows, wg_single, wu_single, wd_single)
    return result.reshape(slot_rows.shape)


def slot_shards(tokens, routes, gates, w_gate, w_up, w_down, score_head, doc_ids):
    tok_dev, width = tokens.shape
    experts = lax.axis_size("ep")
    capacity = min(tok_dev, 3 * tok_dev * TOP // (2 * experts))
    flat_routes = routes.reshape(-1)
    onehot = (flat_routes[:, None] == jnp.arange(experts, dtype=jnp.int32)[None, :]).astype(
        jnp.int32
    )
    ranked = jnp.cumsum(onehot, axis=0)
    slot = jnp.sum(ranked * onehot, axis=1) - 1
    destination = flat_routes * capacity + slot
    repeated = jnp.repeat(tokens, TOP, axis=0)
    send_rows = jnp.zeros((experts * capacity, width), jnp.bfloat16).at[destination].set(repeated)
    send_gates = (
        jnp.zeros((experts * capacity,), jnp.bfloat16).at[destination].set(gates.reshape(-1))
    )
    recv_rows, recv_gates = (
        lax.all_to_all(
            send_rows.reshape(experts, capacity, width),
            "ep",
            split_axis=0,
            concat_axis=0,
            tiled=True,
        ),
        lax.all_to_all(
            send_gates.reshape(experts, capacity), "ep", split_axis=0, concat_axis=0, tiled=True
        ),
    )
    wg_single = w_gate[0]
    wu_single = w_up[0]
    wd_single = w_down[0]
    results = run_expert(recv_rows, recv_gates, wg_single, wu_single, wd_single)
    returned = lax.all_to_all(results, "ep", split_axis=0, concat_axis=0, tiled=True)
    returned_flat = returned.reshape(experts * capacity, width)
    gathered = returned_flat[destination].astype(jnp.float32).reshape(tok_dev, TOP, width)
    mixed = jnp.sum(gathered, axis=1).astype(jnp.bfloat16)
    token_score = jnp.dot(mixed.astype(jnp.float32), score_head, precision=lax.Precision.HIGHEST)
    passage_score = token_score.reshape(-1, PASSAGE).sum(axis=1) / math.sqrt(PASSAGE)
    doc_count = lax.axis_size("ep") * lax.axis_size("dp") * tok_dev // PASSAGE // 4
    doc_range = jnp.arange(doc_count, dtype=jnp.int32)[None, :]
    all_scores, all_docs = (
        lax.all_gather(passage_score, ("ep", "dp"), axis=0, tiled=True),
        lax.all_gather(doc_ids.astype(jnp.float32), ("ep", "dp"), axis=0, tiled=True),
    )
    member = all_docs[:, None] == doc_range.astype(jnp.float32)
    column = all_scores[:, None]
    passage_index = jnp.arange(all_scores.shape[0], dtype=jnp.int32)[:, None]
    max_score = jnp.where(member, column, -1e30).max(axis=0)
    sum_score = jnp.where(member, column, 0.0).sum(axis=0)
    first_index = jnp.where(member, passage_index, all_scores.shape[0]).min(axis=0)
    first_score = jnp.where(member & (passage_index == first_index[None, :]), column, 0.0).sum(
        axis=0
    )
    return (mixed, jnp.stack([max_score, first_score, sum_score]))


def pool(all_scores, all_docs, doc_count):
    doc_range = jnp.arange(doc_count, dtype=jnp.int32)[None, :]
    member = all_docs[:, None] == doc_range.astype(jnp.float32)
    column = all_scores[:, None]
    passage_index = jnp.arange(all_scores.shape[0], dtype=jnp.int32)[:, None]
    max_score = jnp.where(member, column, -1e30).max(axis=0)
    sum_score = jnp.where(member, column, 0.0).sum(axis=0)
    first_index = jnp.where(member, passage_index, all_scores.shape[0]).min(axis=0)
    first_score = jnp.where(member & (passage_index == first_index[None, :]), column, 0.0).sum(
        axis=0
    )
    return jnp.stack([max_score, first_score, sum_score])


LANES = 128


def tile_of(extent, most):
    return most if extent % most == 0 else extent


def expert_kernel(
    xa, xb, wg0, wu0, wd0, wg1, wu1, wd1, gate, head, after,
    outa, outb, score,
    rows, hidden, scale, out, x_sem, out_sem,
):
    tok, width = xa.shape
    ff = wg0.shape[1]
    local = tok // PASSAGE
    ff_tile = tile_of(ff, 256)
    out_tile = tile_of(width, 512)
    blocks = [pl.ds(n * tok, tok) for n in range(2)]
    x_copies = [
        pltpu.make_async_copy(ref, rows.at[blocks[n], :], x_sem.at[n])
        for n, ref in enumerate((xa, xb))
    ]
    for copy in x_copies:
        copy.start()

    diagonal = lax.broadcasted_iota(jnp.int32, (tok, tok), 0) == lax.broadcasted_iota(
        jnp.int32, (tok, tok), 1
    )
    for n in range(2):
        for e in range(2):
            row = gate[pl.ds(2 * n + e, 1), :]
            scale[e, blocks[n], :] = jnp.sum(
                jnp.where(diagonal, row, 0.0), axis=1, keepdims=True
            )

    for copy in x_copies:
        copy.wait()
    for e, (wg, wu) in enumerate(((wg0, wu0), (wg1, wu1))):
        for j in range(ff // ff_tile):
            columns = pl.ds(j * ff_tile, ff_tile)
            gate_part = jnp.dot(rows[...], wg[:, columns], preferred_element_type=jnp.float32)
            up_part = jnp.dot(rows[...], wu[:, columns], preferred_element_type=jnp.float32)
            value = gate_part / (1.0 + jnp.exp(-gate_part)) * up_part
            hidden[e, :, columns] = value.astype(jnp.bfloat16)

    totals = [jnp.zeros((1, LANES), jnp.float32) for _ in range(2 * local)]
    out_copies = []
    for j in range(width // out_tile):
        columns = pl.ds(j * out_tile, out_tile)
        weighted = sum(
            scale[e] * jnp.dot(hidden[e], wd[:, columns], preferred_element_type=jnp.float32)
            for e, wd in enumerate((wd0, wd1))
        )
        out[:, columns] = weighted.astype(jnp.bfloat16)
        scored = weighted * head[:, columns]
        lanes = sum(
            scored[:, k * LANES : (k + 1) * LANES] for k in range(out_tile // LANES)
        )
        for p in range(2 * local):
            totals[p] += jnp.sum(lanes[p * PASSAGE : (p + 1) * PASSAGE], axis=0, keepdims=True)
        for n, ref in enumerate((outa, outb)):
            copy = pltpu.make_async_copy(
                out.at[blocks[n], columns], ref.at[:, columns], out_sem.at[n, j]
            )
            copy.start()
            out_copies.append(copy)
    for p in range(2 * local):
        score[pl.ds(p, 1), :] = totals[p]
    for copy in out_copies:
        copy.wait()


def load_kernel(first, *refs):
    count = (len(refs) - 1) // 2
    copies = [
        pltpu.make_async_copy(src, dst, refs[-1].at[n])
        for n, (src, dst) in enumerate(zip(refs[:count], refs[count:-1]))
    ]
    for copy in copies:
        copy.start()
    for copy in copies:
        copy.wait()


def load(arrays, first):
    arrays = [pltpu.with_memory_space_constraint(a, pltpu.HBM) for a in arrays]
    return pl.pallas_call(
        load_kernel,
        in_specs=[pl.BlockSpec(memory_space=pl.ANY)] * (1 + len(arrays)),
        out_specs=[pl.BlockSpec(memory_space=pltpu.VMEM)] * len(arrays),
        out_shape=[pltpu.VMEM(a.shape, a.dtype) for a in arrays],
        scratch_shapes=[pltpu.SemaphoreType.DMA((len(arrays),))],
        compiler_params=pltpu.CompilerParams(vmem_limit_bytes=2**20),
        name="load",
    )(first, *arrays)


def tie_kernel(value, first, passed):
    pass


def tie(value, first):
    anywhere = pl.BlockSpec(memory_space=pl.ANY)
    return pl.pallas_call(
        tie_kernel,
        in_specs=[anywhere, anywhere],
        out_specs=anywhere,
        out_shape=jax.ShapeDtypeStruct(value.shape, value.dtype),
        input_output_aliases={0: 0},
        compiler_params=pltpu.CompilerParams(vmem_limit_bytes=2**20),
        name="tie",
    )(value, first)


def expert_call(blocks, weights, gate, head, after):
    tok, width = blocks[0].shape
    ff = weights[0].shape[1]
    local = tok // PASSAGE
    anywhere = pl.BlockSpec(memory_space=pl.ANY)
    vmem = pl.BlockSpec(memory_space=pltpu.VMEM)
    bf16 = jnp.bfloat16
    return pl.pallas_call(
        expert_kernel,
        in_specs=[anywhere] * 2 + [vmem] * 8 + [anywhere],
        out_specs=[anywhere, anywhere, vmem],
        out_shape=[
            jax.ShapeDtypeStruct((tok, width), bf16),
            jax.ShapeDtypeStruct((tok, width), bf16),
            jax.ShapeDtypeStruct((2 * local, LANES), jnp.float32),
        ],
        scratch_shapes=[
            pltpu.VMEM((2 * tok, width), bf16),
            pltpu.VMEM((2, 2 * tok, ff), bf16),
            pltpu.VMEM((2, 2 * tok, 1), jnp.float32),
            pltpu.VMEM((2 * tok, width), bf16),
            pltpu.SemaphoreType.DMA((2,)),
            pltpu.SemaphoreType.DMA((2, width // tile_of(width, 512))),
        ],
        compiler_params=pltpu.CompilerParams(vmem_limit_bytes=16 * 2**20),
        cost_estimate=pl.CostEstimate(
            flops=24 * tok * width * ff,
            bytes_accessed=2 * (6 * width * ff + 4 * tok * width),
            transcendentals=4 * tok * ff,
        ),
        name="expert",
    )(*blocks, *weights, gate, head, after)


def dense_shards(tokens, routes, gates, w_gate, w_up, w_down, score_head, doc_ids):
    tok_dev, width = tokens.shape
    experts = lax.axis_size("ep")
    groups = lax.axis_size("dp")
    local = tok_dev // PASSAGE
    ring = experts // 4
    me = lax.axis_index("ep")
    onward = lambda v: lax.ppermute(
        v, "ep", [(i, (i + 4) % experts) for i in range(experts)]
    )
    across = lambda v: lax.ppermute(v, "ep", [(i, i ^ 2) for i in range(experts)])
    sibling = lambda v: lax.ppermute(v, "ep", [(i, i ^ 1) for i in range(experts)])

    near = [tokens]
    for s in range(1, ring):
        near.append(onward(near[-1]))
    far = [across(v) for v in near]
    own = (w_gate[0], w_up[0], w_down[0])


    chosen = routes[:, None, :] == jnp.arange(experts, dtype=jnp.int32)[None, :, None]
    dense_gates = jnp.where(chosen, gates[:, None, :], jnp.bfloat16(0)).sum(axis=2).T
    chip_gates = dense_gates.reshape(experts // 2, 2, tok_dev)
    sent_gates = jnp.stack([chip_gates, chip_gates[:, ::-1]], axis=1)
    gate_rows = lax.all_to_all(
        sent_gates.reshape(experts, 2 * tok_dev), "ep", split_axis=0, concat_axis=0, tiled=True
    )
    place = (me // 4 - jnp.arange(ring, dtype=jnp.int32)) % ring
    order = (place[:, None] * 4 + (me % 4 ^ jnp.array([0, 2], jnp.int32))[None, :]).reshape(-1)
    position = order[:, None] == jnp.arange(experts, dtype=jnp.int32)[None, :]
    slot_gates = gate_rows.astype(jnp.float32)[order].reshape(ring, 4, tok_dev)

    weights = tuple(load(own, slot_gates)) + tuple(sibling(w) for w in own)
    weights = tuple(pltpu.with_memory_space_constraint(w, pltpu.VMEM) for w in weights)

    head = score_head[None, :]
    scores = [None] * ring
    mine = [None] * ring
    other = [None] * ring
    after = far[0]
    turns = [*range(1, ring), 0]
    for s in turns:
        mine[s], other[s], scores[s] = expert_call(
            (near[s], far[s]), weights, slot_gates[s], head, after
        )
        after = scores[s]
    carried = None
    for s in turns:
        total = mine[s].astype(jnp.float32) + across(other[s]).astype(jnp.float32)
        if carried is not None:
            total = total + carried.astype(jnp.float32)
        total = total.astype(jnp.bfloat16)
        if s > 0:
            carried, last_sent = onward(total), total
    mixed = total

    slot_scores = jnp.stack(scores).sum(axis=2).reshape(2 * ring, local) / math.sqrt(PASSAGE)
    part_score = jnp.where(position[:, :, None], slot_scores[:, None, :], 0.0).sum(axis=0)
    told = jnp.concatenate([part_score.reshape(-1), doc_ids.astype(jnp.float32)])
    told = jnp.pad(told, (0, -told.shape[0] % LANES))[None, :]
    told = tie(told, last_sent)
    heard = lax.all_to_all(
        jnp.broadcast_to(told, (experts * groups, told.shape[1])),
        ("ep", "dp"),
        split_axis=0,
        concat_axis=0,
        tiled=True,
    )
    count = experts * local
    all_scores = heard[:, :count].reshape(experts, groups, experts, local).sum(axis=0)
    all_scores = all_scores.transpose(1, 0, 2).reshape(-1)
    all_docs = heard[:, count : count + local].reshape(-1)
    return (mixed, pool(all_scores, all_docs, count * groups // 4))


def shards(tokens, *rest):
    tok_dev = tokens.shape[0]
    experts = lax.axis_size("ep")
    capacity = min(tok_dev, 3 * tok_dev * TOP // (2 * experts))
    dense = 2 * capacity >= tok_dev and experts % 4 == 0 and tok_dev % PASSAGE == 0
    return (dense_shards if dense else slot_shards)(tokens, *rest)


def solution(mesh):
    return jax.shard_map(
        shards,
        mesh=mesh,
        in_specs=(
            P(("ep", "dp"), None),
            P(("ep", "dp"), None),
            P(("ep", "dp"), None),
            P("ep", None, None),
            P("ep", None, None),
            P("ep", None, None),
            P(),
            P(("ep", "dp")),
        ),
        out_specs=(P(("ep", "dp"), None), P()),
        check_vma=False,
    )
```

```python
import functools
import math

import jax
import jax.numpy as jnp
from jax import lax
from jax.experimental import pallas as pl
from jax.experimental.pallas import tpu as pltpu
from jax.sharding import PartitionSpec as P

TOP = 8
PASSAGE = 128


def expert_rows(rows, gate_rows, wg_single, wu_single, wd_single):
    gate_part = jnp.dot(rows, wg_single, preferred_element_type=jnp.float32)
    up_part = jnp.dot(rows, wu_single, preferred_element_type=jnp.float32)
    hidden = (jax.nn.silu(gate_part) * up_part).astype(jnp.bfloat16)
    result = jnp.dot(hidden, wd_single, preferred_element_type=jnp.float32)
    return (gate_rows.astype(jnp.float32)[:, None] * result).astype(jnp.bfloat16)


def run_expert(slot_rows, slot_gates, wg_single, wu_single, wd_single):
    width = slot_rows.shape[-1]
    rows = slot_rows.reshape(-1, width)
    gate_rows = slot_gates.reshape(-1)
    result = expert_rows(rows, gate_rows, wg_single, wu_single, wd_single)
    return result.reshape(slot_rows.shape)


def slot_shards(tokens, routes, gates, w_gate, w_up, w_down, score_head, doc_ids):
    tok_dev, width = tokens.shape
    experts = lax.axis_size("ep")
    capacity = min(tok_dev, 3 * tok_dev * TOP // (2 * experts))
    flat_routes = routes.reshape(-1)
    onehot = (flat_routes[:, None] == jnp.arange(experts, dtype=jnp.int32)[None, :]).astype(
        jnp.int32
    )
    ranked = jnp.cumsum(onehot, axis=0)
    slot = jnp.sum(ranked * onehot, axis=1) - 1
    destination = flat_routes * capacity + slot
    repeated = jnp.repeat(tokens, TOP, axis=0)
    send_rows = jnp.zeros((experts * capacity, width), jnp.bfloat16).at[destination].set(repeated)
    send_gates = (
        jnp.zeros((experts * capacity,), jnp.bfloat16).at[destination].set(gates.reshape(-1))
    )
    recv_rows, recv_gates = (
        lax.all_to_all(
            send_rows.reshape(experts, capacity, width),
            "ep",
            split_axis=0,
            concat_axis=0,
            tiled=True,
        ),
        lax.all_to_all(
            send_gates.reshape(experts, capacity), "ep", split_axis=0, concat_axis=0, tiled=True
        ),
    )
    wg_single = w_gate[0]
    wu_single = w_up[0]
    wd_single = w_down[0]
    results = run_expert(recv_rows, recv_gates, wg_single, wu_single, wd_single)
    returned = lax.all_to_all(results, "ep", split_axis=0, concat_axis=0, tiled=True)
    returned_flat = returned.reshape(experts * capacity, width)
    gathered = returned_flat[destination].astype(jnp.float32).reshape(tok_dev, TOP, width)
    mixed = jnp.sum(gathered, axis=1).astype(jnp.bfloat16)
    token_score = jnp.dot(mixed.astype(jnp.float32), score_head, precision=lax.Precision.HIGHEST)
    passage_score = token_score.reshape(-1, PASSAGE).sum(axis=1) / math.sqrt(PASSAGE)
    doc_count = lax.axis_size("ep") * lax.axis_size("dp") * tok_dev // PASSAGE // 4
    doc_range = jnp.arange(doc_count, dtype=jnp.int32)[None, :]
    all_scores, all_docs = (
        lax.all_gather(passage_score, ("ep", "dp"), axis=0, tiled=True),
        lax.all_gather(doc_ids.astype(jnp.float32), ("ep", "dp"), axis=0, tiled=True),
    )
    member = all_docs[:, None] == doc_range.astype(jnp.float32)
    column = all_scores[:, None]
    passage_index = jnp.arange(all_scores.shape[0], dtype=jnp.int32)[:, None]
    max_score = jnp.where(member, column, -1e30).max(axis=0)
    sum_score = jnp.where(member, column, 0.0).sum(axis=0)
    first_index = jnp.where(member, passage_index, all_scores.shape[0]).min(axis=0)
    first_score = jnp.where(member & (passage_index == first_index[None, :]), column, 0.0).sum(
        axis=0
    )
    return (mixed, jnp.stack([max_score, first_score, sum_score]))


def pool(all_scores, all_docs, doc_count):
    doc_range = jnp.arange(doc_count, dtype=jnp.int32)[None, :]
    member = all_docs[:, None] == doc_range.astype(jnp.float32)
    column = all_scores[:, None]
    passage_index = jnp.arange(all_scores.shape[0], dtype=jnp.int32)[:, None]
    max_score = jnp.where(member, column, -1e30).max(axis=0)
    sum_score = jnp.where(member, column, 0.0).sum(axis=0)
    first_index = jnp.where(member, passage_index, all_scores.shape[0]).min(axis=0)
    first_score = jnp.where(member & (passage_index == first_index[None, :]), column, 0.0).sum(
        axis=0
    )
    return jnp.stack([max_score, first_score, sum_score])


LANES = 128


def tile_of(extent, most):
    return most if extent % most == 0 else extent


def expert_kernel(
    slot, xa, xb, wg0, wu0, wd0, wg1, wu1, wd1, gate, head, after, held,
    outa, outb, score, passed,
    rows, hidden, scale, x_sem,
):
    tok, width = xa.shape
    local = tok // PASSAGE
    out_tile = tile_of(width, 1024)
    blocks = [pl.ds(n * tok, tok) for n in range(2)]
    x_copies = [
        pltpu.make_async_copy(ref, rows.at[blocks[n], :], x_sem.at[n])
        for n, ref in enumerate((xa, xb))
    ]
    for copy in x_copies:
        copy.start()

    diagonal = lax.broadcasted_iota(jnp.int32, (tok, tok), 0) == lax.broadcasted_iota(
        jnp.int32, (tok, tok), 1
    )
    for n in range(2):
        for e in range(2):
            row = gate[pl.ds(2 * slot + n, 1), pl.ds(e * tok, tok)]
            scale[e, blocks[n], :] = jnp.sum(
                jnp.where(diagonal, row, 0.0), axis=1, keepdims=True
            )

    for copy in x_copies:
        copy.wait()
    for e, (wg, wu) in enumerate(((wg0, wu0), (wg1, wu1))):
        gate_part = jnp.dot(rows[...], wg[...], preferred_element_type=jnp.float32)
        up_part = jnp.dot(rows[...], wu[...], preferred_element_type=jnp.float32)
        value = gate_part / (1.0 + jnp.exp(-gate_part)) * up_part
        hidden[e] = value.astype(jnp.bfloat16)

    totals = [jnp.zeros((1, LANES), jnp.float32) for _ in range(2 * local)]
    for j in range(width // out_tile):
        columns = pl.ds(j * out_tile, out_tile)
        weighted = sum(
            scale[e] * jnp.dot(hidden[e], wd[:, columns], preferred_element_type=jnp.float32)
            for e, wd in enumerate((wd0, wd1))
        )
        rounded = weighted.astype(jnp.bfloat16)
        outa[:, columns] = rounded[:tok]
        outb[:, columns] = rounded[tok:]
        scored = weighted * head[:, columns]
        lanes = sum(
            scored[:, k * LANES : (k + 1) * LANES] for k in range(out_tile // LANES)
        )
        for p in range(2 * local):
            totals[p] += jnp.sum(lanes[p * PASSAGE : (p + 1) * PASSAGE], axis=0, keepdims=True)
    for p in range(2 * local):
        score[pl.ds(p, 1), :] = totals[p]


def load_kernel(first, *refs):
    count = (len(refs) - 1) // 2
    copies = [
        pltpu.make_async_copy(src, dst, refs[-1].at[n])
        for n, (src, dst) in enumerate(zip(refs[:count], refs[count:-1]))
    ]
    for copy in copies:
        copy.start()
    for copy in copies:
        copy.wait()


def load(arrays, first):
    arrays = [pltpu.with_memory_space_constraint(a, pltpu.HBM) for a in arrays]
    return pl.pallas_call(
        load_kernel,
        in_specs=[pl.BlockSpec(memory_space=pl.ANY)] * (1 + len(arrays)),
        out_specs=[pl.BlockSpec(memory_space=pltpu.VMEM)] * len(arrays),
        out_shape=[pltpu.VMEM(a.shape, a.dtype) for a in arrays],
        scratch_shapes=[pltpu.SemaphoreType.DMA((len(arrays),))],
        compiler_params=pltpu.CompilerParams(vmem_limit_bytes=2**20),
        name="load",
    )(first, *arrays)


def tie_kernel(*refs):
    pass


def tie(value, *firsts):
    anywhere = pl.BlockSpec(memory_space=pl.ANY)
    return pl.pallas_call(
        tie_kernel,
        in_specs=[anywhere] * (1 + len(firsts)),
        out_specs=anywhere,
        out_shape=jax.ShapeDtypeStruct(value.shape, value.dtype),
        input_output_aliases={0: 0},
        compiler_params=pltpu.CompilerParams(vmem_limit_bytes=2**20),
        name="tie",
    )(value, *firsts)


def expert_call(slot, blocks, weights, gate, head, after, held):
    tok, width = blocks[0].shape
    ff = weights[0].shape[1]
    local = tok // PASSAGE
    anywhere = pl.BlockSpec(memory_space=pl.ANY)
    vmem = pl.BlockSpec(memory_space=pltpu.VMEM)
    bf16 = jnp.bfloat16
    return pl.pallas_call(
        functools.partial(expert_kernel, slot),
        in_specs=[anywhere] * 2 + [vmem] * 8 + [anywhere, anywhere],
        out_specs=[vmem, vmem, vmem, anywhere],
        out_shape=[
            pltpu.VMEM((tok, width), bf16),
            pltpu.VMEM((tok, width), bf16),
            jax.ShapeDtypeStruct((2 * local, LANES), jnp.float32),
            jax.ShapeDtypeStruct(held.shape, held.dtype),
        ],
        input_output_aliases={11: 3},
        scratch_shapes=[
            pltpu.VMEM((2 * tok, width), bf16),
            pltpu.VMEM((2, 2 * tok, ff), bf16),
            pltpu.VMEM((2, 2 * tok, 1), jnp.float32),
            pltpu.SemaphoreType.DMA((2,)),
        ],
        compiler_params=pltpu.CompilerParams(vmem_limit_bytes=16 * 2**20),
        cost_estimate=pl.CostEstimate(flops=1, bytes_accessed=1, transcendentals=0),
        name="expert",
    )(*blocks, *weights, gate, head, after, held)


def dense_shards(tokens, routes, gates, w_gate, w_up, w_down, score_head, doc_ids):
    tok_dev, width = tokens.shape
    experts = lax.axis_size("ep")
    groups = lax.axis_size("dp")
    local = tok_dev // PASSAGE
    ring = experts // 4
    me = lax.axis_index("ep")
    onward = lambda v: lax.ppermute(
        v, "ep", [(i, (i + 4) % experts) for i in range(experts)]
    )
    across = lambda v: lax.ppermute(v, "ep", [(i, i ^ 2) for i in range(experts)])
    sibling = lambda v: lax.ppermute(v, "ep", [(i, i ^ 1) for i in range(experts)])

    own = (w_gate[0], w_up[0], w_down[0])

    chosen = routes[:, None, :] == jnp.arange(experts, dtype=jnp.int32)[None, :, None]
    dense_gates = jnp.where(chosen, gates[:, None, :], jnp.bfloat16(0)).sum(axis=2).T
    chip_gates = dense_gates.reshape(experts // 2, 2, tok_dev)
    sent_gates = jnp.stack([chip_gates, chip_gates[:, ::-1]], axis=1)
    sent_gates = sent_gates.reshape(experts, 2 * tok_dev)
    gate_rows = lax.all_to_all(sent_gates, "ep", split_axis=0, concat_axis=0, tiled=True)
    row = jnp.arange(2 * ring, dtype=jnp.int32)
    order = lax.rem(me // 4 - row // 2 + ring, ring) * 4 + (me % 4 ^ row % 2 * 2)
    position = order[:, None] == jnp.arange(experts, dtype=jnp.int32)[None, :]
    slot_gates = gate_rows.astype(jnp.float32)[order]

    near = [tokens]
    far = [across(tokens)]

    def step(meanwhile):
        near.append(tie(onward(near[-1]), far[-1], meanwhile))
        far.append(across(near[-1]))

    head = score_head[None, :]
    scores = [None] * ring
    mine = [None] * ring
    other = [None] * ring

    def work(s, after, held):
        mine[s], other[s], scores[s], passed = expert_call(
            s, (near[s], far[s]), weights, slot_gates, head, after, held
        )
        return passed

    step(sent_gates)
    weights = load(own, slot_gates)
    step(weights[0])
    weights = weights + load([sibling(w) for w in own], slot_gates)
    weights = [pltpu.with_memory_space_constraint(w, pltpu.VMEM) for w in weights]
    held = jnp.zeros((8, LANES), jnp.float32)
    turns = [1, 0, *range(2, ring)]
    for n, s in enumerate(turns):
        if n == ring - 1:
            other[0] = work(s, held, other[0])
        else:
            held = work(s, near[-1], held)
        if len(near) < ring:
            step(scores[s])
    carried = None
    sent = []
    for s in [*range(1, ring), 0]:
        total = mine[s].astype(jnp.float32) + across(other[s]).astype(jnp.float32)
        if carried is not None:
            total = total + carried.astype(jnp.float32)
        total = total.astype(jnp.bfloat16)
        if s > 0:
            carried = onward(total)
            sent.append(total)
    mixed = total

    slot_scores = jnp.stack(scores).sum(axis=2).reshape(2 * ring, local) / math.sqrt(PASSAGE)
    part_score = jnp.where(position[:, :, None], slot_scores[:, None, :], 0.0).sum(axis=0)
    told = jnp.concatenate([part_score.reshape(-1), doc_ids.astype(jnp.float32)])
    told = jnp.pad(told, (0, -told.shape[0] % LANES))[None, :]
    told = tie(told, sent[-2])
    heard = lax.all_to_all(
        jnp.broadcast_to(told, (experts * groups, told.shape[1])),
        ("ep", "dp"),
        split_axis=0,
        concat_axis=0,
        tiled=True,
    )
    count = experts * local
    all_scores = heard[:, :count].reshape(experts, groups, experts, local).sum(axis=0)
    all_scores = all_scores.transpose(1, 0, 2).reshape(-1)
    all_docs = heard[:, count : count + local].reshape(-1)
    return (mixed, pool(all_scores, all_docs, count * groups // 4))


def shards(tokens, *rest):
    tok_dev = tokens.shape[0]
    experts = lax.axis_size("ep")
    capacity = min(tok_dev, 3 * tok_dev * TOP // (2 * experts))
    dense = 2 * capacity >= tok_dev and experts % 4 == 0 and tok_dev % PASSAGE == 0
    return (dense_shards if dense else slot_shards)(tokens, *rest)


def solution(mesh):
    return jax.shard_map(
        shards,
        mesh=mesh,
        in_specs=(
            P(("ep", "dp"), None),
            P(("ep", "dp"), None),
            P(("ep", "dp"), None),
            P("ep", None, None),
            P("ep", None, None),
            P("ep", None, None),
            P(),
            P(("ep", "dp")),
        ),
        out_specs=(P(("ep", "dp"), None), P()),
        check_vma=False,
    )
```

```python
import functools
import math

import jax
import jax.numpy as jnp
from jax import lax
from jax.experimental import pallas as pl
from jax.experimental.pallas import tpu as pltpu
from jax.sharding import PartitionSpec as P

TOP = 8
PASSAGE = 128


def expert_rows(rows, gate_rows, wg_single, wu_single, wd_single):
    gate_part = jnp.dot(rows, wg_single, preferred_element_type=jnp.float32)
    up_part = jnp.dot(rows, wu_single, preferred_element_type=jnp.float32)
    hidden = (jax.nn.silu(gate_part) * up_part).astype(jnp.bfloat16)
    result = jnp.dot(hidden, wd_single, preferred_element_type=jnp.float32)
    return (gate_rows.astype(jnp.float32)[:, None] * result).astype(jnp.bfloat16)


def run_expert(slot_rows, slot_gates, wg_single, wu_single, wd_single):
    width = slot_rows.shape[-1]
    rows = slot_rows.reshape(-1, width)
    gate_rows = slot_gates.reshape(-1)
    result = expert_rows(rows, gate_rows, wg_single, wu_single, wd_single)
    return result.reshape(slot_rows.shape)


def slot_shards(tokens, routes, gates, w_gate, w_up, w_down, score_head, doc_ids):
    tok_dev, width = tokens.shape
    experts = lax.axis_size("ep")
    capacity = min(tok_dev, 3 * tok_dev * TOP // (2 * experts))
    flat_routes = routes.reshape(-1)
    onehot = (flat_routes[:, None] == jnp.arange(experts, dtype=jnp.int32)[None, :]).astype(
        jnp.int32
    )
    ranked = jnp.cumsum(onehot, axis=0)
    slot = jnp.sum(ranked * onehot, axis=1) - 1
    destination = flat_routes * capacity + slot
    repeated = jnp.repeat(tokens, TOP, axis=0)
    send_rows = jnp.zeros((experts * capacity, width), jnp.bfloat16).at[destination].set(repeated)
    send_gates = (
        jnp.zeros((experts * capacity,), jnp.bfloat16).at[destination].set(gates.reshape(-1))
    )
    recv_rows, recv_gates = (
        lax.all_to_all(
            send_rows.reshape(experts, capacity, width),
            "ep",
            split_axis=0,
            concat_axis=0,
            tiled=True,
        ),
        lax.all_to_all(
            send_gates.reshape(experts, capacity), "ep", split_axis=0, concat_axis=0, tiled=True
        ),
    )
    wg_single = w_gate[0]
    wu_single = w_up[0]
    wd_single = w_down[0]
    results = run_expert(recv_rows, recv_gates, wg_single, wu_single, wd_single)
    returned = lax.all_to_all(results, "ep", split_axis=0, concat_axis=0, tiled=True)
    returned_flat = returned.reshape(experts * capacity, width)
    gathered = returned_flat[destination].astype(jnp.float32).reshape(tok_dev, TOP, width)
    mixed = jnp.sum(gathered, axis=1).astype(jnp.bfloat16)
    token_score = jnp.dot(mixed.astype(jnp.float32), score_head, precision=lax.Precision.HIGHEST)
    passage_score = token_score.reshape(-1, PASSAGE).sum(axis=1) / math.sqrt(PASSAGE)
    doc_count = lax.axis_size("ep") * lax.axis_size("dp") * tok_dev // PASSAGE // 4
    doc_range = jnp.arange(doc_count, dtype=jnp.int32)[None, :]
    all_scores, all_docs = (
        lax.all_gather(passage_score, ("ep", "dp"), axis=0, tiled=True),
        lax.all_gather(doc_ids.astype(jnp.float32), ("ep", "dp"), axis=0, tiled=True),
    )
    member = all_docs[:, None] == doc_range.astype(jnp.float32)
    column = all_scores[:, None]
    passage_index = jnp.arange(all_scores.shape[0], dtype=jnp.int32)[:, None]
    max_score = jnp.where(member, column, -1e30).max(axis=0)
    sum_score = jnp.where(member, column, 0.0).sum(axis=0)
    first_index = jnp.where(member, passage_index, all_scores.shape[0]).min(axis=0)
    first_score = jnp.where(member & (passage_index == first_index[None, :]), column, 0.0).sum(
        axis=0
    )
    return (mixed, jnp.stack([max_score, first_score, sum_score]))


def pool(all_scores, all_docs, doc_count):
    doc_range = jnp.arange(doc_count, dtype=jnp.int32)[None, :]
    member = all_docs[:, None] == doc_range.astype(jnp.float32)
    column = all_scores[:, None]
    passage_index = jnp.arange(all_scores.shape[0], dtype=jnp.int32)[:, None]
    max_score = jnp.where(member, column, -1e30).max(axis=0)
    sum_score = jnp.where(member, column, 0.0).sum(axis=0)
    first_index = jnp.where(member, passage_index, all_scores.shape[0]).min(axis=0)
    first_score = jnp.where(member & (passage_index == first_index[None, :]), column, 0.0).sum(
        axis=0
    )
    return jnp.stack([max_score, first_score, sum_score])


LANES = 128


def tile_of(extent, most):
    return most if extent % most == 0 else extent


def expert_kernel(
    slot, xa, xb, wg0, wu0, wd0, wg1, wu1, wd1, gate, head, after, held,
    outa, outb, score, passed,
    rows, hidden, scale, x_sem,
):
    tok, width = xa.shape
    local = tok // PASSAGE
    out_tile = tile_of(width, 1024)
    blocks = [pl.ds(n * tok, tok) for n in range(2)]
    x_copies = [
        pltpu.make_async_copy(ref, rows.at[blocks[n], :], x_sem.at[n])
        for n, ref in enumerate((xa, xb))
    ]
    for copy in x_copies:
        copy.start()

    diagonal = lax.broadcasted_iota(jnp.int32, (tok, tok), 0) == lax.broadcasted_iota(
        jnp.int32, (tok, tok), 1
    )
    for n in range(2):
        for e in range(2):
            row = gate[pl.ds(2 * slot + n, 1), pl.ds(e * tok, tok)]
            scale[e, blocks[n], :] = jnp.sum(
                jnp.where(diagonal, row, 0.0), axis=1, keepdims=True
            )

    for copy in x_copies:
        copy.wait()
    for e, (wg, wu) in enumerate(((wg0, wu0), (wg1, wu1))):
        gate_part = jnp.dot(rows[...], wg[...], preferred_element_type=jnp.float32)
        up_part = jnp.dot(rows[...], wu[...], preferred_element_type=jnp.float32)
        value = gate_part / (1.0 + jnp.exp(-gate_part)) * up_part
        hidden[e] = value.astype(jnp.bfloat16)

    totals = [jnp.zeros((1, LANES), jnp.float32) for _ in range(2 * local)]
    for j in range(width // out_tile):
        columns = pl.ds(j * out_tile, out_tile)
        weighted = sum(
            scale[e] * jnp.dot(hidden[e], wd[:, columns], preferred_element_type=jnp.float32)
            for e, wd in enumerate((wd0, wd1))
        )
        rounded = weighted.astype(jnp.bfloat16)
        outa[:, columns] = rounded[:tok]
        outb[:, columns] = rounded[tok:]
        scored = weighted * head[:, columns]
        lanes = sum(
            scored[:, k * LANES : (k + 1) * LANES] for k in range(out_tile // LANES)
        )
        for p in range(2 * local):
            totals[p] += jnp.sum(lanes[p * PASSAGE : (p + 1) * PASSAGE], axis=0, keepdims=True)
    for p in range(2 * local):
        score[pl.ds(p, 1), :] = totals[p]


def load_kernel(first, *refs):
    count = (len(refs) - 1) // 2
    copies = [
        pltpu.make_async_copy(src, dst, refs[-1].at[n])
        for n, (src, dst) in enumerate(zip(refs[:count], refs[count:-1]))
    ]
    for copy in copies:
        copy.start()
    for copy in copies:
        copy.wait()


def load(arrays, first):
    arrays = [pltpu.with_memory_space_constraint(a, pltpu.HBM) for a in arrays]
    return pl.pallas_call(
        load_kernel,
        in_specs=[pl.BlockSpec(memory_space=pl.ANY)] * (1 + len(arrays)),
        out_specs=[pl.BlockSpec(memory_space=pltpu.VMEM)] * len(arrays),
        out_shape=[pltpu.VMEM(a.shape, a.dtype) for a in arrays],
        scratch_shapes=[pltpu.SemaphoreType.DMA((len(arrays),))],
        compiler_params=pltpu.CompilerParams(vmem_limit_bytes=2**20),
        name="load",
    )(first, *arrays)


def tie_kernel(*refs):
    pass


def tie(value, *firsts):
    anywhere = pl.BlockSpec(memory_space=pl.ANY)
    return pl.pallas_call(
        tie_kernel,
        in_specs=[anywhere] * (1 + len(firsts)),
        out_specs=anywhere,
        out_shape=jax.ShapeDtypeStruct(value.shape, value.dtype),
        input_output_aliases={0: 0},
        compiler_params=pltpu.CompilerParams(vmem_limit_bytes=2**20),
        name="tie",
    )(value, *firsts)


def expert_call(slot, blocks, weights, gate, head, after, held):
    tok, width = blocks[0].shape
    ff = weights[0].shape[1]
    local = tok // PASSAGE
    anywhere = pl.BlockSpec(memory_space=pl.ANY)
    vmem = pl.BlockSpec(memory_space=pltpu.VMEM)
    bf16 = jnp.bfloat16
    return pl.pallas_call(
        functools.partial(expert_kernel, slot),
        in_specs=[anywhere] * 2 + [vmem] * 8 + [anywhere, anywhere],
        out_specs=[vmem, vmem, vmem, anywhere],
        out_shape=[
            pltpu.VMEM((tok, width), bf16),
            pltpu.VMEM((tok, width), bf16),
            jax.ShapeDtypeStruct((2 * local, LANES), jnp.float32),
            jax.ShapeDtypeStruct(held.shape, held.dtype),
        ],
        input_output_aliases={11: 3},
        scratch_shapes=[
            pltpu.VMEM((2 * tok, width), bf16),
            pltpu.VMEM((2, 2 * tok, ff), bf16),
            pltpu.VMEM((2, 2 * tok, 1), jnp.float32),
            pltpu.SemaphoreType.DMA((2,)),
        ],
        compiler_params=pltpu.CompilerParams(vmem_limit_bytes=16 * 2**20),
        cost_estimate=pl.CostEstimate(flops=1, bytes_accessed=1, transcendentals=0),
        name="expert",
    )(*blocks, *weights, gate, head, after, held)


def dense_shards(tokens, routes, gates, w_gate, w_up, w_down, score_head, doc_ids):
    tok_dev, width = tokens.shape
    experts = lax.axis_size("ep")
    groups = lax.axis_size("dp")
    local = tok_dev // PASSAGE
    ring = experts // 4
    me = lax.axis_index("ep")
    onward = lambda v: lax.ppermute(
        v, "ep", [(i, (i + 4) % experts) for i in range(experts)]
    )
    across = lambda v: lax.ppermute(v, "ep", [(i, i ^ 2) for i in range(experts)])
    sibling = lambda v: lax.ppermute(v, "ep", [(i, i ^ 1) for i in range(experts)])

    own = (w_gate[0], w_up[0], w_down[0])

    target = jnp.arange(2 * experts, dtype=jnp.int32)
    wanted = target // 2 ^ target % 2
    chosen = routes.T[:, None, :] == wanted[None, :, None]
    sent_gates = jnp.where(chosen, gates.T[:, None, :], jnp.bfloat16(0)).sum(axis=0)
    sent_gates = sent_gates.reshape(experts, 2 * tok_dev)
    gate_rows = lax.all_to_all(sent_gates, "ep", split_axis=0, concat_axis=0, tiled=True)
    row = jnp.arange(2 * ring, dtype=jnp.int32)
    order = lax.rem(me // 4 - row // 2 + ring, ring) * 4 + (me % 4 ^ row % 2 * 2)
    position = order[:, None] == jnp.arange(experts, dtype=jnp.int32)[None, :]
    slot_gates = gate_rows.astype(jnp.float32)[order]

    near = [tokens]
    far = [across(tokens)]

    def step(*meanwhile):
        near.append(tie(onward(near[-1]), far[-1], *meanwhile))
        far.append(across(near[-1]))

    head = score_head[None, :]
    scores = [None] * ring
    mine = [None] * ring
    other = [None] * ring

    def work(s, after, held):
        mine[s], other[s], scores[s], passed = expert_call(
            s, (near[s], far[s]), weights, slot_gates, head, after, held
        )
        return passed

    step(slot_gates)
    weights = load(own, slot_gates)
    step(weights[0])
    weights = weights + load([sibling(w) for w in own], slot_gates)
    weights = [pltpu.with_memory_space_constraint(w, pltpu.VMEM) for w in weights]
    held = jnp.zeros((8, LANES), jnp.float32)
    turns = [1, 0, *range(2, ring)]
    for n, s in enumerate(turns):
        if n == ring - 1:
            other[0] = work(s, held, other[0])
        else:
            held = work(s, near[-1], held)
        if len(near) < ring:
            step(scores[s])
    carried = None
    sent = []
    for s in [*range(1, ring), 0]:
        theirs = across(other[s])
        total = mine[s].astype(jnp.float32) + theirs.astype(jnp.float32)
        if carried is not None:
            total = total + carried.astype(jnp.float32)
        total = total.astype(jnp.bfloat16)
        if s > 0:
            carried = onward(total)
            sent.append(total)
    mixed = total

    slot_scores = jnp.stack(scores).sum(axis=2).reshape(2 * ring, local) / math.sqrt(PASSAGE)
    part_score = jnp.where(position[:, :, None], slot_scores[:, None, :], 0.0).sum(axis=0)
    told = jnp.concatenate([part_score.reshape(-1), doc_ids.astype(jnp.float32)])
    told = jnp.pad(told, (0, -told.shape[0] % LANES))[None, :]
    told = tie(told, sent[-2])
    heard = lax.all_to_all(
        jnp.broadcast_to(told, (experts * groups, told.shape[1])),
        ("ep", "dp"),
        split_axis=0,
        concat_axis=0,
        tiled=True,
    )
    count = experts * local
    all_scores = heard[:, :count].reshape(experts, groups, experts, local).sum(axis=0)
    all_scores = all_scores.transpose(1, 0, 2).reshape(-1)
    all_docs = heard[:, count : count + local].reshape(-1)
    return (mixed, pool(all_scores, all_docs, count * groups // 4))


def shards(tokens, *rest):
    tok_dev = tokens.shape[0]
    experts = lax.axis_size("ep")
    capacity = min(tok_dev, 3 * tok_dev * TOP // (2 * experts))
    dense = 2 * capacity >= tok_dev and experts % 4 == 0 and tok_dev % PASSAGE == 0
    return (dense_shards if dense else slot_shards)(tokens, *rest)


def solution(mesh):
    return jax.shard_map(
        shards,
        mesh=mesh,
        in_specs=(
            P(("ep", "dp"), None),
            P(("ep", "dp"), None),
            P(("ep", "dp"), None),
            P("ep", None, None),
            P("ep", None, None),
            P("ep", None, None),
            P(),
            P(("ep", "dp")),
        ),
        out_specs=(P(("ep", "dp"), None), P()),
        check_vma=False,
    )
```

```python
import functools
import math

import jax
import jax.numpy as jnp
from jax import lax
from jax.experimental import pallas as pl
from jax.experimental.pallas import tpu as pltpu
from jax.sharding import PartitionSpec as P

TOP = 8
PASSAGE = 128


def expert_rows(rows, gate_rows, wg_single, wu_single, wd_single):
    gate_part = jnp.dot(rows, wg_single, preferred_element_type=jnp.float32)
    up_part = jnp.dot(rows, wu_single, preferred_element_type=jnp.float32)
    hidden = (jax.nn.silu(gate_part) * up_part).astype(jnp.bfloat16)
    result = jnp.dot(hidden, wd_single, preferred_element_type=jnp.float32)
    return (gate_rows.astype(jnp.float32)[:, None] * result).astype(jnp.bfloat16)


def run_expert(slot_rows, slot_gates, wg_single, wu_single, wd_single):
    width = slot_rows.shape[-1]
    rows = slot_rows.reshape(-1, width)
    gate_rows = slot_gates.reshape(-1)
    result = expert_rows(rows, gate_rows, wg_single, wu_single, wd_single)
    return result.reshape(slot_rows.shape)


def slot_shards(tokens, routes, gates, w_gate, w_up, w_down, score_head, doc_ids):
    tok_dev, width = tokens.shape
    experts = lax.axis_size("ep")
    capacity = min(tok_dev, 3 * tok_dev * TOP // (2 * experts))
    flat_routes = routes.reshape(-1)
    onehot = (flat_routes[:, None] == jnp.arange(experts, dtype=jnp.int32)[None, :]).astype(
        jnp.int32
    )
    ranked = jnp.cumsum(onehot, axis=0)
    slot = jnp.sum(ranked * onehot, axis=1) - 1
    destination = flat_routes * capacity + slot
    repeated = jnp.repeat(tokens, TOP, axis=0)
    send_rows = jnp.zeros((experts * capacity, width), jnp.bfloat16).at[destination].set(repeated)
    send_gates = (
        jnp.zeros((experts * capacity,), jnp.bfloat16).at[destination].set(gates.reshape(-1))
    )
    recv_rows, recv_gates = (
        lax.all_to_all(
            send_rows.reshape(experts, capacity, width),
            "ep",
            split_axis=0,
            concat_axis=0,
            tiled=True,
        ),
        lax.all_to_all(
            send_gates.reshape(experts, capacity), "ep", split_axis=0, concat_axis=0, tiled=True
        ),
    )
    wg_single = w_gate[0]
    wu_single = w_up[0]
    wd_single = w_down[0]
    results = run_expert(recv_rows, recv_gates, wg_single, wu_single, wd_single)
    returned = lax.all_to_all(results, "ep", split_axis=0, concat_axis=0, tiled=True)
    returned_flat = returned.reshape(experts * capacity, width)
    gathered = returned_flat[destination].astype(jnp.float32).reshape(tok_dev, TOP, width)
    mixed = jnp.sum(gathered, axis=1).astype(jnp.bfloat16)
    token_score = jnp.dot(mixed.astype(jnp.float32), score_head, precision=lax.Precision.HIGHEST)
    passage_score = token_score.reshape(-1, PASSAGE).sum(axis=1) / math.sqrt(PASSAGE)
    doc_count = lax.axis_size("ep") * lax.axis_size("dp") * tok_dev // PASSAGE // 4
    doc_range = jnp.arange(doc_count, dtype=jnp.int32)[None, :]
    all_scores, all_docs = (
        lax.all_gather(passage_score, ("ep", "dp"), axis=0, tiled=True),
        lax.all_gather(doc_ids.astype(jnp.float32), ("ep", "dp"), axis=0, tiled=True),
    )
    member = all_docs[:, None] == doc_range.astype(jnp.float32)
    column = all_scores[:, None]
    passage_index = jnp.arange(all_scores.shape[0], dtype=jnp.int32)[:, None]
    max_score = jnp.where(member, column, -1e30).max(axis=0)
    sum_score = jnp.where(member, column, 0.0).sum(axis=0)
    first_index = jnp.where(member, passage_index, all_scores.shape[0]).min(axis=0)
    first_score = jnp.where(member & (passage_index == first_index[None, :]), column, 0.0).sum(
        axis=0
    )
    return (mixed, jnp.stack([max_score, first_score, sum_score]))


def pool(all_scores, all_docs, doc_count):
    doc_range = jnp.arange(doc_count, dtype=jnp.int32)[None, :]
    member = all_docs[:, None] == doc_range.astype(jnp.float32)
    column = all_scores[:, None]
    passage_index = jnp.arange(all_scores.shape[0], dtype=jnp.int32)[:, None]
    max_score = jnp.where(member, column, -1e30).max(axis=0)
    sum_score = jnp.where(member, column, 0.0).sum(axis=0)
    first_index = jnp.where(member, passage_index, all_scores.shape[0]).min(axis=0)
    first_score = jnp.where(member & (passage_index == first_index[None, :]), column, 0.0).sum(
        axis=0
    )
    return jnp.stack([max_score, first_score, sum_score])


LANES = 128


def tile_of(extent, most):
    return most if extent % most == 0 else extent


def expert_kernel(slot, inputs, outputs, *refs):
    pieces, refs = refs[:inputs], refs[inputs:]
    (wg0, wu0, wd0, wg1, wu1, wd1, gate, head, after, held), refs = refs[:10], refs[10:]
    results, refs = refs[:outputs], refs[outputs:]
    score, passed, rows, hidden, scale, x_sem = refs
    tok, width = pieces[0].shape
    local = tok // PASSAGE
    out_tile = tile_of(width, 1024)
    blocks = [pl.ds(n * tok, tok) for n in range(2)]
    x_copies, start = [], 0
    for n, ref in enumerate(pieces):
        place = rows.at[pl.ds(start, ref.shape[0]), :]
        x_copies.append(pltpu.make_async_copy(ref, place, x_sem.at[n]))
        start += ref.shape[0]
    for copy in x_copies:
        copy.start()

    diagonal = lax.broadcasted_iota(jnp.int32, (tok, tok), 0) == lax.broadcasted_iota(
        jnp.int32, (tok, tok), 1
    )
    for n in range(2):
        for e in range(2):
            row = gate[pl.ds(2 * slot + n, 1), pl.ds(e * tok, tok)]
            scale[e, blocks[n], :] = jnp.sum(
                jnp.where(diagonal, row, 0.0), axis=1, keepdims=True
            )

    for copy in x_copies:
        copy.wait()
    for e, (wg, wu) in enumerate(((wg0, wu0), (wg1, wu1))):
        gate_part = jnp.dot(rows[...], wg[...], preferred_element_type=jnp.float32)
        up_part = jnp.dot(rows[...], wu[...], preferred_element_type=jnp.float32)
        value = gate_part / (1.0 + jnp.exp(-gate_part)) * up_part
        hidden[e] = value.astype(jnp.bfloat16)

    totals = [jnp.zeros((1, LANES), jnp.float32) for _ in range(2 * local)]
    for j in range(width // out_tile):
        columns = pl.ds(j * out_tile, out_tile)
        weighted = sum(
            scale[e] * jnp.dot(hidden[e], wd[:, columns], preferred_element_type=jnp.float32)
            for e, wd in enumerate((wd0, wd1))
        )
        rounded = weighted.astype(jnp.bfloat16)
        start = 0
        for ref in results:
            ref[:, columns] = rounded[start : start + ref.shape[0]]
            start += ref.shape[0]
        scored = weighted * head[:, columns]
        lanes = sum(
            scored[:, k * LANES : (k + 1) * LANES] for k in range(out_tile // LANES)
        )
        for p in range(2 * local):
            totals[p] += jnp.sum(lanes[p * PASSAGE : (p + 1) * PASSAGE], axis=0, keepdims=True)
    for p in range(2 * local):
        score[pl.ds(p, 1), :] = totals[p]


def load_kernel(count, *refs):
    refs = refs[-2 * count - 1 :]
    copies = [
        pltpu.make_async_copy(src, dst, refs[-1].at[n])
        for n, (src, dst) in enumerate(zip(refs[:count], refs[count:-1]))
    ]
    for copy in copies:
        copy.start()
    for copy in copies:
        copy.wait()


def load(arrays, *firsts):
    arrays = [pltpu.with_memory_space_constraint(a, pltpu.HBM) for a in arrays]
    return pl.pallas_call(
        functools.partial(load_kernel, len(arrays)),
        in_specs=[pl.BlockSpec(memory_space=pl.ANY)] * (len(firsts) + len(arrays)),
        out_specs=[pl.BlockSpec(memory_space=pltpu.VMEM)] * len(arrays),
        out_shape=[pltpu.VMEM(a.shape, a.dtype) for a in arrays],
        scratch_shapes=[pltpu.SemaphoreType.DMA((len(arrays),))],
        compiler_params=pltpu.CompilerParams(vmem_limit_bytes=2**20),
        name="load",
    )(*firsts, *arrays)


def tie_kernel(*refs):
    pass


def tie(value, *firsts):
    anywhere = pl.BlockSpec(memory_space=pl.ANY)
    return pl.pallas_call(
        tie_kernel,
        in_specs=[anywhere] * (1 + len(firsts)),
        out_specs=anywhere,
        out_shape=jax.ShapeDtypeStruct(value.shape, value.dtype),
        input_output_aliases={0: 0},
        compiler_params=pltpu.CompilerParams(vmem_limit_bytes=2**20),
        name="tie",
    )(value, *firsts)


def expert_call(slot, pieces, out_rows, weights, gate, head, after, held):
    tok, width = pieces[0].shape
    ff = weights[0].shape[1]
    local = tok // PASSAGE
    count = len(pieces)
    anywhere = pl.BlockSpec(memory_space=pl.ANY)
    vmem = pl.BlockSpec(memory_space=pltpu.VMEM)
    bf16 = jnp.bfloat16
    return pl.pallas_call(
        functools.partial(expert_kernel, slot, count, len(out_rows)),
        in_specs=[anywhere] * count + [vmem] * 8 + [anywhere, anywhere],
        out_specs=[vmem] * len(out_rows) + [vmem, anywhere],
        out_shape=[pltpu.VMEM((rows, width), bf16) for rows in out_rows]
        + [
            jax.ShapeDtypeStruct((2 * local, LANES), jnp.float32),
            jax.ShapeDtypeStruct(held.shape, held.dtype),
        ],
        input_output_aliases={count + 9: len(out_rows) + 1},
        scratch_shapes=[
            pltpu.VMEM((2 * tok, width), bf16),
            pltpu.VMEM((2, 2 * tok, ff), bf16),
            pltpu.VMEM((2, 2 * tok, 1), jnp.float32),
            pltpu.SemaphoreType.DMA((count,)),
        ],
        compiler_params=pltpu.CompilerParams(vmem_limit_bytes=16 * 2**20),
        cost_estimate=pl.CostEstimate(flops=1, bytes_accessed=1, transcendentals=0),
        name="expert",
    )(*pieces, *weights, gate, head, after, held)


def dense_shards(tokens, routes, gates, w_gate, w_up, w_down, score_head, doc_ids):
    tok_dev, width = tokens.shape
    experts = lax.axis_size("ep")
    groups = lax.axis_size("dp")
    local = tok_dev // PASSAGE
    ring = experts // 4
    me = lax.axis_index("ep")
    onward = lambda v: lax.ppermute(
        v, "ep", [(i, (i + 4) % experts) for i in range(experts)]
    )
    across = lambda v: lax.ppermute(v, "ep", [(i, i ^ 2) for i in range(experts)])
    sibling = lambda v: lax.ppermute(v, "ep", [(i, i ^ 1) for i in range(experts)])

    own = (w_gate[0], w_up[0], w_down[0])

    target = jnp.arange(2 * experts, dtype=jnp.int32)
    wanted = target // 2 ^ target % 2
    chosen = routes.T[:, None, :] == wanted[None, :, None]
    sent_gates = jnp.where(chosen, gates.T[:, None, :], jnp.bfloat16(0)).sum(axis=0)
    sent_gates = sent_gates.reshape(experts, 2 * tok_dev)
    gate_rows = lax.all_to_all(sent_gates, "ep", split_axis=0, concat_axis=0, tiled=True)
    def place_of(row):
        return lax.rem(me // 4 - row // 2 + ring, ring) * 4 + (me % 4 ^ row % 2 * 2)

    order = place_of(jnp.arange(2 * ring, dtype=jnp.int32))
    slot_gates = gate_rows.astype(jnp.float32)[order]

    passages = experts * groups * local
    lane = jnp.arange(passages * 2 + -passages * 2 % LANES, dtype=jnp.int32)[:, None]
    part = jnp.arange(2 * ring * local, dtype=jnp.int32)
    at = lax.rem(part, local)
    score_lane = (place_of(part // local) * groups + lax.axis_index("dp")) * local + at
    first = passages + (me * groups + lax.axis_index("dp")) * local
    doc_lane = first + jnp.arange(local, dtype=jnp.int32)

    half = tok_dev // 2
    near = [tokens]
    far = [(across(tokens),)]

    def step(*meanwhile):
        near.append(tie(onward(near[-1]), *far[-1], *meanwhile))
        if len(near) < ring:
            far.append((across(near[-1]),))
        else:
            far.append((across(near[-1][:half]), onward(far[-1][0][half:])))

    head = score_head[None, :]
    scores = [None] * ring
    mine = [None] * ring
    other = [None] * ring

    def work(s, after, held):
        split = (half, half) if s in (0, ring - 1) else (tok_dev,)
        mine[s], *other[s], scores[s], passed = expert_call(
            s, (near[s], *far[s]), (tok_dev, *split), weights, slot_gates, head, after, held
        )
        return passed

    step(slot_gates)
    weights = load(own, slot_gates, score_lane, doc_lane)
    step(weights[0])
    weights = weights + load([sibling(w) for w in own], slot_gates)
    weights = [pltpu.with_memory_space_constraint(w, pltpu.VMEM) for w in weights]
    held = jnp.zeros((8, LANES), jnp.float32)
    turns = [1, 0, *range(2, ring)]
    for n, s in enumerate(turns):
        if n == ring - 1:
            other[0][0] = work(s, held, other[0][0])
        else:
            held = tie(held, *far[-1]) if n == 2 else held
            held = work(s, near[-1], held)
        if len(near) < ring:
            step(scores[s])
    joined = onward(other[-1].pop()).astype(jnp.float32) + other[0][1].astype(jnp.float32)
    other[0][1] = joined.astype(jnp.bfloat16)
    crossed = [[across(v) for v in pieces] for pieces in other]
    mine[-2] = tie(mine[-2], scores[-1])
    mine[-1] = tie(mine[-1], *crossed[0])
    carried = None
    sent = []
    for s in [*range(1, ring), 0]:
        theirs = [v.astype(jnp.float32) for v in crossed[s]]
        if s == ring - 1:
            theirs.append(jnp.zeros((half, width), jnp.float32))
        total = mine[s].astype(jnp.float32) + jnp.concatenate(theirs, axis=0)
        if carried is not None:
            total = total + carried.astype(jnp.float32)
        total = total.astype(jnp.bfloat16)
        if s > 0:
            carried = onward(total)
            sent.append(total)
    mixed = total

    slot_scores = jnp.stack(scores).sum(axis=2).reshape(-1) / math.sqrt(PASSAGE)
    totals = jnp.where(lane == score_lane[None, :], slot_scores[None, :], 0.0).sum(axis=1)
    docs = doc_ids.astype(jnp.float32)
    totals = totals + jnp.where(lane == doc_lane[None, :], docs[None, :], 0.0).sum(axis=1)
    totals = totals[None, :]
    moments = {1: sent[-2], 2: other[0][1]}
    for n, axis, apart in [
        (n, axis, 1 << n)
        for axis in ("ep", "dp")
        for n in range(lax.axis_size(axis).bit_length() - 1)
    ]:
        pairs = [(i, i ^ apart) for i in range(lax.axis_size(axis))]
        if axis == "ep" and n in moments:
            totals = tie(totals, moments[n])
        totals = totals + lax.ppermute(totals, axis, pairs)
    return (mixed, pool(totals[0, :passages], totals[0, passages : 2 * passages], passages // 4))


def shards(tokens, *rest):
    tok_dev = tokens.shape[0]
    experts = lax.axis_size("ep")
    capacity = min(tok_dev, 3 * tok_dev * TOP // (2 * experts))
    dense = 2 * capacity >= tok_dev and tok_dev % PASSAGE == 0 and experts > 8
    for size in (experts, lax.axis_size("dp")):
        dense = dense and size & (size - 1) == 0
    return (dense_shards if dense else slot_shards)(tokens, *rest)


def solution(mesh):
    return jax.shard_map(
        shards,
        mesh=mesh,
        in_specs=(
            P(("ep", "dp"), None),
            P(("ep", "dp"), None),
            P(("ep", "dp"), None),
            P("ep", None, None),
            P("ep", None, None),
            P("ep", None, None),
            P(),
            P(("ep", "dp")),
        ),
        out_specs=(P(("ep", "dp"), None), P()),
        check_vma=False,
    )
```

```python
import functools
import math

import jax
import jax.numpy as jnp
from jax import lax
from jax.experimental import pallas as pl
from jax.experimental.pallas import tpu as pltpu
from jax.sharding import PartitionSpec as P

TOP = 8
PASSAGE = 128


def expert_rows(rows, gate_rows, wg_single, wu_single, wd_single):
    gate_part = jnp.dot(rows, wg_single, preferred_element_type=jnp.float32)
    up_part = jnp.dot(rows, wu_single, preferred_element_type=jnp.float32)
    hidden = (jax.nn.silu(gate_part) * up_part).astype(jnp.bfloat16)
    result = jnp.dot(hidden, wd_single, preferred_element_type=jnp.float32)
    return (gate_rows.astype(jnp.float32)[:, None] * result).astype(jnp.bfloat16)


def run_expert(slot_rows, slot_gates, wg_single, wu_single, wd_single):
    width = slot_rows.shape[-1]
    rows = slot_rows.reshape(-1, width)
    gate_rows = slot_gates.reshape(-1)
    result = expert_rows(rows, gate_rows, wg_single, wu_single, wd_single)
    return result.reshape(slot_rows.shape)


def slot_shards(tokens, routes, gates, w_gate, w_up, w_down, score_head, doc_ids):
    tok_dev, width = tokens.shape
    experts = lax.axis_size("ep")
    capacity = min(tok_dev, 3 * tok_dev * TOP // (2 * experts))
    flat_routes = routes.reshape(-1)
    onehot = (flat_routes[:, None] == jnp.arange(experts, dtype=jnp.int32)[None, :]).astype(
        jnp.int32
    )
    ranked = jnp.cumsum(onehot, axis=0)
    slot = jnp.sum(ranked * onehot, axis=1) - 1
    destination = flat_routes * capacity + slot
    repeated = jnp.repeat(tokens, TOP, axis=0)
    send_rows = jnp.zeros((experts * capacity, width), jnp.bfloat16).at[destination].set(repeated)
    send_gates = (
        jnp.zeros((experts * capacity,), jnp.bfloat16).at[destination].set(gates.reshape(-1))
    )
    recv_rows, recv_gates = (
        lax.all_to_all(
            send_rows.reshape(experts, capacity, width),
            "ep",
            split_axis=0,
            concat_axis=0,
            tiled=True,
        ),
        lax.all_to_all(
            send_gates.reshape(experts, capacity), "ep", split_axis=0, concat_axis=0, tiled=True
        ),
    )
    wg_single = w_gate[0]
    wu_single = w_up[0]
    wd_single = w_down[0]
    results = run_expert(recv_rows, recv_gates, wg_single, wu_single, wd_single)
    returned = lax.all_to_all(results, "ep", split_axis=0, concat_axis=0, tiled=True)
    returned_flat = returned.reshape(experts * capacity, width)
    gathered = returned_flat[destination].astype(jnp.float32).reshape(tok_dev, TOP, width)
    mixed = jnp.sum(gathered, axis=1).astype(jnp.bfloat16)
    token_score = jnp.dot(mixed.astype(jnp.float32), score_head, precision=lax.Precision.HIGHEST)
    passage_score = token_score.reshape(-1, PASSAGE).sum(axis=1) / math.sqrt(PASSAGE)
    doc_count = lax.axis_size("ep") * lax.axis_size("dp") * tok_dev // PASSAGE // 4
    doc_range = jnp.arange(doc_count, dtype=jnp.int32)[None, :]
    all_scores, all_docs = (
        lax.all_gather(passage_score, ("ep", "dp"), axis=0, tiled=True),
        lax.all_gather(doc_ids.astype(jnp.float32), ("ep", "dp"), axis=0, tiled=True),
    )
    member = all_docs[:, None] == doc_range.astype(jnp.float32)
    column = all_scores[:, None]
    passage_index = jnp.arange(all_scores.shape[0], dtype=jnp.int32)[:, None]
    max_score = jnp.where(member, column, -1e30).max(axis=0)
    sum_score = jnp.where(member, column, 0.0).sum(axis=0)
    first_index = jnp.where(member, passage_index, all_scores.shape[0]).min(axis=0)
    first_score = jnp.where(member & (passage_index == first_index[None, :]), column, 0.0).sum(
        axis=0
    )
    return (mixed, jnp.stack([max_score, first_score, sum_score]))


def pool(all_scores, all_docs, doc_count):
    doc_range = jnp.arange(doc_count, dtype=jnp.int32)[None, :]
    member = all_docs[:, None] == doc_range.astype(jnp.float32)
    column = all_scores[:, None]
    passage_index = jnp.arange(all_scores.shape[0], dtype=jnp.int32)[:, None]
    max_score = jnp.where(member, column, -1e30).max(axis=0)
    sum_score = jnp.where(member, column, 0.0).sum(axis=0)
    first_index = jnp.where(member, passage_index, all_scores.shape[0]).min(axis=0)
    first_score = jnp.where(member & (passage_index == first_index[None, :]), column, 0.0).sum(
        axis=0
    )
    return jnp.stack([max_score, first_score, sum_score])


LANES = 128


def tile_of(extent, most):
    return most if extent % most == 0 else extent


def expert_kernel(
    slot, xa, xb, wg0, wu0, wd0, wg1, wu1, wd1, gate, head, after, held,
    outa, outb, score, passed,
    rows, hidden, scale, x_sem,
):
    tok, width = xa.shape
    local = tok // PASSAGE
    out_tile = tile_of(width, 1024)
    blocks = [pl.ds(n * tok, tok) for n in range(2)]
    x_copies = [
        pltpu.make_async_copy(ref, rows.at[blocks[n], :], x_sem.at[n])
        for n, ref in enumerate((xa, xb))
    ]
    for copy in x_copies:
        copy.start()

    diagonal = lax.broadcasted_iota(jnp.int32, (tok, tok), 0) == lax.broadcasted_iota(
        jnp.int32, (tok, tok), 1
    )
    for n in range(2):
        for e in range(2):
            row = gate[pl.ds(2 * slot + n, 1), pl.ds(e * tok, tok)]
            scale[e, blocks[n], :] = jnp.sum(
                jnp.where(diagonal, row, 0.0), axis=1, keepdims=True
            )

    for copy in x_copies:
        copy.wait()
    for e, (wg, wu) in enumerate(((wg0, wu0), (wg1, wu1))):
        gate_part = jnp.dot(rows[...], wg[...], preferred_element_type=jnp.float32)
        up_part = jnp.dot(rows[...], wu[...], preferred_element_type=jnp.float32)
        value = gate_part / (1.0 + jnp.exp(-gate_part)) * up_part
        hidden[e] = value.astype(jnp.bfloat16)

    totals = [jnp.zeros((1, LANES), jnp.float32) for _ in range(2 * local)]
    for j in range(width // out_tile):
        columns = pl.ds(j * out_tile, out_tile)
        weighted = sum(
            scale[e] * jnp.dot(hidden[e], wd[:, columns], preferred_element_type=jnp.float32)
            for e, wd in enumerate((wd0, wd1))
        )
        rounded = weighted.astype(jnp.bfloat16)
        outa[:, columns] = rounded[:tok]
        outb[:, columns] = rounded[tok:]
        scored = weighted * head[:, columns]
        lanes = sum(
            scored[:, k * LANES : (k + 1) * LANES] for k in range(out_tile // LANES)
        )
        for p in range(2 * local):
            totals[p] += jnp.sum(lanes[p * PASSAGE : (p + 1) * PASSAGE], axis=0, keepdims=True)
    for p in range(2 * local):
        score[pl.ds(p, 1), :] = totals[p]


def load_kernel(first, *refs):
    count = (len(refs) - 1) // 2
    copies = [
        pltpu.make_async_copy(src, dst, refs[-1].at[n])
        for n, (src, dst) in enumerate(zip(refs[:count], refs[count:-1]))
    ]
    for copy in copies:
        copy.start()
    for copy in copies:
        copy.wait()


def load(arrays, first):
    arrays = [pltpu.with_memory_space_constraint(a, pltpu.HBM) for a in arrays]
    return pl.pallas_call(
        load_kernel,
        in_specs=[pl.BlockSpec(memory_space=pl.ANY)] * (1 + len(arrays)),
        out_specs=[pl.BlockSpec(memory_space=pltpu.VMEM)] * len(arrays),
        out_shape=[pltpu.VMEM(a.shape, a.dtype) for a in arrays],
        scratch_shapes=[pltpu.SemaphoreType.DMA((len(arrays),))],
        compiler_params=pltpu.CompilerParams(vmem_limit_bytes=2**20),
        name="load",
    )(first, *arrays)


def tie_kernel(*refs):
    pass


def tie(value, *firsts):
    anywhere = pl.BlockSpec(memory_space=pl.ANY)
    return pl.pallas_call(
        tie_kernel,
        in_specs=[anywhere] * (1 + len(firsts)),
        out_specs=anywhere,
        out_shape=jax.ShapeDtypeStruct(value.shape, value.dtype),
        input_output_aliases={0: 0},
        compiler_params=pltpu.CompilerParams(vmem_limit_bytes=2**20),
        name="tie",
    )(value, *firsts)


def expert_call(slot, blocks, weights, gate, head, after, held):
    tok, width = blocks[0].shape
    ff = weights[0].shape[1]
    local = tok // PASSAGE
    anywhere = pl.BlockSpec(memory_space=pl.ANY)
    vmem = pl.BlockSpec(memory_space=pltpu.VMEM)
    bf16 = jnp.bfloat16
    return pl.pallas_call(
        functools.partial(expert_kernel, slot),
        in_specs=[anywhere] * 2 + [vmem] * 8 + [anywhere, anywhere],
        out_specs=[vmem, vmem, vmem, anywhere],
        out_shape=[
            pltpu.VMEM((tok, width), bf16),
            pltpu.VMEM((tok, width), bf16),
            jax.ShapeDtypeStruct((2 * local, LANES), jnp.float32),
            jax.ShapeDtypeStruct(held.shape, held.dtype),
        ],
        input_output_aliases={11: 3},
        scratch_shapes=[
            pltpu.VMEM((2 * tok, width), bf16),
            pltpu.VMEM((2, 2 * tok, ff), bf16),
            pltpu.VMEM((2, 2 * tok, 1), jnp.float32),
            pltpu.SemaphoreType.DMA((2,)),
        ],
        compiler_params=pltpu.CompilerParams(vmem_limit_bytes=16 * 2**20),
        cost_estimate=pl.CostEstimate(flops=1, bytes_accessed=1, transcendentals=0),
        name="expert",
    )(*blocks, *weights, gate, head, after, held)


def dense_shards(tokens, routes, gates, w_gate, w_up, w_down, score_head, doc_ids):
    tok_dev, width = tokens.shape
    experts = lax.axis_size("ep")
    groups = lax.axis_size("dp")
    local = tok_dev // PASSAGE
    ring = experts // 4
    me = lax.axis_index("ep")
    onward = lambda v: lax.ppermute(
        v, "ep", [(i, (i + 4) % experts) for i in range(experts)]
    )
    across = lambda v: lax.ppermute(v, "ep", [(i, i ^ 2) for i in range(experts)])
    sibling = lambda v: lax.ppermute(v, "ep", [(i, i ^ 1) for i in range(experts)])

    own = (w_gate[0], w_up[0], w_down[0])

    target = jnp.arange(2 * experts, dtype=jnp.int32)
    wanted = target // 2 ^ target % 2
    chosen = routes.T[:, None, :] == wanted[None, :, None]
    sent_gates = jnp.where(chosen, gates.T[:, None, :], jnp.bfloat16(0)).sum(axis=0)
    sent_gates = sent_gates.reshape(experts, 2 * tok_dev)
    gate_rows = lax.all_to_all(sent_gates, "ep", split_axis=0, concat_axis=0, tiled=True)
    row = jnp.arange(2 * ring, dtype=jnp.int32)
    order = lax.rem(me // 4 - row // 2 + ring, ring) * 4 + (me % 4 ^ row % 2 * 2)
    position = order[:, None] == jnp.arange(experts, dtype=jnp.int32)[None, :]
    slot_gates = gate_rows.astype(jnp.float32)[order]

    near = [tokens]
    far = [across(tokens)]

    def step(*meanwhile):
        near.append(tie(onward(near[-1]), far[-1], *meanwhile))
        far.append(across(near[-1]) if len(near) < ring else onward(far[-1]))

    head = score_head[None, :]
    scores = [None] * ring
    mine = [None] * ring
    other = [None] * ring

    def work(s, after, held):
        mine[s], other[s], scores[s], passed = expert_call(
            s, (near[s], far[s]), weights, slot_gates, head, after, held
        )
        return passed

    step(slot_gates)
    weights = load(own, slot_gates)
    step(weights[0])
    weights = weights + load([sibling(w) for w in own], slot_gates)
    weights = [pltpu.with_memory_space_constraint(w, pltpu.VMEM) for w in weights]
    held = jnp.zeros((8, LANES), jnp.float32)
    turns = [1, 0, *range(2, ring)]
    for n, s in enumerate(turns):
        if n == ring - 1:
            other[0] = work(s, held, other[0])
        else:
            held = work(s, near[-1], held)
        if len(near) < ring:
            step(scores[s])
    carried = None
    sent = []
    for s in [*range(1, ring), 0]:
        theirs = across(other[s])
        total = mine[s].astype(jnp.float32) + theirs.astype(jnp.float32)
        if carried is not None:
            total = total + carried.astype(jnp.float32)
        total = total.astype(jnp.bfloat16)
        if s > 0:
            carried = onward(total)
            sent.append(total)
    mixed = total

    slot_scores = jnp.stack(scores).sum(axis=2).reshape(2 * ring, local) / math.sqrt(PASSAGE)
    part_score = jnp.where(position[:, :, None], slot_scores[:, None, :], 0.0).sum(axis=0)
    told = jnp.concatenate([part_score.reshape(-1), doc_ids.astype(jnp.float32)])
    told = jnp.pad(told, (0, -told.shape[0] % LANES))[None, :]
    told = tie(told, sent[-2])
    heard = lax.all_to_all(
        jnp.broadcast_to(told, (experts * groups, told.shape[1])),
        ("ep", "dp"),
        split_axis=0,
        concat_axis=0,
        tiled=True,
    )
    count = experts * local
    all_scores = heard[:, :count].reshape(experts, groups, experts, local).sum(axis=0)
    all_scores = all_scores.transpose(1, 0, 2).reshape(-1)
    all_docs = heard[:, count : count + local].reshape(-1)
    return (mixed, pool(all_scores, all_docs, count * groups // 4))


def shards(tokens, *rest):
    tok_dev = tokens.shape[0]
    experts = lax.axis_size("ep")
    capacity = min(tok_dev, 3 * tok_dev * TOP // (2 * experts))
    dense = 2 * capacity >= tok_dev and experts % 4 == 0 and tok_dev % PASSAGE == 0
    return (dense_shards if dense else slot_shards)(tokens, *rest)


def solution(mesh):
    return jax.shard_map(
        shards,
        mesh=mesh,
        in_specs=(
            P(("ep", "dp"), None),
            P(("ep", "dp"), None),
            P(("ep", "dp"), None),
            P("ep", None, None),
            P("ep", None, None),
            P("ep", None, None),
            P(),
            P(("ep", "dp")),
        ),
        out_specs=(P(("ep", "dp"), None), P()),
        check_vma=False,
    )
```

```python
import functools
import math

import jax
import jax.numpy as jnp
from jax import lax
from jax.experimental import pallas as pl
from jax.experimental.pallas import tpu as pltpu
from jax.sharding import PartitionSpec as P

TOP = 8
PASSAGE = 128


def expert_rows(rows, gate_rows, wg_single, wu_single, wd_single):
    gate_part = jnp.dot(rows, wg_single, preferred_element_type=jnp.float32)
    up_part = jnp.dot(rows, wu_single, preferred_element_type=jnp.float32)
    hidden = (jax.nn.silu(gate_part) * up_part).astype(jnp.bfloat16)
    result = jnp.dot(hidden, wd_single, preferred_element_type=jnp.float32)
    return (gate_rows.astype(jnp.float32)[:, None] * result).astype(jnp.bfloat16)


def run_expert(slot_rows, slot_gates, wg_single, wu_single, wd_single):
    width = slot_rows.shape[-1]
    rows = slot_rows.reshape(-1, width)
    gate_rows = slot_gates.reshape(-1)
    result = expert_rows(rows, gate_rows, wg_single, wu_single, wd_single)
    return result.reshape(slot_rows.shape)


def slot_shards(tokens, routes, gates, w_gate, w_up, w_down, score_head, doc_ids):
    tok_dev, width = tokens.shape
    experts = lax.axis_size("ep")
    capacity = min(tok_dev, 3 * tok_dev * TOP // (2 * experts))
    flat_routes = routes.reshape(-1)
    onehot = (flat_routes[:, None] == jnp.arange(experts, dtype=jnp.int32)[None, :]).astype(
        jnp.int32
    )
    ranked = jnp.cumsum(onehot, axis=0)
    slot = jnp.sum(ranked * onehot, axis=1) - 1
    destination = flat_routes * capacity + slot
    repeated = jnp.repeat(tokens, TOP, axis=0)
    send_rows = jnp.zeros((experts * capacity, width), jnp.bfloat16).at[destination].set(repeated)
    send_gates = (
        jnp.zeros((experts * capacity,), jnp.bfloat16).at[destination].set(gates.reshape(-1))
    )
    recv_rows, recv_gates = (
        lax.all_to_all(
            send_rows.reshape(experts, capacity, width),
            "ep",
            split_axis=0,
            concat_axis=0,
            tiled=True,
        ),
        lax.all_to_all(
            send_gates.reshape(experts, capacity), "ep", split_axis=0, concat_axis=0, tiled=True
        ),
    )
    wg_single = w_gate[0]
    wu_single = w_up[0]
    wd_single = w_down[0]
    results = run_expert(recv_rows, recv_gates, wg_single, wu_single, wd_single)
    returned = lax.all_to_all(results, "ep", split_axis=0, concat_axis=0, tiled=True)
    returned_flat = returned.reshape(experts * capacity, width)
    gathered = returned_flat[destination].astype(jnp.float32).reshape(tok_dev, TOP, width)
    mixed = jnp.sum(gathered, axis=1).astype(jnp.bfloat16)
    token_score = jnp.dot(mixed.astype(jnp.float32), score_head, precision=lax.Precision.HIGHEST)
    passage_score = token_score.reshape(-1, PASSAGE).sum(axis=1) / math.sqrt(PASSAGE)
    doc_count = lax.axis_size("ep") * lax.axis_size("dp") * tok_dev // PASSAGE // 4
    doc_range = jnp.arange(doc_count, dtype=jnp.int32)[None, :]
    all_scores, all_docs = (
        lax.all_gather(passage_score, ("ep", "dp"), axis=0, tiled=True),
        lax.all_gather(doc_ids.astype(jnp.float32), ("ep", "dp"), axis=0, tiled=True),
    )
    member = all_docs[:, None] == doc_range.astype(jnp.float32)
    column = all_scores[:, None]
    passage_index = jnp.arange(all_scores.shape[0], dtype=jnp.int32)[:, None]
    max_score = jnp.where(member, column, -1e30).max(axis=0)
    sum_score = jnp.where(member, column, 0.0).sum(axis=0)
    first_index = jnp.where(member, passage_index, all_scores.shape[0]).min(axis=0)
    first_score = jnp.where(member & (passage_index == first_index[None, :]), column, 0.0).sum(
        axis=0
    )
    return (mixed, jnp.stack([max_score, first_score, sum_score]))


def pool(all_scores, all_docs, doc_count):
    doc_range = jnp.arange(doc_count, dtype=jnp.int32)[None, :]
    member = all_docs[:, None] == doc_range.astype(jnp.float32)
    column = all_scores[:, None]
    passage_index = jnp.arange(all_scores.shape[0], dtype=jnp.int32)[:, None]
    max_score = jnp.where(member, column, -1e30).max(axis=0)
    sum_score = jnp.where(member, column, 0.0).sum(axis=0)
    first_index = jnp.where(member, passage_index, all_scores.shape[0]).min(axis=0)
    first_score = jnp.where(member & (passage_index == first_index[None, :]), column, 0.0).sum(
        axis=0
    )
    return jnp.stack([max_score, first_score, sum_score])


LANES = 128


def tile_of(extent, most):
    return most if extent % most == 0 else extent


def expert_kernel(
    xa, xb, wg0, wu0, wd0, wg1, wu1, wd1, pick, head, after, held,
    outa, outb, score, passed,
    rows, gates, hidden, x_sem,
):
    tok = xa.shape[0]
    width = rows.shape[1]
    local = tok // PASSAGE
    out_tile = tile_of(width, 1024)
    x_copies = []
    for n, ref in enumerate((xa, xb)):
        block = pl.ds(n * tok, tok)
        for m, (first, dst) in enumerate(((0, rows), (width, gates))):
            src = ref.at[:, pl.ds(first, dst.shape[1])]
            x_copies.append(pltpu.make_async_copy(src, dst.at[block, :], x_sem.at[n, m]))
    for copy in x_copies:
        copy.start()

    for copy in x_copies:
        copy.wait()
    for e, (wg, wu) in enumerate(((wg0, wu0), (wg1, wu1))):
        gate_part = jnp.dot(rows[...], wg[...], preferred_element_type=jnp.float32)
        up_part = jnp.dot(rows[...], wu[...], preferred_element_type=jnp.float32)
        value = gate_part / (1.0 + jnp.exp(-gate_part)) * up_part
        hidden[e] = value.astype(jnp.bfloat16)

    scale = [
        jnp.sum(gates[...].astype(jnp.float32) * pick[pl.ds(e, 1), :], axis=1, keepdims=True)
        for e in range(2)
    ]
    totals = [jnp.zeros((1, LANES), jnp.float32) for _ in range(2 * local)]
    for j in range(width // out_tile):
        columns = pl.ds(j * out_tile, out_tile)
        weighted = sum(
            scale[e] * jnp.dot(hidden[e], wd[:, columns], preferred_element_type=jnp.float32)
            for e, wd in enumerate((wd0, wd1))
        )
        rounded = weighted.astype(jnp.bfloat16)
        outa[:, columns] = rounded[:tok]
        outb[:, columns] = rounded[tok:]
        scored = weighted * head[:, columns]
        lanes = sum(
            scored[:, k * LANES : (k + 1) * LANES] for k in range(out_tile // LANES)
        )
        for p in range(2 * local):
            totals[p] += jnp.sum(lanes[p * PASSAGE : (p + 1) * PASSAGE], axis=0, keepdims=True)
    for p in range(2 * local):
        score[pl.ds(p, 1), :] = totals[p]


def load_kernel(count, *refs):
    refs = refs[-2 * count - 1 :]
    copies = [
        pltpu.make_async_copy(src, dst, refs[-1].at[n])
        for n, (src, dst) in enumerate(zip(refs[:count], refs[count:-1]))
    ]
    for copy in copies:
        copy.start()
    for copy in copies:
        copy.wait()


def load(arrays, *firsts):
    arrays = [pltpu.with_memory_space_constraint(a, pltpu.HBM) for a in arrays]
    return pl.pallas_call(
        functools.partial(load_kernel, len(arrays)),
        in_specs=[pl.BlockSpec(memory_space=pl.ANY)] * (len(firsts) + len(arrays)),
        out_specs=[pl.BlockSpec(memory_space=pltpu.VMEM)] * len(arrays),
        out_shape=[pltpu.VMEM(a.shape, a.dtype) for a in arrays],
        scratch_shapes=[pltpu.SemaphoreType.DMA((len(arrays),))],
        compiler_params=pltpu.CompilerParams(vmem_limit_bytes=2**20),
        name="load",
    )(*firsts, *arrays)


def tie_kernel(*refs):
    pass


def tie(value, *firsts):
    anywhere = pl.BlockSpec(memory_space=pl.ANY)
    return pl.pallas_call(
        tie_kernel,
        in_specs=[anywhere] * (1 + len(firsts)),
        out_specs=anywhere,
        out_shape=jax.ShapeDtypeStruct(value.shape, value.dtype),
        input_output_aliases={0: 0},
        compiler_params=pltpu.CompilerParams(vmem_limit_bytes=2**20),
        name="tie",
    )(value, *firsts)


def expert_call(blocks, weights, pick, head, after, held):
    tok = blocks[0].shape[0]
    width = weights[0].shape[0]
    ff = weights[0].shape[1]
    local = tok // PASSAGE
    anywhere = pl.BlockSpec(memory_space=pl.ANY)
    vmem = pl.BlockSpec(memory_space=pltpu.VMEM)
    bf16 = jnp.bfloat16
    return pl.pallas_call(
        expert_kernel,
        in_specs=[anywhere] * 2 + [vmem] * 8 + [anywhere, anywhere],
        out_specs=[vmem, vmem, vmem, anywhere],
        out_shape=[
            pltpu.VMEM((tok, width), bf16),
            pltpu.VMEM((tok, width), bf16),
            jax.ShapeDtypeStruct((2 * local, LANES), jnp.float32),
            jax.ShapeDtypeStruct(held.shape, held.dtype),
        ],
        input_output_aliases={11: 3},
        scratch_shapes=[
            pltpu.VMEM((2 * tok, width), bf16),
            pltpu.VMEM((2 * tok, blocks[0].shape[1] - width), bf16),
            pltpu.VMEM((2, 2 * tok, ff), bf16),
            pltpu.SemaphoreType.DMA((2, 2)),
        ],
        compiler_params=pltpu.CompilerParams(vmem_limit_bytes=16 * 2**20),
        cost_estimate=pl.CostEstimate(flops=1, bytes_accessed=1, transcendentals=0),
        name="expert",
    )(*blocks, *weights, pick, head, after, held)


def dense_shards(tokens, routes, gates, w_gate, w_up, w_down, score_head, doc_ids):
    tok_dev, width = tokens.shape
    experts = lax.axis_size("ep")
    groups = lax.axis_size("dp")
    local = tok_dev // PASSAGE
    ring = experts // 4
    me = lax.axis_index("ep")
    onward = lambda v: lax.ppermute(
        v, "ep", [(i, (i + 4) % experts) for i in range(experts)]
    )
    across = lambda v: lax.ppermute(v, "ep", [(i, i ^ 2) for i in range(experts)])
    sibling = lambda v: lax.ppermute(v, "ep", [(i, i ^ 1) for i in range(experts)])

    own = (w_gate[0], w_up[0], w_down[0])

    lane = jnp.arange(experts + -experts % LANES, dtype=jnp.int32)
    chosen = routes[:, :, None] == lane[None, None, :]
    table = jnp.where(chosen, gates[:, :, None], jnp.bfloat16(0)).sum(axis=1)
    block = jnp.concatenate([tokens, table], axis=1)
    pick = lane[None, :] == (me ^ jnp.arange(2, dtype=jnp.int32))[:, None]
    pick = pick.astype(jnp.float32)
    row = jnp.arange(2 * ring, dtype=jnp.int32)
    order = lax.rem(me // 4 - row // 2 + ring, ring) * 4 + (me % 4 ^ row % 2 * 2)
    position = order[:, None] == jnp.arange(experts, dtype=jnp.int32)[None, :]
    turn = jnp.arange(groups, dtype=jnp.int32)
    source = lax.rem(lax.axis_index("dp") - turn + groups, groups)[:, None] == turn[None, :]
    source = source.astype(jnp.float32)

    near = [block]
    far = [across(block)]

    def step(*meanwhile):
        near.append(tie(onward(near[-1]), far[-1], *meanwhile))
        far.append(across(near[-1]) if len(near) < ring else onward(far[-1]))

    head = score_head[None, :]
    scores = [None] * ring
    mine = [None] * ring
    other = [None] * ring

    def work(s, after, held):
        mine[s], other[s], scores[s], passed = expert_call(
            (near[s], far[s]), weights, pick, head, after, held
        )
        return passed

    weights = load(own, pick, order, source)
    step(weights[0])
    weights = weights + load([sibling(w) for w in own], near[1])
    weights = [pltpu.with_memory_space_constraint(w, pltpu.VMEM) for w in weights]
    held = jnp.zeros((8, LANES), jnp.float32)
    for s in range(ring):
        if s == ring - 1:
            other[0] = work(s, held, other[0])
        else:
            held = work(s, near[-1], held)
        if len(near) < ring:
            step(scores[s])
    mine[1] = tie(mine[1], near[-1])
    mine[-2] = tie(mine[-2], scores[-1])
    crossed = [across(v) for v in other]
    carried = None
    sent = []
    for s in [*range(1, ring), 0]:
        theirs = across(other[s])
        total = mine[s].astype(jnp.float32) + theirs.astype(jnp.float32)
        if carried is not None:
            total = total + carried.astype(jnp.float32)
        total = total.astype(jnp.bfloat16)
        if s > 0:
            carried = onward(total)
            sent.append(total)
    mixed = total

    slot_scores = jnp.stack(scores).sum(axis=2).reshape(2 * ring, local) / math.sqrt(PASSAGE)
    part_score = jnp.where(position[:, :, None], slot_scores[:, None, :], 0.0).sum(axis=0)
    count = experts * local

    def in_lanes(*parts):
        line = jnp.concatenate(parts)
        return jnp.pad(line, (0, -line.shape[0] % LANES))[None, :]

    told = in_lanes(part_score.reshape(-1), doc_ids.astype(jnp.float32))
    told = tie(told, sent[-2], crossed[-1])
    heard = lax.all_to_all(
        jnp.broadcast_to(told, (experts, told.shape[1])),
        "ep",
        split_axis=0,
        concat_axis=0,
        tiled=True,
    )
    line = in_lanes(
        heard[:, :count].sum(axis=0), heard[:, count : count + local].reshape(-1)
    )
    lines = [line]
    for r in range(1, groups):
        pairs = [(i, (i + r) % groups) for i in range(groups)]
        lines.append(lax.ppermute(line, "dp", pairs))
    lines = (jnp.stack(lines) * source[:, :, None]).sum(axis=0)

    def in_order(part):
        return part.reshape(groups, experts, local).transpose(1, 0, 2).reshape(-1)

    all_scores, all_docs = (in_order(lines[:, n * count : (n + 1) * count]) for n in range(2))
    return (mixed, pool(all_scores, all_docs, count * groups // 4))


def shards(tokens, *rest):
    tok_dev = tokens.shape[0]
    experts = lax.axis_size("ep")
    capacity = min(tok_dev, 3 * tok_dev * TOP // (2 * experts))
    dense = 2 * capacity >= tok_dev and experts % 4 == 0 and tok_dev % PASSAGE == 0
    return (dense_shards if dense else slot_shards)(tokens, *rest)


def solution(mesh):
    return jax.shard_map(
        shards,
        mesh=mesh,
        in_specs=(
            P(("ep", "dp"), None),
            P(("ep", "dp"), None),
            P(("ep", "dp"), None),
            P("ep", None, None),
            P("ep", None, None),
            P("ep", None, None),
            P(),
            P(("ep", "dp")),
        ),
        out_specs=(P(("ep", "dp"), None), P()),
        check_vma=False,
    )
```

```python
import functools
import math

import jax
import jax.numpy as jnp
from jax import lax
from jax.experimental import pallas as pl
from jax.experimental.pallas import tpu as pltpu
from jax.sharding import PartitionSpec as P

TOP = 8
PASSAGE = 128


def expert_rows(rows, gate_rows, wg_single, wu_single, wd_single):
    gate_part = jnp.dot(rows, wg_single, preferred_element_type=jnp.float32)
    up_part = jnp.dot(rows, wu_single, preferred_element_type=jnp.float32)
    hidden = (jax.nn.silu(gate_part) * up_part).astype(jnp.bfloat16)
    result = jnp.dot(hidden, wd_single, preferred_element_type=jnp.float32)
    return (gate_rows.astype(jnp.float32)[:, None] * result).astype(jnp.bfloat16)


def run_expert(slot_rows, slot_gates, wg_single, wu_single, wd_single):
    width = slot_rows.shape[-1]
    rows = slot_rows.reshape(-1, width)
    gate_rows = slot_gates.reshape(-1)
    result = expert_rows(rows, gate_rows, wg_single, wu_single, wd_single)
    return result.reshape(slot_rows.shape)


def slot_shards(tokens, routes, gates, w_gate, w_up, w_down, score_head, doc_ids):
    tok_dev, width = tokens.shape
    experts = lax.axis_size("ep")
    capacity = min(tok_dev, 3 * tok_dev * TOP // (2 * experts))
    flat_routes = routes.reshape(-1)
    onehot = (flat_routes[:, None] == jnp.arange(experts, dtype=jnp.int32)[None, :]).astype(
        jnp.int32
    )
    ranked = jnp.cumsum(onehot, axis=0)
    slot = jnp.sum(ranked * onehot, axis=1) - 1
    destination = flat_routes * capacity + slot
    repeated = jnp.repeat(tokens, TOP, axis=0)
    send_rows = jnp.zeros((experts * capacity, width), jnp.bfloat16).at[destination].set(repeated)
    send_gates = (
        jnp.zeros((experts * capacity,), jnp.bfloat16).at[destination].set(gates.reshape(-1))
    )
    recv_rows, recv_gates = (
        lax.all_to_all(
            send_rows.reshape(experts, capacity, width),
            "ep",
            split_axis=0,
            concat_axis=0,
            tiled=True,
        ),
        lax.all_to_all(
            send_gates.reshape(experts, capacity), "ep", split_axis=0, concat_axis=0, tiled=True
        ),
    )
    wg_single = w_gate[0]
    wu_single = w_up[0]
    wd_single = w_down[0]
    results = run_expert(recv_rows, recv_gates, wg_single, wu_single, wd_single)
    returned = lax.all_to_all(results, "ep", split_axis=0, concat_axis=0, tiled=True)
    returned_flat = returned.reshape(experts * capacity, width)
    gathered = returned_flat[destination].astype(jnp.float32).reshape(tok_dev, TOP, width)
    mixed = jnp.sum(gathered, axis=1).astype(jnp.bfloat16)
    token_score = jnp.dot(mixed.astype(jnp.float32), score_head, precision=lax.Precision.HIGHEST)
    passage_score = token_score.reshape(-1, PASSAGE).sum(axis=1) / math.sqrt(PASSAGE)
    doc_count = lax.axis_size("ep") * lax.axis_size("dp") * tok_dev // PASSAGE // 4
    doc_range = jnp.arange(doc_count, dtype=jnp.int32)[None, :]
    all_scores, all_docs = (
        lax.all_gather(passage_score, ("ep", "dp"), axis=0, tiled=True),
        lax.all_gather(doc_ids.astype(jnp.float32), ("ep", "dp"), axis=0, tiled=True),
    )
    member = all_docs[:, None] == doc_range.astype(jnp.float32)
    column = all_scores[:, None]
    passage_index = jnp.arange(all_scores.shape[0], dtype=jnp.int32)[:, None]
    max_score = jnp.where(member, column, -1e30).max(axis=0)
    sum_score = jnp.where(member, column, 0.0).sum(axis=0)
    first_index = jnp.where(member, passage_index, all_scores.shape[0]).min(axis=0)
    first_score = jnp.where(member & (passage_index == first_index[None, :]), column, 0.0).sum(
        axis=0
    )
    return (mixed, jnp.stack([max_score, first_score, sum_score]))


def pool(all_scores, all_docs, doc_count):
    doc_range = jnp.arange(doc_count, dtype=jnp.int32)[None, :]
    member = all_docs[:, None] == doc_range.astype(jnp.float32)
    column = all_scores[:, None]
    passage_index = jnp.arange(all_scores.shape[0], dtype=jnp.int32)[:, None]
    max_score = jnp.where(member, column, -1e30).max(axis=0)
    sum_score = jnp.where(member, column, 0.0).sum(axis=0)
    first_index = jnp.where(member, passage_index, all_scores.shape[0]).min(axis=0)
    first_score = jnp.where(member & (passage_index == first_index[None, :]), column, 0.0).sum(
        axis=0
    )
    return jnp.stack([max_score, first_score, sum_score])


LANES = 128


def tile_of(extent, most):
    return most if extent % most == 0 else extent


def expert_kernel(
    slot, xa, xb, wg0, wu0, wd0, wg1, wu1, wd1, gate, head, after, held,
    outa, outb, score, passed,
    rows, hidden, scale, x_sem,
):
    tok, width = xa.shape
    local = tok // PASSAGE
    out_tile = tile_of(width, 1024)
    blocks = [pl.ds(n * tok, tok) for n in range(2)]
    x_copies = [
        pltpu.make_async_copy(ref, rows.at[blocks[n], :], x_sem.at[n])
        for n, ref in enumerate((xa, xb))
    ]
    for copy in x_copies:
        copy.start()

    diagonal = lax.broadcasted_iota(jnp.int32, (tok, tok), 0) == lax.broadcasted_iota(
        jnp.int32, (tok, tok), 1
    )
    for n in range(2):
        for e in range(2):
            row = gate[pl.ds(2 * slot + n, 1), pl.ds(e * tok, tok)]
            scale[e, blocks[n], :] = jnp.sum(
                jnp.where(diagonal, row, 0.0), axis=1, keepdims=True
            )

    for copy in x_copies:
        copy.wait()
    for e, (wg, wu) in enumerate(((wg0, wu0), (wg1, wu1))):
        gate_part = jnp.dot(rows[...], wg[...], preferred_element_type=jnp.float32)
        up_part = jnp.dot(rows[...], wu[...], preferred_element_type=jnp.float32)
        value = gate_part / (1.0 + jnp.exp(-gate_part)) * up_part
        hidden[e] = value.astype(jnp.bfloat16)

    totals = [jnp.zeros((1, LANES), jnp.float32) for _ in range(2 * local)]
    for j in range(width // out_tile):
        columns = pl.ds(j * out_tile, out_tile)
        weighted = sum(
            scale[e] * jnp.dot(hidden[e], wd[:, columns], preferred_element_type=jnp.float32)
            for e, wd in enumerate((wd0, wd1))
        )
        rounded = weighted.astype(jnp.bfloat16)
        outa[:, columns] = rounded[:tok]
        outb[:, columns] = rounded[tok:]
        scored = weighted * head[:, columns]
        lanes = sum(
            scored[:, k * LANES : (k + 1) * LANES] for k in range(out_tile // LANES)
        )
        for p in range(2 * local):
            totals[p] += jnp.sum(lanes[p * PASSAGE : (p + 1) * PASSAGE], axis=0, keepdims=True)
    for p in range(2 * local):
        score[pl.ds(p, 1), :] = totals[p]


def load_kernel(count, *refs):
    refs = refs[-2 * count - 1 :]
    copies = [
        pltpu.make_async_copy(src, dst, refs[-1].at[n])
        for n, (src, dst) in enumerate(zip(refs[:count], refs[count:-1]))
    ]
    for copy in copies:
        copy.start()
    for copy in copies:
        copy.wait()


def load(arrays, *firsts):
    arrays = [pltpu.with_memory_space_constraint(a, pltpu.HBM) for a in arrays]
    return pl.pallas_call(
        functools.partial(load_kernel, len(arrays)),
        in_specs=[pl.BlockSpec(memory_space=pl.ANY)] * (len(firsts) + len(arrays)),
        out_specs=[pl.BlockSpec(memory_space=pltpu.VMEM)] * len(arrays),
        out_shape=[pltpu.VMEM(a.shape, a.dtype) for a in arrays],
        scratch_shapes=[pltpu.SemaphoreType.DMA((len(arrays),))],
        compiler_params=pltpu.CompilerParams(vmem_limit_bytes=2**20),
        name="load",
    )(*firsts, *arrays)


def tie_kernel(*refs):
    pass


def tie(value, *firsts):
    anywhere = pl.BlockSpec(memory_space=pl.ANY)
    return pl.pallas_call(
        tie_kernel,
        in_specs=[anywhere] * (1 + len(firsts)),
        out_specs=anywhere,
        out_shape=jax.ShapeDtypeStruct(value.shape, value.dtype),
        input_output_aliases={0: 0},
        compiler_params=pltpu.CompilerParams(vmem_limit_bytes=2**20),
        name="tie",
    )(value, *firsts)


def expert_call(slot, blocks, weights, gate, head, after, held):
    tok, width = blocks[0].shape
    ff = weights[0].shape[1]
    local = tok // PASSAGE
    anywhere = pl.BlockSpec(memory_space=pl.ANY)
    vmem = pl.BlockSpec(memory_space=pltpu.VMEM)
    bf16 = jnp.bfloat16
    return pl.pallas_call(
        functools.partial(expert_kernel, slot),
        in_specs=[anywhere] * 2 + [vmem] * 8 + [anywhere, anywhere],
        out_specs=[vmem, vmem, vmem, anywhere],
        out_shape=[
            pltpu.VMEM((tok, width), bf16),
            pltpu.VMEM((tok, width), bf16),
            jax.ShapeDtypeStruct((2 * local, LANES), jnp.float32),
            jax.ShapeDtypeStruct(held.shape, held.dtype),
        ],
        input_output_aliases={11: 3},
        scratch_shapes=[
            pltpu.VMEM((2 * tok, width), bf16),
            pltpu.VMEM((2, 2 * tok, ff), bf16),
            pltpu.VMEM((2, 2 * tok, 1), jnp.float32),
            pltpu.SemaphoreType.DMA((2,)),
        ],
        compiler_params=pltpu.CompilerParams(vmem_limit_bytes=16 * 2**20),
        cost_estimate=pl.CostEstimate(flops=1, bytes_accessed=1, transcendentals=0),
        name="expert",
    )(*blocks, *weights, gate, head, after, held)


def dense_shards(tokens, routes, gates, w_gate, w_up, w_down, score_head, doc_ids):
    tok_dev, width = tokens.shape
    experts = lax.axis_size("ep")
    groups = lax.axis_size("dp")
    local = tok_dev // PASSAGE
    ring = experts // 4
    me = lax.axis_index("ep")
    places = [*range(0, ring, 2), *reversed(range(1, ring, 2))]
    onward = lambda v: lax.ppermute(
        v,
        "ep",
        [
            (4 * places[n] + i, 4 * places[(n + 1) % ring] + i)
            for n in range(ring)
            for i in range(4)
        ],
    )
    across = lambda v: lax.ppermute(v, "ep", [(i, i ^ 2) for i in range(experts)])
    sibling = lambda v: lax.ppermute(v, "ep", [(i, i ^ 1) for i in range(experts)])

    own = (w_gate[0], w_up[0], w_down[0])

    target = jnp.arange(2 * experts, dtype=jnp.int32)
    wanted = target // 2 ^ target % 2
    chosen = routes.T[:, None, :] == wanted[None, :, None]
    sent_gates = jnp.where(chosen, gates.T[:, None, :], jnp.bfloat16(0)).sum(axis=0)
    sent_gates = sent_gates.reshape(experts, 2 * tok_dev)
    gate_rows = lax.all_to_all(sent_gates, "ep", split_axis=0, concat_axis=0, tiled=True)
    row = jnp.arange(2 * ring, dtype=jnp.int32)
    z = me // 4
    at = jnp.where(z % 2 == 0, z // 2, ring - (z + 1) // 2)
    back = lax.rem(at - row // 2 + ring, ring)
    back = jnp.where(back < (ring + 1) // 2, 2 * back, 2 * (ring - back) - 1)
    order = back * 4 + (me % 4 ^ row % 2 * 2)
    position = order[:, None] == jnp.arange(experts, dtype=jnp.int32)[None, :]
    slot_gates = gate_rows.astype(jnp.float32)[order]

    near = [tokens]
    far = [across(tokens)]

    def step(*meanwhile):
        near.append(tie(onward(near[-1]), far[-1], *meanwhile))
        far.append(across(near[-1]) if len(near) < ring else onward(far[-1]))

    head = score_head[None, :]
    scores = [None] * ring
    mine = [None] * ring
    other = [None] * ring

    def work(s, after, held):
        mine[s], other[s], scores[s], passed = expert_call(
            s, (near[s], far[s]), weights, slot_gates, head, after, held
        )
        return passed

    step(slot_gates)
    weights = load(own, slot_gates)
    step(weights[0])
    weights = weights + load([sibling(w) for w in own], slot_gates)
    weights = [pltpu.with_memory_space_constraint(w, pltpu.VMEM) for w in weights]
    held = jnp.zeros((8, LANES), jnp.float32)
    turns = [1, 0, *range(2, ring)]
    for n, s in enumerate(turns):
        if n == ring - 1:
            other[0] = work(s, held, other[0])
        else:
            held = work(s, near[-1], held)
        if len(near) < ring:
            step(scores[s])
    carried = None
    sent = []
    for s in [*range(1, ring), 0]:
        crossing = tie(other[0], sent[-1]) if s == 0 else other[s]
        total = mine[s].astype(jnp.float32) + across(crossing).astype(jnp.float32)
        if carried is not None:
            total = total + carried.astype(jnp.float32)
        total = total.astype(jnp.bfloat16)
        if s > 0:
            carried = onward(total)
            sent.append(total)
    mixed = total

    slot_scores = jnp.stack(scores).sum(axis=2).reshape(2 * ring, local) / math.sqrt(PASSAGE)
    part_score = jnp.where(position[:, :, None], slot_scores[:, None, :], 0.0).sum(axis=0)
    told = jnp.concatenate([part_score.reshape(-1), doc_ids.astype(jnp.float32)])
    told = jnp.pad(told, (0, -told.shape[0] % LANES))[None, :]
    told = tie(told, sent[-2])
    heard = lax.all_to_all(
        jnp.broadcast_to(told, (experts * groups, told.shape[1])),
        ("ep", "dp"),
        split_axis=0,
        concat_axis=0,
        tiled=True,
    )
    count = experts * local
    all_scores = heard[:, :count].reshape(experts, groups, experts, local).sum(axis=0)
    all_scores = all_scores.transpose(1, 0, 2).reshape(-1)
    all_docs = heard[:, count : count + local].reshape(-1)
    return (mixed, pool(all_scores, all_docs, count * groups // 4))


def shards(tokens, *rest):
    tok_dev = tokens.shape[0]
    experts = lax.axis_size("ep")
    capacity = min(tok_dev, 3 * tok_dev * TOP // (2 * experts))
    dense = 2 * capacity >= tok_dev and experts % 4 == 0 and tok_dev % PASSAGE == 0
    return (dense_shards if dense else slot_shards)(tokens, *rest)


def solution(mesh):
    return jax.shard_map(
        shards,
        mesh=mesh,
        in_specs=(
            P(("ep", "dp"), None),
            P(("ep", "dp"), None),
            P(("ep", "dp"), None),
            P("ep", None, None),
            P("ep", None, None),
            P("ep", None, None),
            P(),
            P(("ep", "dp")),
        ),
        out_specs=(P(("ep", "dp"), None), P()),
        check_vma=False,
    )
```

```python
import functools
import math

import jax
import jax.numpy as jnp
from jax import lax
from jax.experimental import pallas as pl
from jax.experimental.pallas import tpu as pltpu
from jax.sharding import PartitionSpec as P

TOP = 8
PASSAGE = 128


def expert_rows(rows, gate_rows, wg_single, wu_single, wd_single):
    gate_part = jnp.dot(rows, wg_single, preferred_element_type=jnp.float32)
    up_part = jnp.dot(rows, wu_single, preferred_element_type=jnp.float32)
    hidden = (jax.nn.silu(gate_part) * up_part).astype(jnp.bfloat16)
    result = jnp.dot(hidden, wd_single, preferred_element_type=jnp.float32)
    return (gate_rows.astype(jnp.float32)[:, None] * result).astype(jnp.bfloat16)


def run_expert(slot_rows, slot_gates, wg_single, wu_single, wd_single):
    width = slot_rows.shape[-1]
    rows = slot_rows.reshape(-1, width)
    gate_rows = slot_gates.reshape(-1)
    result = expert_rows(rows, gate_rows, wg_single, wu_single, wd_single)
    return result.reshape(slot_rows.shape)


def slot_shards(tokens, routes, gates, w_gate, w_up, w_down, score_head, doc_ids):
    tok_dev, width = tokens.shape
    experts = lax.axis_size("ep")
    capacity = min(tok_dev, 3 * tok_dev * TOP // (2 * experts))
    flat_routes = routes.reshape(-1)
    onehot = (flat_routes[:, None] == jnp.arange(experts, dtype=jnp.int32)[None, :]).astype(
        jnp.int32
    )
    ranked = jnp.cumsum(onehot, axis=0)
    slot = jnp.sum(ranked * onehot, axis=1) - 1
    destination = flat_routes * capacity + slot
    repeated = jnp.repeat(tokens, TOP, axis=0)
    send_rows = jnp.zeros((experts * capacity, width), jnp.bfloat16).at[destination].set(repeated)
    send_gates = (
        jnp.zeros((experts * capacity,), jnp.bfloat16).at[destination].set(gates.reshape(-1))
    )
    recv_rows, recv_gates = (
        lax.all_to_all(
            send_rows.reshape(experts, capacity, width),
            "ep",
            split_axis=0,
            concat_axis=0,
            tiled=True,
        ),
        lax.all_to_all(
            send_gates.reshape(experts, capacity), "ep", split_axis=0, concat_axis=0, tiled=True
        ),
    )
    wg_single = w_gate[0]
    wu_single = w_up[0]
    wd_single = w_down[0]
    results = run_expert(recv_rows, recv_gates, wg_single, wu_single, wd_single)
    returned = lax.all_to_all(results, "ep", split_axis=0, concat_axis=0, tiled=True)
    returned_flat = returned.reshape(experts * capacity, width)
    gathered = returned_flat[destination].astype(jnp.float32).reshape(tok_dev, TOP, width)
    mixed = jnp.sum(gathered, axis=1).astype(jnp.bfloat16)
    token_score = jnp.dot(mixed.astype(jnp.float32), score_head, precision=lax.Precision.HIGHEST)
    passage_score = token_score.reshape(-1, PASSAGE).sum(axis=1) / math.sqrt(PASSAGE)
    doc_count = lax.axis_size("ep") * lax.axis_size("dp") * tok_dev // PASSAGE // 4
    doc_range = jnp.arange(doc_count, dtype=jnp.int32)[None, :]
    all_scores, all_docs = (
        lax.all_gather(passage_score, ("ep", "dp"), axis=0, tiled=True),
        lax.all_gather(doc_ids.astype(jnp.float32), ("ep", "dp"), axis=0, tiled=True),
    )
    member = all_docs[:, None] == doc_range.astype(jnp.float32)
    column = all_scores[:, None]
    passage_index = jnp.arange(all_scores.shape[0], dtype=jnp.int32)[:, None]
    max_score = jnp.where(member, column, -1e30).max(axis=0)
    sum_score = jnp.where(member, column, 0.0).sum(axis=0)
    first_index = jnp.where(member, passage_index, all_scores.shape[0]).min(axis=0)
    first_score = jnp.where(member & (passage_index == first_index[None, :]), column, 0.0).sum(
        axis=0
    )
    return (mixed, jnp.stack([max_score, first_score, sum_score]))


def pool(all_scores, all_docs, doc_count):
    doc_range = jnp.arange(doc_count, dtype=jnp.int32)[None, :]
    member = all_docs[:, None] == doc_range.astype(jnp.float32)
    column = all_scores[:, None]
    passage_index = jnp.arange(all_scores.shape[0], dtype=jnp.int32)[:, None]
    max_score = jnp.where(member, column, -1e30).max(axis=0)
    sum_score = jnp.where(member, column, 0.0).sum(axis=0)
    first_index = jnp.where(member, passage_index, all_scores.shape[0]).min(axis=0)
    first_score = jnp.where(member & (passage_index == first_index[None, :]), column, 0.0).sum(
        axis=0
    )
    return jnp.stack([max_score, first_score, sum_score])


LANES = 128


def tile_of(extent, most):
    return most if extent % most == 0 else extent


def expert_kernel(
    slot, xa, xb, wg0, wu0, wd0, wg1, wu1, wd1, gate, head, after, held,
    outa, outb, score, passed,
    rows, hidden, scale, x_sem,
):
    tok, width = xa.shape
    local = tok // PASSAGE
    out_tile = tile_of(width, 1024)
    blocks = [pl.ds(n * tok, tok) for n in range(2)]
    x_copies = [
        pltpu.make_async_copy(ref, rows.at[blocks[n], :], x_sem.at[n])
        for n, ref in enumerate((xa, xb))
    ]
    for copy in x_copies:
        copy.start()

    diagonal = lax.broadcasted_iota(jnp.int32, (tok, tok), 0) == lax.broadcasted_iota(
        jnp.int32, (tok, tok), 1
    )
    for n in range(2):
        for e in range(2):
            row = gate[pl.ds(2 * slot + n, 1), pl.ds(e * tok, tok)]
            scale[e, blocks[n], :] = jnp.sum(
                jnp.where(diagonal, row, 0.0), axis=1, keepdims=True
            )

    for copy in x_copies:
        copy.wait()
    for e, (wg, wu) in enumerate(((wg0, wu0), (wg1, wu1))):
        gate_part = jnp.dot(rows[...], wg[...], preferred_element_type=jnp.float32)
        up_part = jnp.dot(rows[...], wu[...], preferred_element_type=jnp.float32)
        value = gate_part / (1.0 + jnp.exp(-gate_part)) * up_part
        hidden[e] = value.astype(jnp.bfloat16)

    totals = [jnp.zeros((1, LANES), jnp.float32) for _ in range(2 * local)]
    for j in range(width // out_tile):
        columns = pl.ds(j * out_tile, out_tile)
        weighted = sum(
            scale[e] * jnp.dot(hidden[e], wd[:, columns], preferred_element_type=jnp.float32)
            for e, wd in enumerate((wd0, wd1))
        )
        rounded = weighted.astype(jnp.bfloat16)
        outa[:, columns] = rounded[:tok]
        outb[:, columns] = rounded[tok:]
        scored = weighted * head[:, columns]
        lanes = sum(
            scored[:, k * LANES : (k + 1) * LANES] for k in range(out_tile // LANES)
        )
        for p in range(2 * local):
            totals[p] += jnp.sum(lanes[p * PASSAGE : (p + 1) * PASSAGE], axis=0, keepdims=True)
    for p in range(2 * local):
        score[pl.ds(p, 1), :] = totals[p]


def load_kernel(count, *refs):
    refs = refs[-2 * count - 1 :]
    copies = [
        pltpu.make_async_copy(src, dst, refs[-1].at[n])
        for n, (src, dst) in enumerate(zip(refs[:count], refs[count:-1]))
    ]
    for copy in copies:
        copy.start()
    for copy in copies:
        copy.wait()


def load(arrays, *firsts):
    arrays = [pltpu.with_memory_space_constraint(a, pltpu.HBM) for a in arrays]
    return pl.pallas_call(
        functools.partial(load_kernel, len(arrays)),
        in_specs=[pl.BlockSpec(memory_space=pl.ANY)] * (len(firsts) + len(arrays)),
        out_specs=[pl.BlockSpec(memory_space=pltpu.VMEM)] * len(arrays),
        out_shape=[pltpu.VMEM(a.shape, a.dtype) for a in arrays],
        scratch_shapes=[pltpu.SemaphoreType.DMA((len(arrays),))],
        compiler_params=pltpu.CompilerParams(vmem_limit_bytes=2**20),
        name="load",
    )(*firsts, *arrays)


def tie_kernel(*refs):
    pass


def tie(value, *firsts):
    anywhere = pl.BlockSpec(memory_space=pl.ANY)
    return pl.pallas_call(
        tie_kernel,
        in_specs=[anywhere] * (1 + len(firsts)),
        out_specs=anywhere,
        out_shape=jax.ShapeDtypeStruct(value.shape, value.dtype),
        input_output_aliases={0: 0},
        compiler_params=pltpu.CompilerParams(vmem_limit_bytes=2**20),
        name="tie",
    )(value, *firsts)


def expert_call(slot, blocks, weights, gate, head, after, held):
    tok, width = blocks[0].shape
    ff = weights[0].shape[1]
    local = tok // PASSAGE
    anywhere = pl.BlockSpec(memory_space=pl.ANY)
    vmem = pl.BlockSpec(memory_space=pltpu.VMEM)
    bf16 = jnp.bfloat16
    return pl.pallas_call(
        functools.partial(expert_kernel, slot),
        in_specs=[anywhere] * 2 + [vmem] * 8 + [anywhere, anywhere],
        out_specs=[vmem, vmem, vmem, anywhere],
        out_shape=[
            pltpu.VMEM((tok, width), bf16),
            pltpu.VMEM((tok, width), bf16),
            jax.ShapeDtypeStruct((2 * local, LANES), jnp.float32),
            jax.ShapeDtypeStruct(held.shape, held.dtype),
        ],
        input_output_aliases={11: 3},
        scratch_shapes=[
            pltpu.VMEM((2 * tok, width), bf16),
            pltpu.VMEM((2, 2 * tok, ff), bf16),
            pltpu.VMEM((2, 2 * tok, 1), jnp.float32),
            pltpu.SemaphoreType.DMA((2,)),
        ],
        compiler_params=pltpu.CompilerParams(vmem_limit_bytes=16 * 2**20),
        cost_estimate=pl.CostEstimate(flops=1, bytes_accessed=1, transcendentals=0),
        name="expert",
    )(*blocks, *weights, gate, head, after, held)


def dense_shards(tokens, routes, gates, w_gate, w_up, w_down, score_head, doc_ids):
    tok_dev, width = tokens.shape
    experts = lax.axis_size("ep")
    groups = lax.axis_size("dp")
    local = tok_dev // PASSAGE
    ring = experts // 4
    me = lax.axis_index("ep")
    places = [*range(0, ring, 2), *reversed(range(1, ring, 2))]
    onward = lambda v: lax.ppermute(
        v,
        "ep",
        [
            (4 * places[n] + i, 4 * places[(n + 1) % ring] + i)
            for n in range(ring)
            for i in range(4)
        ],
    )
    across = lambda v: lax.ppermute(v, "ep", [(i, i ^ 2) for i in range(experts)])
    sibling = lambda v: lax.ppermute(v, "ep", [(i, i ^ 1) for i in range(experts)])

    own = (w_gate[0], w_up[0], w_down[0])

    target = jnp.arange(2 * experts, dtype=jnp.int32)
    wanted = target // 2 ^ target % 2
    chosen = routes.T[:, None, :] == wanted[None, :, None]
    sent_gates = jnp.where(chosen, gates.T[:, None, :], jnp.bfloat16(0)).sum(axis=0)
    sent_gates = sent_gates.reshape(experts, 2 * tok_dev)
    gate_rows = lax.all_to_all(sent_gates, "ep", split_axis=0, concat_axis=0, tiled=True)
    row = jnp.arange(2 * ring, dtype=jnp.int32)
    z = me // 4
    at = jnp.where(z % 2 == 0, z // 2, ring - (z + 1) // 2)
    back = lax.rem(at - row // 2 + ring, ring)
    back = jnp.where(back < (ring + 1) // 2, 2 * back, 2 * (ring - back) - 1)
    order = back * 4 + (me % 4 ^ row % 2 * 2)
    position = order[:, None] == jnp.arange(experts, dtype=jnp.int32)[None, :]
    slot_gates = gate_rows.astype(jnp.float32)[order]

    near = [tokens]
    far = [across(tokens)]

    def step(*meanwhile):
        near.append(tie(onward(near[-1]), far[-1], *meanwhile))
        far.append(across(near[-1]) if len(near) < ring else onward(far[-1]))

    head = score_head[None, :]
    scores = [None] * ring
    mine = [None] * ring
    other = [None] * ring

    def work(s, after, held):
        mine[s], other[s], scores[s], passed = expert_call(
            s, (near[s], far[s]), weights, slot_gates, head, after, held
        )
        return passed

    step(slot_gates)
    weights = load(own, slot_gates) + load([sibling(w) for w in own], slot_gates)
    step(weights[0], weights[-1])
    weights = [pltpu.with_memory_space_constraint(w, pltpu.VMEM) for w in weights]
    held = jnp.zeros((8, LANES), jnp.float32)
    for s in [1, 0, *range(2, ring)]:
        if s == ring - 1:
            other[0] = work(s, held, other[0])
        else:
            mark = sibling(tie(held, near[-1])) if s > 0 else near[-1]
            held = work(s, mark, held)
        if s != 1 and len(near) < ring:
            step(scores[s])
    mine[1] = tie(mine[1], scores[2])
    carried = None
    sent = []
    for s in [*range(1, ring), 0]:
        crossed = across(tie(other[0], crossed) if s == 0 else other[s])
        total = mine[s].astype(jnp.float32) + crossed.astype(jnp.float32)
        if carried is not None:
            total = total + carried.astype(jnp.float32)
        total = total.astype(jnp.bfloat16)
        if s > 0:
            carried = onward(total)
            sent.append(total)
    mixed = total

    slot_scores = jnp.stack(scores).sum(axis=2).reshape(2 * ring, local) / math.sqrt(PASSAGE)
    part_score = jnp.where(position[:, :, None], slot_scores[:, None, :], 0.0).sum(axis=0)
    told = jnp.concatenate([part_score.reshape(-1), doc_ids.astype(jnp.float32)])
    told = jnp.pad(told, (0, -told.shape[0] % LANES))[None, :]
    told = tie(told, sent[-2])
    heard = lax.all_to_all(
        jnp.broadcast_to(told, (experts * groups, told.shape[1])),
        ("ep", "dp"),
        split_axis=0,
        concat_axis=0,
        tiled=True,
    )
    count = experts * local
    all_scores = heard[:, :count].reshape(experts, groups, experts, local).sum(axis=0)
    all_scores = all_scores.transpose(1, 0, 2).reshape(-1)
    all_docs = heard[:, count : count + local].reshape(-1)
    return (mixed, pool(all_scores, all_docs, count * groups // 4))


def shards(tokens, *rest):
    tok_dev = tokens.shape[0]
    experts = lax.axis_size("ep")
    capacity = min(tok_dev, 3 * tok_dev * TOP // (2 * experts))
    dense = 2 * capacity >= tok_dev and experts % 4 == 0 and tok_dev % PASSAGE == 0
    return (dense_shards if dense else slot_shards)(tokens, *rest)


def solution(mesh):
    return jax.shard_map(
        shards,
        mesh=mesh,
        in_specs=(
            P(("ep", "dp"), None),
            P(("ep", "dp"), None),
            P(("ep", "dp"), None),
            P("ep", None, None),
            P("ep", None, None),
            P("ep", None, None),
            P(),
            P(("ep", "dp")),
        ),
        out_specs=(P(("ep", "dp"), None), P()),
        check_vma=False,
    )
```

```python
import functools
import math

import jax
import jax.numpy as jnp
from jax import lax
from jax.experimental import pallas as pl
from jax.experimental.pallas import tpu as pltpu
from jax.sharding import PartitionSpec as P

TOP = 8
PASSAGE = 128


def expert_rows(rows, gate_rows, wg_single, wu_single, wd_single):
    gate_part = jnp.dot(rows, wg_single, preferred_element_type=jnp.float32)
    up_part = jnp.dot(rows, wu_single, preferred_element_type=jnp.float32)
    hidden = (jax.nn.silu(gate_part) * up_part).astype(jnp.bfloat16)
    result = jnp.dot(hidden, wd_single, preferred_element_type=jnp.float32)
    return (gate_rows.astype(jnp.float32)[:, None] * result).astype(jnp.bfloat16)


def run_expert(slot_rows, slot_gates, wg_single, wu_single, wd_single):
    width = slot_rows.shape[-1]
    rows = slot_rows.reshape(-1, width)
    gate_rows = slot_gates.reshape(-1)
    result = expert_rows(rows, gate_rows, wg_single, wu_single, wd_single)
    return result.reshape(slot_rows.shape)


def slot_shards(tokens, routes, gates, w_gate, w_up, w_down, score_head, doc_ids):
    tok_dev, width = tokens.shape
    experts = lax.axis_size("ep")
    capacity = min(tok_dev, 3 * tok_dev * TOP // (2 * experts))
    flat_routes = routes.reshape(-1)
    onehot = (flat_routes[:, None] == jnp.arange(experts, dtype=jnp.int32)[None, :]).astype(
        jnp.int32
    )
    ranked = jnp.cumsum(onehot, axis=0)
    slot = jnp.sum(ranked * onehot, axis=1) - 1
    destination = flat_routes * capacity + slot
    repeated = jnp.repeat(tokens, TOP, axis=0)
    send_rows = jnp.zeros((experts * capacity, width), jnp.bfloat16).at[destination].set(repeated)
    send_gates = (
        jnp.zeros((experts * capacity,), jnp.bfloat16).at[destination].set(gates.reshape(-1))
    )
    recv_rows, recv_gates = (
        lax.all_to_all(
            send_rows.reshape(experts, capacity, width),
            "ep",
            split_axis=0,
            concat_axis=0,
            tiled=True,
        ),
        lax.all_to_all(
            send_gates.reshape(experts, capacity), "ep", split_axis=0, concat_axis=0, tiled=True
        ),
    )
    wg_single = w_gate[0]
    wu_single = w_up[0]
    wd_single = w_down[0]
    results = run_expert(recv_rows, recv_gates, wg_single, wu_single, wd_single)
    returned = lax.all_to_all(results, "ep", split_axis=0, concat_axis=0, tiled=True)
    returned_flat = returned.reshape(experts * capacity, width)
    gathered = returned_flat[destination].astype(jnp.float32).reshape(tok_dev, TOP, width)
    mixed = jnp.sum(gathered, axis=1).astype(jnp.bfloat16)
    token_score = jnp.dot(mixed.astype(jnp.float32), score_head, precision=lax.Precision.HIGHEST)
    passage_score = token_score.reshape(-1, PASSAGE).sum(axis=1) / math.sqrt(PASSAGE)
    doc_count = lax.axis_size("ep") * lax.axis_size("dp") * tok_dev // PASSAGE // 4
    doc_range = jnp.arange(doc_count, dtype=jnp.int32)[None, :]
    all_scores, all_docs = (
        lax.all_gather(passage_score, ("ep", "dp"), axis=0, tiled=True),
        lax.all_gather(doc_ids.astype(jnp.float32), ("ep", "dp"), axis=0, tiled=True),
    )
    member = all_docs[:, None] == doc_range.astype(jnp.float32)
    column = all_scores[:, None]
    passage_index = jnp.arange(all_scores.shape[0], dtype=jnp.int32)[:, None]
    max_score = jnp.where(member, column, -1e30).max(axis=0)
    sum_score = jnp.where(member, column, 0.0).sum(axis=0)
    first_index = jnp.where(member, passage_index, all_scores.shape[0]).min(axis=0)
    first_score = jnp.where(member & (passage_index == first_index[None, :]), column, 0.0).sum(
        axis=0
    )
    return (mixed, jnp.stack([max_score, first_score, sum_score]))


def pool(all_scores, all_docs, doc_count):
    doc_range = jnp.arange(doc_count, dtype=jnp.int32)[None, :]
    member = all_docs[:, None] == doc_range.astype(jnp.float32)
    column = all_scores[:, None]
    passage_index = jnp.arange(all_scores.shape[0], dtype=jnp.int32)[:, None]
    max_score = jnp.where(member, column, -1e30).max(axis=0)
    sum_score = jnp.where(member, column, 0.0).sum(axis=0)
    first_index = jnp.where(member, passage_index, all_scores.shape[0]).min(axis=0)
    first_score = jnp.where(member & (passage_index == first_index[None, :]), column, 0.0).sum(
        axis=0
    )
    return jnp.stack([max_score, first_score, sum_score])


LANES = 128


def tile_of(extent, most):
    return most if extent % most == 0 else extent


def expert_kernel(
    slot, xa, xb, wg0, wu0, wd0, wg1, wu1, wd1, gate, head, after, held,
    outa, outb, score, passed,
    rows, hidden, scale, x_sem,
):
    tok, width = xa.shape
    local = tok // PASSAGE
    out_tile = tile_of(width, 1024)
    blocks = [pl.ds(n * tok, tok) for n in range(2)]
    x_copies = [
        pltpu.make_async_copy(ref, rows.at[blocks[n], :], x_sem.at[n])
        for n, ref in enumerate((xa, xb))
    ]
    for copy in x_copies:
        copy.start()

    diagonal = lax.broadcasted_iota(jnp.int32, (tok, tok), 0) == lax.broadcasted_iota(
        jnp.int32, (tok, tok), 1
    )
    for n in range(2):
        for e in range(2):
            row = gate[2 * slot + n, pl.ds(e, 1), :]
            scale[e, blocks[n], :] = jnp.sum(
                jnp.where(diagonal, row, 0.0), axis=1, keepdims=True
            )

    for copy in x_copies:
        copy.wait()
    for e, (wg, wu) in enumerate(((wg0, wu0), (wg1, wu1))):
        gate_part = jnp.dot(rows[...], wg[...], preferred_element_type=jnp.float32)
        up_part = jnp.dot(rows[...], wu[...], preferred_element_type=jnp.float32)
        value = gate_part / (1.0 + jnp.exp(-gate_part)) * up_part
        hidden[e] = value.astype(jnp.bfloat16)

    totals = [jnp.zeros((1, LANES), jnp.float32) for _ in range(2 * local)]
    for j in range(width // out_tile):
        columns = pl.ds(j * out_tile, out_tile)
        weighted = sum(
            scale[e] * jnp.dot(hidden[e], wd[:, columns], preferred_element_type=jnp.float32)
            for e, wd in enumerate((wd0, wd1))
        )
        rounded = weighted.astype(jnp.bfloat16)
        outa[:, columns] = rounded[:tok]
        outb[:, columns] = rounded[tok:]
        scored = weighted * head[:, columns]
        lanes = sum(
            scored[:, k * LANES : (k + 1) * LANES] for k in range(out_tile // LANES)
        )
        for p in range(2 * local):
            totals[p] += jnp.sum(lanes[p * PASSAGE : (p + 1) * PASSAGE], axis=0, keepdims=True)
    for p in range(2 * local):
        score[pl.ds(p, 1), :] = totals[p]


def load_kernel(count, *refs):
    refs = refs[-2 * count - 1 :]
    copies = [
        pltpu.make_async_copy(src, dst, refs[-1].at[n])
        for n, (src, dst) in enumerate(zip(refs[:count], refs[count:-1]))
    ]
    for copy in copies:
        copy.start()
    for copy in copies:
        copy.wait()


def load(arrays, *firsts):
    arrays = [pltpu.with_memory_space_constraint(a, pltpu.HBM) for a in arrays]
    return pl.pallas_call(
        functools.partial(load_kernel, len(arrays)),
        in_specs=[pl.BlockSpec(memory_space=pl.ANY)] * (len(firsts) + len(arrays)),
        out_specs=[pl.BlockSpec(memory_space=pltpu.VMEM)] * len(arrays),
        out_shape=[pltpu.VMEM(a.shape, a.dtype) for a in arrays],
        scratch_shapes=[pltpu.SemaphoreType.DMA((len(arrays),))],
        compiler_params=pltpu.CompilerParams(vmem_limit_bytes=2**20),
        name="load",
    )(*firsts, *arrays)


def tie_kernel(*refs):
    pass


def tie(value, *firsts):
    anywhere = pl.BlockSpec(memory_space=pl.ANY)
    return pl.pallas_call(
        tie_kernel,
        in_specs=[anywhere] * (1 + len(firsts)),
        out_specs=anywhere,
        out_shape=jax.ShapeDtypeStruct(value.shape, value.dtype),
        input_output_aliases={0: 0},
        compiler_params=pltpu.CompilerParams(vmem_limit_bytes=2**20),
        name="tie",
    )(value, *firsts)


def expert_call(slot, blocks, weights, gate, head, after, held):
    tok, width = blocks[0].shape
    ff = weights[0].shape[1]
    local = tok // PASSAGE
    anywhere = pl.BlockSpec(memory_space=pl.ANY)
    vmem = pl.BlockSpec(memory_space=pltpu.VMEM)
    bf16 = jnp.bfloat16
    return pl.pallas_call(
        functools.partial(expert_kernel, slot),
        in_specs=[anywhere] * 2 + [vmem] * 8 + [anywhere, anywhere],
        out_specs=[vmem, vmem, vmem, anywhere],
        out_shape=[
            pltpu.VMEM((tok, width), bf16),
            pltpu.VMEM((tok, width), bf16),
            jax.ShapeDtypeStruct((2 * local, LANES), jnp.float32),
            jax.ShapeDtypeStruct(held.shape, held.dtype),
        ],
        input_output_aliases={11: 3},
        scratch_shapes=[
            pltpu.VMEM((2 * tok, width), bf16),
            pltpu.VMEM((2, 2 * tok, ff), bf16),
            pltpu.VMEM((2, 2 * tok, 1), jnp.float32),
            pltpu.SemaphoreType.DMA((2,)),
        ],
        compiler_params=pltpu.CompilerParams(vmem_limit_bytes=16 * 2**20),
        cost_estimate=pl.CostEstimate(flops=1, bytes_accessed=1, transcendentals=0),
        name="expert",
    )(*blocks, *weights, gate, head, after, held)


def dense_shards(tokens, routes, gates, w_gate, w_up, w_down, score_head, doc_ids):
    tok_dev, width = tokens.shape
    experts = lax.axis_size("ep")
    groups = lax.axis_size("dp")
    local = tok_dev // PASSAGE
    ring = experts // 4
    me = lax.axis_index("ep")
    places = [*range(0, ring, 2), *reversed(range(1, ring, 2))]
    onward = lambda v: lax.ppermute(
        v,
        "ep",
        [
            (4 * places[n] + i, 4 * places[(n + 1) % ring] + i)
            for n in range(ring)
            for i in range(4)
        ],
    )
    across = lambda v: lax.ppermute(v, "ep", [(i, i ^ 2) for i in range(experts)])
    sibling = lambda v: lax.ppermute(v, "ep", [(i, i ^ 1) for i in range(experts)])

    own = (w_gate[0], w_up[0], w_down[0])

    target = jnp.arange(experts, dtype=jnp.int32)
    wanted = target[:, None] ^ jnp.arange(2, dtype=jnp.int32)[None, :]
    sent_gates = jnp.zeros((experts, 2, tok_dev), jnp.bfloat16)
    for k in range(TOP):
        chosen = wanted[:, :, None] == routes[:, k][None, None, :]
        sent_gates = jnp.where(chosen, gates[:, k][None, None, :], sent_gates)
    gate_rows = lax.all_to_all(sent_gates, "ep", split_axis=0, concat_axis=0, tiled=True)
    row = jnp.arange(2 * ring, dtype=jnp.int32)
    z = me // 4
    at = jnp.where(z % 2 == 0, z // 2, ring - (z + 1) // 2)
    back = lax.rem(at - row // 2 + ring, ring)
    back = jnp.where(back < (ring + 1) // 2, 2 * back, 2 * (ring - back) - 1)
    order = back * 4 + (me % 4 ^ row % 2 * 2)
    position = order[:, None] == jnp.arange(experts, dtype=jnp.int32)[None, :]
    slot_gates = gate_rows.astype(jnp.float32)[order]

    near = [tokens]
    far = [across(tokens)]

    def step(*meanwhile):
        near.append(tie(onward(near[-1]), far[-1], *meanwhile))
        far.append(across(near[-1]) if len(near) < ring else onward(far[-1]))

    head = score_head[None, :]
    scores = [None] * ring
    mine = [None] * ring
    other = [None] * ring

    def work(s, after, held):
        mine[s], other[s], scores[s], passed = expert_call(
            s, (near[s], far[s]), weights, slot_gates, head, after, held
        )
        return passed

    step(slot_gates)
    weights = load(own, slot_gates)
    step(weights[0])
    weights = weights + load([sibling(w) for w in own], slot_gates)
    weights = [pltpu.with_memory_space_constraint(w, pltpu.VMEM) for w in weights]
    held = jnp.zeros((8, LANES), jnp.float32)
    turns = [1, 0, *range(2, ring)]
    for n, s in enumerate(turns):
        if n == ring - 1:
            other[0] = work(s, held, other[0])
        else:
            held = work(s, near[-1], held)
        if len(near) < ring:
            step(scores[s])
    carried = None
    sent = []
    for s in [*range(1, ring), 0]:
        crossed = across(tie(other[0], crossed) if s == 0 else other[s])
        total = mine[s].astype(jnp.float32) + crossed.astype(jnp.float32)
        if carried is not None:
            total = total + carried.astype(jnp.float32)
        total = total.astype(jnp.bfloat16)
        if s > 0:
            carried = onward(total)
            sent.append(total)
    mixed = total

    slot_scores = jnp.stack(scores).sum(axis=2).reshape(2 * ring, local) / math.sqrt(PASSAGE)
    part_score = jnp.where(position[:, :, None], slot_scores[:, None, :], 0.0).sum(axis=0)
    told = jnp.concatenate([part_score.reshape(-1), doc_ids.astype(jnp.float32)])
    told = jnp.pad(told, (0, -told.shape[0] % LANES))[None, :]
    told = tie(told, sent[-2])
    heard = lax.all_to_all(
        jnp.broadcast_to(told, (experts * groups, told.shape[1])),
        ("ep", "dp"),
        split_axis=0,
        concat_axis=0,
        tiled=True,
    )
    count = experts * local
    all_scores = heard[:, :count].reshape(experts, groups, experts, local).sum(axis=0)
    all_scores = all_scores.transpose(1, 0, 2).reshape(-1)
    all_docs = heard[:, count : count + local].reshape(-1)
    return (mixed, pool(all_scores, all_docs, count * groups // 4))


def shards(tokens, *rest):
    tok_dev = tokens.shape[0]
    experts = lax.axis_size("ep")
    capacity = min(tok_dev, 3 * tok_dev * TOP // (2 * experts))
    dense = 2 * capacity >= tok_dev and experts % 4 == 0 and tok_dev % PASSAGE == 0
    return (dense_shards if dense else slot_shards)(tokens, *rest)


def solution(mesh):
    return jax.shard_map(
        shards,
        mesh=mesh,
        in_specs=(
            P(("ep", "dp"), None),
            P(("ep", "dp"), None),
            P(("ep", "dp"), None),
            P("ep", None, None),
            P("ep", None, None),
            P("ep", None, None),
            P(),
            P(("ep", "dp")),
        ),
        out_specs=(P(("ep", "dp"), None), P()),
        check_vma=False,
    )
```

```python
import functools
import math

import jax
import jax.numpy as jnp
from jax import lax
from jax.experimental import pallas as pl
from jax.experimental.pallas import tpu as pltpu
from jax.sharding import PartitionSpec as P

TOP = 8
PASSAGE = 128


def expert_rows(rows, gate_rows, wg_single, wu_single, wd_single):
    gate_part = jnp.dot(rows, wg_single, preferred_element_type=jnp.float32)
    up_part = jnp.dot(rows, wu_single, preferred_element_type=jnp.float32)
    hidden = (jax.nn.silu(gate_part) * up_part).astype(jnp.bfloat16)
    result = jnp.dot(hidden, wd_single, preferred_element_type=jnp.float32)
    return (gate_rows.astype(jnp.float32)[:, None] * result).astype(jnp.bfloat16)


def run_expert(slot_rows, slot_gates, wg_single, wu_single, wd_single):
    width = slot_rows.shape[-1]
    rows = slot_rows.reshape(-1, width)
    gate_rows = slot_gates.reshape(-1)
    result = expert_rows(rows, gate_rows, wg_single, wu_single, wd_single)
    return result.reshape(slot_rows.shape)


def slot_shards(tokens, routes, gates, w_gate, w_up, w_down, score_head, doc_ids):
    tok_dev, width = tokens.shape
    experts = lax.axis_size("ep")
    capacity = min(tok_dev, 3 * tok_dev * TOP // (2 * experts))
    flat_routes = routes.reshape(-1)
    onehot = (flat_routes[:, None] == jnp.arange(experts, dtype=jnp.int32)[None, :]).astype(
        jnp.int32
    )
    ranked = jnp.cumsum(onehot, axis=0)
    slot = jnp.sum(ranked * onehot, axis=1) - 1
    destination = flat_routes * capacity + slot
    repeated = jnp.repeat(tokens, TOP, axis=0)
    send_rows = jnp.zeros((experts * capacity, width), jnp.bfloat16).at[destination].set(repeated)
    send_gates = (
        jnp.zeros((experts * capacity,), jnp.bfloat16).at[destination].set(gates.reshape(-1))
    )
    recv_rows, recv_gates = (
        lax.all_to_all(
            send_rows.reshape(experts, capacity, width),
            "ep",
            split_axis=0,
            concat_axis=0,
            tiled=True,
        ),
        lax.all_to_all(
            send_gates.reshape(experts, capacity), "ep", split_axis=0, concat_axis=0, tiled=True
        ),
    )
    wg_single = w_gate[0]
    wu_single = w_up[0]
    wd_single = w_down[0]
    results = run_expert(recv_rows, recv_gates, wg_single, wu_single, wd_single)
    returned = lax.all_to_all(results, "ep", split_axis=0, concat_axis=0, tiled=True)
    returned_flat = returned.reshape(experts * capacity, width)
    gathered = returned_flat[destination].astype(jnp.float32).reshape(tok_dev, TOP, width)
    mixed = jnp.sum(gathered, axis=1).astype(jnp.bfloat16)
    token_score = jnp.dot(mixed.astype(jnp.float32), score_head, precision=lax.Precision.HIGHEST)
    passage_score = token_score.reshape(-1, PASSAGE).sum(axis=1) / math.sqrt(PASSAGE)
    doc_count = lax.axis_size("ep") * lax.axis_size("dp") * tok_dev // PASSAGE // 4
    doc_range = jnp.arange(doc_count, dtype=jnp.int32)[None, :]
    all_scores, all_docs = (
        lax.all_gather(passage_score, ("ep", "dp"), axis=0, tiled=True),
        lax.all_gather(doc_ids.astype(jnp.float32), ("ep", "dp"), axis=0, tiled=True),
    )
    member = all_docs[:, None] == doc_range.astype(jnp.float32)
    column = all_scores[:, None]
    passage_index = jnp.arange(all_scores.shape[0], dtype=jnp.int32)[:, None]
    max_score = jnp.where(member, column, -1e30).max(axis=0)
    sum_score = jnp.where(member, column, 0.0).sum(axis=0)
    first_index = jnp.where(member, passage_index, all_scores.shape[0]).min(axis=0)
    first_score = jnp.where(member & (passage_index == first_index[None, :]), column, 0.0).sum(
        axis=0
    )
    return (mixed, jnp.stack([max_score, first_score, sum_score]))


def pool(all_scores, all_docs, doc_count):
    doc_range = jnp.arange(doc_count, dtype=jnp.int32)[None, :]
    member = all_docs[:, None] == doc_range.astype(jnp.float32)
    column = all_scores[:, None]
    passage_index = jnp.arange(all_scores.shape[0], dtype=jnp.int32)[:, None]
    max_score = jnp.where(member, column, -1e30).max(axis=0)
    sum_score = jnp.where(member, column, 0.0).sum(axis=0)
    first_index = jnp.where(member, passage_index, all_scores.shape[0]).min(axis=0)
    first_score = jnp.where(member & (passage_index == first_index[None, :]), column, 0.0).sum(
        axis=0
    )
    return jnp.stack([max_score, first_score, sum_score])


LANES = 128


def tile_of(extent, most):
    return most if extent % most == 0 else extent


def expert_kernel(
    slot, xa, xb, wg0, wu0, wd0, wg1, wu1, wd1, gate, head, after, held,
    outa, outb, score, passed,
    rows, hidden, scale, x_sem,
):
    tok, width = xa.shape
    local = tok // PASSAGE
    out_tile = tile_of(width, 1024)
    blocks = [pl.ds(n * tok, tok) for n in range(2)]
    x_copies = [
        pltpu.make_async_copy(ref, rows.at[blocks[n], :], x_sem.at[n])
        for n, ref in enumerate((xa, xb))
    ]
    for copy in x_copies:
        copy.start()

    diagonal = lax.broadcasted_iota(jnp.int32, (tok, tok), 0) == lax.broadcasted_iota(
        jnp.int32, (tok, tok), 1
    )
    for n in range(2):
        for e in range(2):
            row = gate[pl.ds(2 * slot + n, 1), pl.ds(e * tok, tok)]
            scale[e, blocks[n], :] = jnp.sum(
                jnp.where(diagonal, row, 0.0), axis=1, keepdims=True
            )

    for copy in x_copies:
        copy.wait()
    for e, (wg, wu) in enumerate(((wg0, wu0), (wg1, wu1))):
        gate_part = jnp.dot(rows[...], wg[...], preferred_element_type=jnp.float32)
        up_part = jnp.dot(rows[...], wu[...], preferred_element_type=jnp.float32)
        value = gate_part / (1.0 + jnp.exp(-gate_part)) * up_part
        hidden[e] = value.astype(jnp.bfloat16)

    totals = [jnp.zeros((1, LANES), jnp.float32) for _ in range(2 * local)]
    for j in range(width // out_tile):
        columns = pl.ds(j * out_tile, out_tile)
        weighted = sum(
            scale[e] * jnp.dot(hidden[e], wd[:, columns], preferred_element_type=jnp.float32)
            for e, wd in enumerate((wd0, wd1))
        )
        rounded = weighted.astype(jnp.bfloat16)
        outa[:, columns] = rounded[:tok]
        outb[:, columns] = rounded[tok:]
        scored = weighted * head[:, columns]
        lanes = sum(
            scored[:, k * LANES : (k + 1) * LANES] for k in range(out_tile // LANES)
        )
        for p in range(2 * local):
            totals[p] += jnp.sum(lanes[p * PASSAGE : (p + 1) * PASSAGE], axis=0, keepdims=True)
    for p in range(2 * local):
        score[pl.ds(p, 1), :] = totals[p]


def load_kernel(count, *refs):
    refs = refs[-2 * count - 1 :]
    copies = [
        pltpu.make_async_copy(src, dst, refs[-1].at[n])
        for n, (src, dst) in enumerate(zip(refs[:count], refs[count:-1]))
    ]
    for copy in copies:
        copy.start()
    for copy in copies:
        copy.wait()


def load(arrays, *firsts):
    arrays = [pltpu.with_memory_space_constraint(a, pltpu.HBM) for a in arrays]
    return pl.pallas_call(
        functools.partial(load_kernel, len(arrays)),
        in_specs=[pl.BlockSpec(memory_space=pl.ANY)] * (len(firsts) + len(arrays)),
        out_specs=[pl.BlockSpec(memory_space=pltpu.VMEM)] * len(arrays),
        out_shape=[pltpu.VMEM(a.shape, a.dtype) for a in arrays],
        scratch_shapes=[pltpu.SemaphoreType.DMA((len(arrays),))],
        compiler_params=pltpu.CompilerParams(vmem_limit_bytes=2**20),
        name="load",
    )(*firsts, *arrays)


def tie_kernel(*refs):
    pass


def tie(value, *firsts):
    anywhere = pl.BlockSpec(memory_space=pl.ANY)
    return pl.pallas_call(
        tie_kernel,
        in_specs=[anywhere] * (1 + len(firsts)),
        out_specs=anywhere,
        out_shape=jax.ShapeDtypeStruct(value.shape, value.dtype),
        input_output_aliases={len(firsts): 0},
        compiler_params=pltpu.CompilerParams(vmem_limit_bytes=2**20),
        name="tie",
    )(*firsts, value)


def expert_call(slot, blocks, weights, gate, head, after, held):
    tok, width = blocks[0].shape
    ff = weights[0].shape[1]
    local = tok // PASSAGE
    anywhere = pl.BlockSpec(memory_space=pl.ANY)
    vmem = pl.BlockSpec(memory_space=pltpu.VMEM)
    bf16 = jnp.bfloat16
    return pl.pallas_call(
        functools.partial(expert_kernel, slot),
        in_specs=[anywhere] * 2 + [vmem] * 8 + [anywhere, anywhere],
        out_specs=[vmem, vmem, vmem, anywhere],
        out_shape=[
            pltpu.VMEM((tok, width), bf16),
            pltpu.VMEM((tok, width), bf16),
            jax.ShapeDtypeStruct((2 * local, LANES), jnp.float32),
            jax.ShapeDtypeStruct(held.shape, held.dtype),
        ],
        input_output_aliases={11: 3},
        scratch_shapes=[
            pltpu.VMEM((2 * tok, width), bf16),
            pltpu.VMEM((2, 2 * tok, ff), bf16),
            pltpu.VMEM((2, 2 * tok, 1), jnp.float32),
            pltpu.SemaphoreType.DMA((2,)),
        ],
        compiler_params=pltpu.CompilerParams(vmem_limit_bytes=16 * 2**20),
        cost_estimate=pl.CostEstimate(flops=1, bytes_accessed=1, transcendentals=0),
        name="expert",
    )(*blocks, *weights, gate, head, after, held)


def dense_shards(tokens, routes, gates, w_gate, w_up, w_down, score_head, doc_ids):
    tok_dev, width = tokens.shape
    experts = lax.axis_size("ep")
    groups = lax.axis_size("dp")
    local = tok_dev // PASSAGE
    ring = experts // 4
    me = lax.axis_index("ep")
    places = [*range(0, ring, 2), *reversed(range(1, ring, 2))]
    onward = lambda v: lax.ppermute(
        v,
        "ep",
        [
            (4 * places[n] + i, 4 * places[(n + 1) % ring] + i)
            for n in range(ring)
            for i in range(4)
        ],
    )
    across = lambda v: lax.ppermute(v, "ep", [(i, i ^ 2) for i in range(experts)])
    sibling = lambda v: lax.ppermute(v, "ep", [(i, i ^ 1) for i in range(experts)])

    own = (w_gate[0], w_up[0], w_down[0])

    cores = [[2 * n + core for n in range(experts // 2)] for core in range(2)]
    target = jnp.arange(experts, dtype=jnp.int32)
    wanted = (target // 2 * 2 + me % 2) ^ target % 2
    chosen = routes.T[:, None, :] == wanted[None, :, None]
    sent_gates = jnp.where(chosen, gates.T[:, None, :], jnp.bfloat16(0)).sum(axis=0)
    sent_gates = sent_gates.reshape(experts // 2, 2 * tok_dev)
    gate_rows = lax.all_to_all(
        sent_gates, "ep", split_axis=0, concat_axis=0, tiled=True, axis_index_groups=cores
    )
    row = jnp.arange(2 * ring, dtype=jnp.int32)
    z = me // 4
    at = jnp.where(z % 2 == 0, z // 2, ring - (z + 1) // 2)
    back = lax.rem(at - row // 2 + ring, ring)
    back = jnp.where(back < (ring + 1) // 2, 2 * back, 2 * (ring - back) - 1)
    order = back * 4 + (me % 4 ^ row % 2 * 2)
    position = order[:, None] == jnp.arange(experts, dtype=jnp.int32)[None, :]
    slot_gates = gate_rows.astype(jnp.float32)[order // 2]

    near = [tokens]
    coming = [onward(tokens)]
    far = [across(tokens)]

    def step(*meanwhile):
        near.append(tie(coming[-1], far[-1], *meanwhile))
        if len(near) < ring:
            coming.append(onward(near[-1]))
            far.append(across(near[-1]))
        else:
            far.append(onward(far[-1]))

    head = score_head[None, :]
    scores = [None] * ring
    mine = [None] * ring
    other = [None] * ring

    def work(s, after, held):
        mine[s], other[s], scores[s], passed = expert_call(
            s, (near[s], far[s]), weights, slot_gates, head, after, held
        )
        return passed

    step(slot_gates)
    weights = load(own, slot_gates)
    step(weights[0])
    weights = weights + load([sibling(w) for w in own], slot_gates)
    weights = [pltpu.with_memory_space_constraint(w, pltpu.VMEM) for w in weights]
    held = jnp.zeros((8, LANES), jnp.float32)
    turns = [1, 0, *range(2, ring)]
    for n, s in enumerate(turns):
        if n == ring - 1:
            other[0] = work(s, held, other[0])
        else:
            held = work(s, near[-1], held)
        if len(near) < ring:
            step(scores[s])
    carried = None
    sent = []
    for s in [*range(1, ring), 0]:
        crossing = tie(other[0], sent[-1]) if s == 0 else other[s]
        total = mine[s].astype(jnp.float32) + across(crossing).astype(jnp.float32)
        if carried is not None:
            total = total + carried.astype(jnp.float32)
        total = total.astype(jnp.bfloat16)
        if s > 0:
            carried = onward(total)
            sent.append(total)
    mixed = total

    slot_scores = jnp.stack(scores).sum(axis=2).reshape(2 * ring, local) / math.sqrt(PASSAGE)
    part_score = jnp.where(position[:, :, None], slot_scores[:, None, :], 0.0).sum(axis=0)
    told = jnp.concatenate([part_score.reshape(-1), doc_ids.astype(jnp.float32)])
    told = jnp.pad(told, (0, -told.shape[0] % LANES))[None, :]
    told = tie(told, sent[-2])
    heard = lax.all_to_all(
        jnp.broadcast_to(told, (experts * groups, told.shape[1])),
        ("ep", "dp"),
        split_axis=0,
        concat_axis=0,
        tiled=True,
    )
    count = experts * local
    all_scores = heard[:, :count].reshape(experts, groups, experts, local).sum(axis=0)
    all_scores = all_scores.transpose(1, 0, 2).reshape(-1)
    all_docs = heard[:, count : count + local].reshape(-1)
    return (mixed, pool(all_scores, all_docs, count * groups // 4))


def shards(tokens, *rest):
    tok_dev = tokens.shape[0]
    experts = lax.axis_size("ep")
    capacity = min(tok_dev, 3 * tok_dev * TOP // (2 * experts))
    dense = 2 * capacity >= tok_dev and experts % 4 == 0 and tok_dev % PASSAGE == 0
    return (dense_shards if dense else slot_shards)(tokens, *rest)


def solution(mesh):
    return jax.shard_map(
        shards,
        mesh=mesh,
        in_specs=(
            P(("ep", "dp"), None),
            P(("ep", "dp"), None),
            P(("ep", "dp"), None),
            P("ep", None, None),
            P("ep", None, None),
            P("ep", None, None),
            P(),
            P(("ep", "dp")),
        ),
        out_specs=(P(("ep", "dp"), None), P()),
        check_vma=False,
    )
```

```python
import functools
import math

import jax
import jax.numpy as jnp
from jax import lax
from jax.experimental import pallas as pl
from jax.experimental.pallas import tpu as pltpu
from jax.sharding import PartitionSpec as P

TOP = 8
PASSAGE = 128


def expert_rows(rows, gate_rows, wg_single, wu_single, wd_single):
    gate_part = jnp.dot(rows, wg_single, preferred_element_type=jnp.float32)
    up_part = jnp.dot(rows, wu_single, preferred_element_type=jnp.float32)
    hidden = (jax.nn.silu(gate_part) * up_part).astype(jnp.bfloat16)
    result = jnp.dot(hidden, wd_single, preferred_element_type=jnp.float32)
    return (gate_rows.astype(jnp.float32)[:, None] * result).astype(jnp.bfloat16)


def run_expert(slot_rows, slot_gates, wg_single, wu_single, wd_single):
    width = slot_rows.shape[-1]
    rows = slot_rows.reshape(-1, width)
    gate_rows = slot_gates.reshape(-1)
    result = expert_rows(rows, gate_rows, wg_single, wu_single, wd_single)
    return result.reshape(slot_rows.shape)


def slot_shards(tokens, routes, gates, w_gate, w_up, w_down, score_head, doc_ids):
    tok_dev, width = tokens.shape
    experts = lax.axis_size("ep")
    capacity = min(tok_dev, 3 * tok_dev * TOP // (2 * experts))
    flat_routes = routes.reshape(-1)
    onehot = (flat_routes[:, None] == jnp.arange(experts, dtype=jnp.int32)[None, :]).astype(
        jnp.int32
    )
    ranked = jnp.cumsum(onehot, axis=0)
    slot = jnp.sum(ranked * onehot, axis=1) - 1
    destination = flat_routes * capacity + slot
    repeated = jnp.repeat(tokens, TOP, axis=0)
    send_rows = jnp.zeros((experts * capacity, width), jnp.bfloat16).at[destination].set(repeated)
    send_gates = (
        jnp.zeros((experts * capacity,), jnp.bfloat16).at[destination].set(gates.reshape(-1))
    )
    recv_rows, recv_gates = (
        lax.all_to_all(
            send_rows.reshape(experts, capacity, width),
            "ep",
            split_axis=0,
            concat_axis=0,
            tiled=True,
        ),
        lax.all_to_all(
            send_gates.reshape(experts, capacity), "ep", split_axis=0, concat_axis=0, tiled=True
        ),
    )
    wg_single = w_gate[0]
    wu_single = w_up[0]
    wd_single = w_down[0]
    results = run_expert(recv_rows, recv_gates, wg_single, wu_single, wd_single)
    returned = lax.all_to_all(results, "ep", split_axis=0, concat_axis=0, tiled=True)
    returned_flat = returned.reshape(experts * capacity, width)
    gathered = returned_flat[destination].astype(jnp.float32).reshape(tok_dev, TOP, width)
    mixed = jnp.sum(gathered, axis=1).astype(jnp.bfloat16)
    token_score = jnp.dot(mixed.astype(jnp.float32), score_head, precision=lax.Precision.HIGHEST)
    passage_score = token_score.reshape(-1, PASSAGE).sum(axis=1) / math.sqrt(PASSAGE)
    doc_count = lax.axis_size("ep") * lax.axis_size("dp") * tok_dev // PASSAGE // 4
    doc_range = jnp.arange(doc_count, dtype=jnp.int32)[None, :]
    all_scores, all_docs = (
        lax.all_gather(passage_score, ("ep", "dp"), axis=0, tiled=True),
        lax.all_gather(doc_ids.astype(jnp.float32), ("ep", "dp"), axis=0, tiled=True),
    )
    member = all_docs[:, None] == doc_range.astype(jnp.float32)
    column = all_scores[:, None]
    passage_index = jnp.arange(all_scores.shape[0], dtype=jnp.int32)[:, None]
    max_score = jnp.where(member, column, -1e30).max(axis=0)
    sum_score = jnp.where(member, column, 0.0).sum(axis=0)
    first_index = jnp.where(member, passage_index, all_scores.shape[0]).min(axis=0)
    first_score = jnp.where(member & (passage_index == first_index[None, :]), column, 0.0).sum(
        axis=0
    )
    return (mixed, jnp.stack([max_score, first_score, sum_score]))


def pool(all_scores, all_docs, doc_count):
    doc_range = jnp.arange(doc_count, dtype=jnp.int32)[None, :]
    member = all_docs[:, None] == doc_range.astype(jnp.float32)
    column = all_scores[:, None]
    passage_index = jnp.arange(all_scores.shape[0], dtype=jnp.int32)[:, None]
    max_score = jnp.where(member, column, -1e30).max(axis=0)
    sum_score = jnp.where(member, column, 0.0).sum(axis=0)
    first_index = jnp.where(member, passage_index, all_scores.shape[0]).min(axis=0)
    first_score = jnp.where(member & (passage_index == first_index[None, :]), column, 0.0).sum(
        axis=0
    )
    return jnp.stack([max_score, first_score, sum_score])


LANES = 128


def tile_of(extent, most):
    return most if extent % most == 0 else extent


def expert_kernel(
    slot, xa, xb, wg0, wu0, wd0, wg1, wu1, wd1, gate, head, after, held,
    outa, outb, score, passed,
    rows, hidden, scale, x_sem,
):
    tok, width = xa.shape
    local = tok // PASSAGE
    out_tile = tile_of(width, 1024)
    blocks = [pl.ds(n * tok, tok) for n in range(2)]
    x_copies = [
        pltpu.make_async_copy(ref, rows.at[blocks[n], :], x_sem.at[n])
        for n, ref in enumerate((xa, xb))
    ]
    for copy in x_copies:
        copy.start()

    diagonal = lax.broadcasted_iota(jnp.int32, (tok, tok), 0) == lax.broadcasted_iota(
        jnp.int32, (tok, tok), 1
    )
    for n in range(2):
        for e in range(2):
            row = gate[2 * slot + n, pl.ds(e, 1), :]
            scale[e, blocks[n], :] = jnp.sum(
                jnp.where(diagonal, row, 0.0), axis=1, keepdims=True
            )

    for copy in x_copies:
        copy.wait()
    for e, (wg, wu) in enumerate(((wg0, wu0), (wg1, wu1))):
        gate_part = jnp.dot(rows[...], wg[...], preferred_element_type=jnp.float32)
        up_part = jnp.dot(rows[...], wu[...], preferred_element_type=jnp.float32)
        value = gate_part / (1.0 + jnp.exp(-gate_part)) * up_part
        hidden[e] = value.astype(jnp.bfloat16)

    totals = [jnp.zeros((1, LANES), jnp.float32) for _ in range(2 * local)]
    for j in range(width // out_tile):
        columns = pl.ds(j * out_tile, out_tile)
        weighted = sum(
            scale[e] * jnp.dot(hidden[e], wd[:, columns], preferred_element_type=jnp.float32)
            for e, wd in enumerate((wd0, wd1))
        )
        rounded = weighted.astype(jnp.bfloat16)
        outa[:, columns] = rounded[:tok]
        outb[:, columns] = rounded[tok:]
        scored = weighted * head[:, columns]
        lanes = sum(
            scored[:, k * LANES : (k + 1) * LANES] for k in range(out_tile // LANES)
        )
        for p in range(2 * local):
            totals[p] += jnp.sum(lanes[p * PASSAGE : (p + 1) * PASSAGE], axis=0, keepdims=True)
    for p in range(2 * local):
        score[pl.ds(p, 1), :] = totals[p]


def gate_kernel(wanted, routes, gates, out):
    found = jnp.zeros((wanted.shape[0], routes.shape[1]), jnp.float32)
    values = gates[...].astype(jnp.float32)
    for k in range(routes.shape[0]):
        chosen = wanted[...] == routes[pl.ds(k, 1), :]
        found = jnp.where(chosen, values[k : k + 1], found)
    for n in range(out.shape[0]):
        out[n] = found[2 * n : 2 * n + 2].astype(jnp.bfloat16)


def load_kernel(count, *refs):
    refs = refs[-2 * count - 1 :]
    copies = [
        pltpu.make_async_copy(src, dst, refs[-1].at[n])
        for n, (src, dst) in enumerate(zip(refs[:count], refs[count:-1]))
    ]
    for copy in copies:
        copy.start()
    for copy in copies:
        copy.wait()


def load(arrays, *firsts):
    arrays = [pltpu.with_memory_space_constraint(a, pltpu.HBM) for a in arrays]
    return pl.pallas_call(
        functools.partial(load_kernel, len(arrays)),
        in_specs=[pl.BlockSpec(memory_space=pl.ANY)] * (len(firsts) + len(arrays)),
        out_specs=[pl.BlockSpec(memory_space=pltpu.VMEM)] * len(arrays),
        out_shape=[pltpu.VMEM(a.shape, a.dtype) for a in arrays],
        scratch_shapes=[pltpu.SemaphoreType.DMA((len(arrays),))],
        compiler_params=pltpu.CompilerParams(vmem_limit_bytes=2**20),
        name="load",
    )(*firsts, *arrays)


def tie_kernel(*refs):
    pass


def tie(value, *firsts):
    anywhere = pl.BlockSpec(memory_space=pl.ANY)
    return pl.pallas_call(
        tie_kernel,
        in_specs=[anywhere] * (1 + len(firsts)),
        out_specs=anywhere,
        out_shape=jax.ShapeDtypeStruct(value.shape, value.dtype),
        input_output_aliases={len(firsts): 0},
        compiler_params=pltpu.CompilerParams(vmem_limit_bytes=2**20),
        name="tie",
    )(*firsts, value)


def expert_call(slot, blocks, weights, gate, head, after, held):
    tok, width = blocks[0].shape
    ff = weights[0].shape[1]
    local = tok // PASSAGE
    anywhere = pl.BlockSpec(memory_space=pl.ANY)
    vmem = pl.BlockSpec(memory_space=pltpu.VMEM)
    bf16 = jnp.bfloat16
    return pl.pallas_call(
        functools.partial(expert_kernel, slot),
        in_specs=[anywhere] * 2 + [vmem] * 8 + [anywhere, anywhere],
        out_specs=[vmem, vmem, vmem, anywhere],
        out_shape=[
            pltpu.VMEM((tok, width), bf16),
            pltpu.VMEM((tok, width), bf16),
            jax.ShapeDtypeStruct((2 * local, LANES), jnp.float32),
            jax.ShapeDtypeStruct(held.shape, held.dtype),
        ],
        input_output_aliases={11: 3},
        scratch_shapes=[
            pltpu.VMEM((2 * tok, width), bf16),
            pltpu.VMEM((2, 2 * tok, ff), bf16),
            pltpu.VMEM((2, 2 * tok, 1), jnp.float32),
            pltpu.SemaphoreType.DMA((2,)),
        ],
        compiler_params=pltpu.CompilerParams(vmem_limit_bytes=16 * 2**20),
        cost_estimate=pl.CostEstimate(flops=1, bytes_accessed=1, transcendentals=0),
        name="expert",
    )(*blocks, *weights, gate, head, after, held)


def dense_shards(tokens, routes, gates, w_gate, w_up, w_down, score_head, doc_ids):
    tok_dev, width = tokens.shape
    experts = lax.axis_size("ep")
    groups = lax.axis_size("dp")
    local = tok_dev // PASSAGE
    ring = experts // 4
    me = lax.axis_index("ep")
    places = [*range(0, ring, 2), *reversed(range(1, ring, 2))]
    onward = lambda v: lax.ppermute(
        v,
        "ep",
        [
            (4 * places[n] + i, 4 * places[(n + 1) % ring] + i)
            for n in range(ring)
            for i in range(4)
        ],
    )
    across = lambda v: lax.ppermute(v, "ep", [(i, i ^ 2) for i in range(experts)])
    sibling = lambda v: lax.ppermute(v, "ep", [(i, i ^ 1) for i in range(experts)])

    own = (w_gate[0], w_up[0], w_down[0])

    cores = [[2 * n + core for n in range(experts // 2)] for core in range(2)]
    target = jnp.arange(experts, dtype=jnp.int32)
    wanted = (target // 2 * 2 + me % 2) ^ target % 2
    sent_gates = pl.pallas_call(
        gate_kernel,
        out_shape=jax.ShapeDtypeStruct((experts // 2, 2, tok_dev), jnp.bfloat16),
        compiler_params=pltpu.CompilerParams(vmem_limit_bytes=2**22),
        name="gates",
    )(wanted[:, None], routes.T, gates.T)
    gate_rows = lax.all_to_all(
        sent_gates, "ep", split_axis=0, concat_axis=0, tiled=True, axis_index_groups=cores
    )
    row = jnp.arange(2 * ring, dtype=jnp.int32)
    z = me // 4
    at = jnp.where(z % 2 == 0, z // 2, ring - (z + 1) // 2)
    back = lax.rem(at - row // 2 + ring, ring)
    back = jnp.where(back < (ring + 1) // 2, 2 * back, 2 * (ring - back) - 1)
    order = back * 4 + (me % 4 ^ row % 2 * 2)
    position = order[:, None] == jnp.arange(experts, dtype=jnp.int32)[None, :]
    slot_gates = gate_rows.astype(jnp.float32)[order // 2]

    near = [tokens]
    coming = [onward(tokens)]
    far = [across(tokens)]

    def step(*meanwhile):
        near.append(tie(coming[-1], far[-1], *meanwhile))
        if len(near) < ring:
            coming.append(onward(near[-1]))
            far.append(across(near[-1]))
        else:
            far.append(onward(far[-1]))

    head = score_head[None, :]
    scores = [None] * ring
    mine = [None] * ring
    other = [None] * ring

    def work(s, after, held):
        mine[s], other[s], scores[s], passed = expert_call(
            s, (near[s], far[s]), weights, slot_gates, head, after, held
        )
        return passed

    step(slot_gates)
    weights = load(own, slot_gates)
    step(weights[0])
    weights = weights + load([sibling(w) for w in own], slot_gates)
    weights = [pltpu.with_memory_space_constraint(w, pltpu.VMEM) for w in weights]
    held = jnp.zeros((8, LANES), jnp.float32)
    turns = [1, 0, *range(2, ring)]
    for n, s in enumerate(turns):
        if n == ring - 1:
            other[0] = work(s, held, other[0])
        else:
            held = work(s, near[-1], held)
        if len(near) < ring:
            step(scores[s])
    carried = None
    sent = []
    for s in [*range(1, ring), 0]:
        crossing = tie(other[0], sent[-1]) if s == 0 else other[s]
        total = mine[s].astype(jnp.float32) + across(crossing).astype(jnp.float32)
        if carried is not None:
            total = total + carried.astype(jnp.float32)
        total = total.astype(jnp.bfloat16)
        if s > 0:
            carried = onward(total)
            sent.append(total)
    mixed = total

    slot_scores = jnp.stack(scores).sum(axis=2).reshape(2 * ring, local) / math.sqrt(PASSAGE)
    part_score = jnp.where(position[:, :, None], slot_scores[:, None, :], 0.0).sum(axis=0)
    told = jnp.concatenate([part_score.reshape(-1), doc_ids.astype(jnp.float32)])
    told = jnp.pad(told, (0, -told.shape[0] % LANES))[None, :]
    told = tie(told, sent[-2])
    heard = lax.all_to_all(
        jnp.broadcast_to(told, (experts * groups, told.shape[1])),
        ("ep", "dp"),
        split_axis=0,
        concat_axis=0,
        tiled=True,
    )
    count = experts * local
    all_scores = heard[:, :count].reshape(experts, groups, experts, local).sum(axis=0)
    all_scores = all_scores.transpose(1, 0, 2).reshape(-1)
    all_docs = heard[:, count : count + local].reshape(-1)
    return (mixed, pool(all_scores, all_docs, count * groups // 4))


def shards(tokens, *rest):
    tok_dev = tokens.shape[0]
    experts = lax.axis_size("ep")
    capacity = min(tok_dev, 3 * tok_dev * TOP // (2 * experts))
    dense = 2 * capacity >= tok_dev and experts % 4 == 0 and tok_dev % PASSAGE == 0
    return (dense_shards if dense else slot_shards)(tokens, *rest)


def solution(mesh):
    return jax.shard_map(
        shards,
        mesh=mesh,
        in_specs=(
            P(("ep", "dp"), None),
            P(("ep", "dp"), None),
            P(("ep", "dp"), None),
            P("ep", None, None),
            P("ep", None, None),
            P("ep", None, None),
            P(),
            P(("ep", "dp")),
        ),
        out_specs=(P(("ep", "dp"), None), P()),
        check_vma=False,
    )
```

```python
import functools
import math

import jax
import jax.numpy as jnp
from jax import lax
from jax.experimental import pallas as pl
from jax.experimental.pallas import tpu as pltpu
from jax.sharding import PartitionSpec as P

TOP = 8
PASSAGE = 128


def expert_rows(rows, gate_rows, wg_single, wu_single, wd_single):
    gate_part = jnp.dot(rows, wg_single, preferred_element_type=jnp.float32)
    up_part = jnp.dot(rows, wu_single, preferred_element_type=jnp.float32)
    hidden = (jax.nn.silu(gate_part) * up_part).astype(jnp.bfloat16)
    result = jnp.dot(hidden, wd_single, preferred_element_type=jnp.float32)
    return (gate_rows.astype(jnp.float32)[:, None] * result).astype(jnp.bfloat16)


def run_expert(slot_rows, slot_gates, wg_single, wu_single, wd_single):
    width = slot_rows.shape[-1]
    rows = slot_rows.reshape(-1, width)
    gate_rows = slot_gates.reshape(-1)
    result = expert_rows(rows, gate_rows, wg_single, wu_single, wd_single)
    return result.reshape(slot_rows.shape)


def slot_shards(tokens, routes, gates, w_gate, w_up, w_down, score_head, doc_ids):
    tok_dev, width = tokens.shape
    experts = lax.axis_size("ep")
    capacity = min(tok_dev, 3 * tok_dev * TOP // (2 * experts))
    flat_routes = routes.reshape(-1)
    onehot = (flat_routes[:, None] == jnp.arange(experts, dtype=jnp.int32)[None, :]).astype(
        jnp.int32
    )
    ranked = jnp.cumsum(onehot, axis=0)
    slot = jnp.sum(ranked * onehot, axis=1) - 1
    destination = flat_routes * capacity + slot
    repeated = jnp.repeat(tokens, TOP, axis=0)
    send_rows = jnp.zeros((experts * capacity, width), jnp.bfloat16).at[destination].set(repeated)
    send_gates = (
        jnp.zeros((experts * capacity,), jnp.bfloat16).at[destination].set(gates.reshape(-1))
    )
    recv_rows, recv_gates = (
        lax.all_to_all(
            send_rows.reshape(experts, capacity, width),
            "ep",
            split_axis=0,
            concat_axis=0,
            tiled=True,
        ),
        lax.all_to_all(
            send_gates.reshape(experts, capacity), "ep", split_axis=0, concat_axis=0, tiled=True
        ),
    )
    wg_single = w_gate[0]
    wu_single = w_up[0]
    wd_single = w_down[0]
    results = run_expert(recv_rows, recv_gates, wg_single, wu_single, wd_single)
    returned = lax.all_to_all(results, "ep", split_axis=0, concat_axis=0, tiled=True)
    returned_flat = returned.reshape(experts * capacity, width)
    gathered = returned_flat[destination].astype(jnp.float32).reshape(tok_dev, TOP, width)
    mixed = jnp.sum(gathered, axis=1).astype(jnp.bfloat16)
    token_score = jnp.dot(mixed.astype(jnp.float32), score_head, precision=lax.Precision.HIGHEST)
    passage_score = token_score.reshape(-1, PASSAGE).sum(axis=1) / math.sqrt(PASSAGE)
    doc_count = lax.axis_size("ep") * lax.axis_size("dp") * tok_dev // PASSAGE // 4
    doc_range = jnp.arange(doc_count, dtype=jnp.int32)[None, :]
    all_scores, all_docs = (
        lax.all_gather(passage_score, ("ep", "dp"), axis=0, tiled=True),
        lax.all_gather(doc_ids.astype(jnp.float32), ("ep", "dp"), axis=0, tiled=True),
    )
    member = all_docs[:, None] == doc_range.astype(jnp.float32)
    column = all_scores[:, None]
    passage_index = jnp.arange(all_scores.shape[0], dtype=jnp.int32)[:, None]
    max_score = jnp.where(member, column, -1e30).max(axis=0)
    sum_score = jnp.where(member, column, 0.0).sum(axis=0)
    first_index = jnp.where(member, passage_index, all_scores.shape[0]).min(axis=0)
    first_score = jnp.where(member & (passage_index == first_index[None, :]), column, 0.0).sum(
        axis=0
    )
    return (mixed, jnp.stack([max_score, first_score, sum_score]))


def pool(all_scores, all_docs, doc_count):
    doc_range = jnp.arange(doc_count, dtype=jnp.int32)[None, :]
    member = all_docs[:, None] == doc_range.astype(jnp.float32)
    column = all_scores[:, None]
    passage_index = jnp.arange(all_scores.shape[0], dtype=jnp.int32)[:, None]
    max_score = jnp.where(member, column, -1e30).max(axis=0)
    sum_score = jnp.where(member, column, 0.0).sum(axis=0)
    first_index = jnp.where(member, passage_index, all_scores.shape[0]).min(axis=0)
    first_score = jnp.where(member & (passage_index == first_index[None, :]), column, 0.0).sum(
        axis=0
    )
    return jnp.stack([max_score, first_score, sum_score])


LANES = 128


def tile_of(extent, most):
    return most if extent % most == 0 else extent


def expert_kernel(
    slot, xa, xb, wg0, wu0, wd0, wg1, wu1, wd1, gate, head, after, held,
    outa, outb, score, passed,
    rows, hidden, scale, x_sem,
):
    tok, width = xa.shape
    local = tok // PASSAGE
    out_tile = tile_of(width, 1024)
    blocks = [pl.ds(n * tok, tok) for n in range(2)]
    x_copies = [
        pltpu.make_async_copy(ref, rows.at[blocks[n], :], x_sem.at[n])
        for n, ref in enumerate((xa, xb))
    ]
    for copy in x_copies:
        copy.start()

    diagonal = lax.broadcasted_iota(jnp.int32, (tok, tok), 0) == lax.broadcasted_iota(
        jnp.int32, (tok, tok), 1
    )
    for n in range(2):
        for e in range(2):
            row = gate[pl.ds(2 * slot + n, 1), pl.ds(e * tok, tok)]
            scale[e, blocks[n], :] = jnp.sum(
                jnp.where(diagonal, row, 0.0), axis=1, keepdims=True
            )

    for copy in x_copies:
        copy.wait()
    for e, (wg, wu) in enumerate(((wg0, wu0), (wg1, wu1))):
        gate_part = jnp.dot(rows[...], wg[...], preferred_element_type=jnp.float32)
        up_part = jnp.dot(rows[...], wu[...], preferred_element_type=jnp.float32)
        value = gate_part / (1.0 + jnp.exp(-gate_part)) * up_part
        hidden[e] = value.astype(jnp.bfloat16)

    totals = [jnp.zeros((1, LANES), jnp.float32) for _ in range(2 * local)]
    for j in range(width // out_tile):
        columns = pl.ds(j * out_tile, out_tile)
        weighted = sum(
            scale[e] * jnp.dot(hidden[e], wd[:, columns], preferred_element_type=jnp.float32)
            for e, wd in enumerate((wd0, wd1))
        )
        rounded = weighted.astype(jnp.bfloat16)
        outa[:, columns] = rounded[:tok]
        outb[:, columns] = rounded[tok:]
        scored = weighted * head[:, columns]
        lanes = sum(
            scored[:, k * LANES : (k + 1) * LANES] for k in range(out_tile // LANES)
        )
        for p in range(2 * local):
            totals[p] += jnp.sum(lanes[p * PASSAGE : (p + 1) * PASSAGE], axis=0, keepdims=True)
    for p in range(2 * local):
        score[pl.ds(p, 1), :] = totals[p]


def load_kernel(count, *refs):
    refs = refs[-2 * count - 1 :]
    copies = [
        pltpu.make_async_copy(src, dst, refs[-1].at[n])
        for n, (src, dst) in enumerate(zip(refs[:count], refs[count:-1]))
    ]
    for copy in copies:
        copy.start()
    for copy in copies:
        copy.wait()


def load(arrays, *firsts):
    arrays = [pltpu.with_memory_space_constraint(a, pltpu.HBM) for a in arrays]
    return pl.pallas_call(
        functools.partial(load_kernel, len(arrays)),
        in_specs=[pl.BlockSpec(memory_space=pl.ANY)] * (len(firsts) + len(arrays)),
        out_specs=[pl.BlockSpec(memory_space=pltpu.VMEM)] * len(arrays),
        out_shape=[pltpu.VMEM(a.shape, a.dtype) for a in arrays],
        scratch_shapes=[pltpu.SemaphoreType.DMA((len(arrays),))],
        compiler_params=pltpu.CompilerParams(vmem_limit_bytes=2**20),
        name="load",
    )(*firsts, *arrays)


def tie_kernel(*refs):
    pass


def tie(value, *firsts):
    anywhere = pl.BlockSpec(memory_space=pl.ANY)
    return pl.pallas_call(
        tie_kernel,
        in_specs=[anywhere] * (1 + len(firsts)),
        out_specs=anywhere,
        out_shape=jax.ShapeDtypeStruct(value.shape, value.dtype),
        input_output_aliases={len(firsts): 0},
        compiler_params=pltpu.CompilerParams(vmem_limit_bytes=2**20),
        name="tie",
    )(*firsts, value)


def expert_call(slot, blocks, weights, gate, head, after, held):
    tok, width = blocks[0].shape
    ff = weights[0].shape[1]
    local = tok // PASSAGE
    anywhere = pl.BlockSpec(memory_space=pl.ANY)
    vmem = pl.BlockSpec(memory_space=pltpu.VMEM)
    bf16 = jnp.bfloat16
    return pl.pallas_call(
        functools.partial(expert_kernel, slot),
        in_specs=[anywhere] * 2 + [vmem] * 8 + [anywhere, anywhere],
        out_specs=[vmem, vmem, vmem, anywhere],
        out_shape=[
            pltpu.VMEM((tok, width), bf16),
            pltpu.VMEM((tok, width), bf16),
            jax.ShapeDtypeStruct((2 * local, LANES), jnp.float32),
            jax.ShapeDtypeStruct(held.shape, held.dtype),
        ],
        input_output_aliases={11: 3},
        scratch_shapes=[
            pltpu.VMEM((2 * tok, width), bf16),
            pltpu.VMEM((2, 2 * tok, ff), bf16),
            pltpu.VMEM((2, 2 * tok, 1), jnp.float32),
            pltpu.SemaphoreType.DMA((2,)),
        ],
        compiler_params=pltpu.CompilerParams(vmem_limit_bytes=16 * 2**20),
        cost_estimate=pl.CostEstimate(flops=1, bytes_accessed=1, transcendentals=0),
        name="expert",
    )(*blocks, *weights, gate, head, after, held)


def dense_shards(tokens, routes, gates, w_gate, w_up, w_down, score_head, doc_ids):
    tok_dev, width = tokens.shape
    experts = lax.axis_size("ep")
    groups = lax.axis_size("dp")
    local = tok_dev // PASSAGE
    ring = experts // 4
    me = lax.axis_index("ep")
    places = [*range(0, ring, 2), *reversed(range(1, ring, 2))]
    onward = lambda v: lax.ppermute(
        v,
        "ep",
        [
            (4 * places[n] + i, 4 * places[(n + 1) % ring] + i)
            for n in range(ring)
            for i in range(4)
        ],
    )
    across = lambda v: lax.ppermute(v, "ep", [(i, i ^ 2) for i in range(experts)])
    sibling = lambda v: lax.ppermute(v, "ep", [(i, i ^ 1) for i in range(experts)])

    own = (w_gate[0], w_up[0], w_down[0])

    cores = [[2 * n + core for n in range(experts // 2)] for core in range(2)]
    target = jnp.arange(experts, dtype=jnp.int32)
    wanted = (target // 2 * 2 + me % 2) ^ target % 2
    chosen = routes.T[:, None, :] == wanted[None, :, None]
    sent_gates = jnp.where(chosen, gates.T[:, None, :], jnp.bfloat16(0)).sum(axis=0)
    sent_gates = sent_gates.reshape(experts // 2, 2 * tok_dev)
    gate_rows = lax.all_to_all(
        sent_gates, "ep", split_axis=0, concat_axis=0, tiled=True, axis_index_groups=cores
    )
    row = jnp.arange(2 * ring, dtype=jnp.int32)
    z = me // 4
    at = jnp.where(z % 2 == 0, z // 2, ring - (z + 1) // 2)
    back = lax.rem(at - row // 2 + ring, ring)
    back = jnp.where(back < (ring + 1) // 2, 2 * back, 2 * (ring - back) - 1)
    order = back * 4 + (me % 4 ^ row % 2 * 2)
    position = order[:, None] == jnp.arange(experts, dtype=jnp.int32)[None, :]
    slot_gates = gate_rows.astype(jnp.float32)[order // 2]

    near = [tokens]
    coming = [onward(tokens)]
    far = [across(tokens)]

    def step(*meanwhile):
        near.append(tie(coming[-1], far[-1], *meanwhile))
        if len(near) < ring:
            coming.append(onward(near[-1]))
            far.append(across(near[-1]))
        else:
            far.append(onward(far[-1]))

    head = score_head[None, :]
    scores = [None] * ring
    mine = [None] * ring
    other = [None] * ring

    def work(s, after, held):
        mine[s], other[s], scores[s], passed = expert_call(
            s, (near[s], far[s]), weights, slot_gates, head, after, held
        )
        return passed

    step(slot_gates)
    weights = load(own, slot_gates)
    step(weights[0])
    weights = weights + load([sibling(w) for w in own], slot_gates)
    weights = [pltpu.with_memory_space_constraint(w, pltpu.VMEM) for w in weights]
    held = jnp.zeros((8, LANES), jnp.float32)
    turns = [1, 0, *range(2, ring)]
    for n, s in enumerate(turns):
        if n == ring - 1:
            other[0] = work(s, held, other[0])
        else:
            held = work(s, near[-1], held)
        if len(near) < ring:
            step(scores[s])
    carried = None
    sent = []
    for s in [*range(1, ring), 0]:
        total = mine[s].astype(jnp.float32) + across(other[s]).astype(jnp.float32)
        if carried is not None:
            total = total + carried.astype(jnp.float32)
        total = total.astype(jnp.bfloat16)
        if s == ring - 1:
            other[0] = tie(other[0], total)
            total = tie(total, other[0])
        if s > 0:
            carried = onward(total)
            sent.append(total)
    mixed = total

    slot_scores = jnp.stack(scores).sum(axis=2).reshape(2 * ring, local) / math.sqrt(PASSAGE)
    part_score = jnp.where(position[:, :, None], slot_scores[:, None, :], 0.0).sum(axis=0)
    told = jnp.concatenate([part_score.reshape(-1), doc_ids.astype(jnp.float32)])
    told = jnp.pad(told, (0, -told.shape[0] % LANES))[None, :]
    told = tie(told, sent[-2])
    heard = lax.all_to_all(
        jnp.broadcast_to(told, (experts * groups, told.shape[1])),
        ("ep", "dp"),
        split_axis=0,
        concat_axis=0,
        tiled=True,
    )
    count = experts * local
    all_scores = heard[:, :count].reshape(experts, groups, experts, local).sum(axis=0)
    all_scores = all_scores.transpose(1, 0, 2).reshape(-1)
    all_docs = heard[:, count : count + local].reshape(-1)
    return (mixed, pool(all_scores, all_docs, count * groups // 4))


def shards(tokens, *rest):
    tok_dev = tokens.shape[0]
    experts = lax.axis_size("ep")
    capacity = min(tok_dev, 3 * tok_dev * TOP // (2 * experts))
    dense = 2 * capacity >= tok_dev and experts % 4 == 0 and tok_dev % PASSAGE == 0
    return (dense_shards if dense else slot_shards)(tokens, *rest)


def solution(mesh):
    return jax.shard_map(
        shards,
        mesh=mesh,
        in_specs=(
            P(("ep", "dp"), None),
            P(("ep", "dp"), None),
            P(("ep", "dp"), None),
            P("ep", None, None),
            P("ep", None, None),
            P("ep", None, None),
            P(),
            P(("ep", "dp")),
        ),
        out_specs=(P(("ep", "dp"), None), P()),
        check_vma=False,
    )
```

```python
import functools
import math

import jax
import jax.numpy as jnp
from jax import lax
from jax.experimental import pallas as pl
from jax.experimental.pallas import tpu as pltpu
from jax.sharding import PartitionSpec as P

TOP = 8
PASSAGE = 128


def expert_rows(rows, gate_rows, wg_single, wu_single, wd_single):
    gate_part = jnp.dot(rows, wg_single, preferred_element_type=jnp.float32)
    up_part = jnp.dot(rows, wu_single, preferred_element_type=jnp.float32)
    hidden = (jax.nn.silu(gate_part) * up_part).astype(jnp.bfloat16)
    result = jnp.dot(hidden, wd_single, preferred_element_type=jnp.float32)
    return (gate_rows.astype(jnp.float32)[:, None] * result).astype(jnp.bfloat16)


def run_expert(slot_rows, slot_gates, wg_single, wu_single, wd_single):
    width = slot_rows.shape[-1]
    rows = slot_rows.reshape(-1, width)
    gate_rows = slot_gates.reshape(-1)
    result = expert_rows(rows, gate_rows, wg_single, wu_single, wd_single)
    return result.reshape(slot_rows.shape)


def slot_shards(tokens, routes, gates, w_gate, w_up, w_down, score_head, doc_ids):
    tok_dev, width = tokens.shape
    experts = lax.axis_size("ep")
    capacity = min(tok_dev, 3 * tok_dev * TOP // (2 * experts))
    flat_routes = routes.reshape(-1)
    onehot = (flat_routes[:, None] == jnp.arange(experts, dtype=jnp.int32)[None, :]).astype(
        jnp.int32
    )
    ranked = jnp.cumsum(onehot, axis=0)
    slot = jnp.sum(ranked * onehot, axis=1) - 1
    destination = flat_routes * capacity + slot
    repeated = jnp.repeat(tokens, TOP, axis=0)
    send_rows = jnp.zeros((experts * capacity, width), jnp.bfloat16).at[destination].set(repeated)
    send_gates = (
        jnp.zeros((experts * capacity,), jnp.bfloat16).at[destination].set(gates.reshape(-1))
    )
    recv_rows, recv_gates = (
        lax.all_to_all(
            send_rows.reshape(experts, capacity, width),
            "ep",
            split_axis=0,
            concat_axis=0,
            tiled=True,
        ),
        lax.all_to_all(
            send_gates.reshape(experts, capacity), "ep", split_axis=0, concat_axis=0, tiled=True
        ),
    )
    wg_single = w_gate[0]
    wu_single = w_up[0]
    wd_single = w_down[0]
    results = run_expert(recv_rows, recv_gates, wg_single, wu_single, wd_single)
    returned = lax.all_to_all(results, "ep", split_axis=0, concat_axis=0, tiled=True)
    returned_flat = returned.reshape(experts * capacity, width)
    gathered = returned_flat[destination].astype(jnp.float32).reshape(tok_dev, TOP, width)
    mixed = jnp.sum(gathered, axis=1).astype(jnp.bfloat16)
    token_score = jnp.dot(mixed.astype(jnp.float32), score_head, precision=lax.Precision.HIGHEST)
    passage_score = token_score.reshape(-1, PASSAGE).sum(axis=1) / math.sqrt(PASSAGE)
    doc_count = lax.axis_size("ep") * lax.axis_size("dp") * tok_dev // PASSAGE // 4
    doc_range = jnp.arange(doc_count, dtype=jnp.int32)[None, :]
    all_scores, all_docs = (
        lax.all_gather(passage_score, ("ep", "dp"), axis=0, tiled=True),
        lax.all_gather(doc_ids.astype(jnp.float32), ("ep", "dp"), axis=0, tiled=True),
    )
    member = all_docs[:, None] == doc_range.astype(jnp.float32)
    column = all_scores[:, None]
    passage_index = jnp.arange(all_scores.shape[0], dtype=jnp.int32)[:, None]
    max_score = jnp.where(member, column, -1e30).max(axis=0)
    sum_score = jnp.where(member, column, 0.0).sum(axis=0)
    first_index = jnp.where(member, passage_index, all_scores.shape[0]).min(axis=0)
    first_score = jnp.where(member & (passage_index == first_index[None, :]), column, 0.0).sum(
        axis=0
    )
    return (mixed, jnp.stack([max_score, first_score, sum_score]))


def pool(all_scores, all_docs, doc_count):
    doc_range = jnp.arange(doc_count, dtype=jnp.int32)[None, :]
    member = all_docs[:, None] == doc_range.astype(jnp.float32)
    column = all_scores[:, None]
    passage_index = jnp.arange(all_scores.shape[0], dtype=jnp.int32)[:, None]
    max_score = jnp.where(member, column, -1e30).max(axis=0)
    sum_score = jnp.where(member, column, 0.0).sum(axis=0)
    first_index = jnp.where(member, passage_index, all_scores.shape[0]).min(axis=0)
    first_score = jnp.where(member & (passage_index == first_index[None, :]), column, 0.0).sum(
        axis=0
    )
    return jnp.stack([max_score, first_score, sum_score])


LANES = 128


def tile_of(extent, most):
    return most if extent % most == 0 else extent


def expert_kernel(
    slot, xa, xb, wg0, wu0, wd0, wg1, wu1, wd1, gate, head, after, held,
    outa, outb, score, passed,
    rows, hidden, scale, x_sem,
):
    tok, width = xa.shape
    local = tok // PASSAGE
    out_tile = tile_of(width, 1024)
    blocks = [pl.ds(n * tok, tok) for n in range(2)]
    x_copies = [
        pltpu.make_async_copy(ref, rows.at[blocks[n], :], x_sem.at[n])
        for n, ref in enumerate((xa, xb))
    ]
    for copy in x_copies:
        copy.start()

    diagonal = lax.broadcasted_iota(jnp.int32, (tok, tok), 0) == lax.broadcasted_iota(
        jnp.int32, (tok, tok), 1
    )
    for n in range(2):
        for e in range(2):
            row = gate[pl.ds(2 * slot + n, 1), pl.ds(e * tok, tok)]
            scale[e, blocks[n], :] = jnp.sum(
                jnp.where(diagonal, row, 0.0), axis=1, keepdims=True
            )

    for copy in x_copies:
        copy.wait()
    for e, (wg, wu) in enumerate(((wg0, wu0), (wg1, wu1))):
        gate_part = jnp.dot(rows[...], wg[...], preferred_element_type=jnp.float32)
        up_part = jnp.dot(rows[...], wu[...], preferred_element_type=jnp.float32)
        value = gate_part / (1.0 + jnp.exp(-gate_part)) * up_part
        hidden[e] = value.astype(jnp.bfloat16)

    totals = [jnp.zeros((1, LANES), jnp.float32) for _ in range(2 * local)]
    for j in range(width // out_tile):
        columns = pl.ds(j * out_tile, out_tile)
        weighted = sum(
            scale[e] * jnp.dot(hidden[e], wd[:, columns], preferred_element_type=jnp.float32)
            for e, wd in enumerate((wd0, wd1))
        )
        rounded = weighted.astype(jnp.bfloat16)
        outa[:, columns] = rounded[:tok]
        outb[:, columns] = rounded[tok:]
        scored = weighted * head[:, columns]
        lanes = sum(
            scored[:, k * LANES : (k + 1) * LANES] for k in range(out_tile // LANES)
        )
        for p in range(2 * local):
            totals[p] += jnp.sum(lanes[p * PASSAGE : (p + 1) * PASSAGE], axis=0, keepdims=True)
    for p in range(2 * local):
        score[pl.ds(p, 1), :] = totals[p]


def load_kernel(count, *refs):
    refs = refs[-2 * count - 1 :]
    copies = [
        pltpu.make_async_copy(src, dst, refs[-1].at[n])
        for n, (src, dst) in enumerate(zip(refs[:count], refs[count:-1]))
    ]
    for copy in copies:
        copy.start()
    for copy in copies:
        copy.wait()


def load(arrays, *firsts):
    arrays = [pltpu.with_memory_space_constraint(a, pltpu.HBM) for a in arrays]
    return pl.pallas_call(
        functools.partial(load_kernel, len(arrays)),
        in_specs=[pl.BlockSpec(memory_space=pl.ANY)] * (len(firsts) + len(arrays)),
        out_specs=[pl.BlockSpec(memory_space=pltpu.VMEM)] * len(arrays),
        out_shape=[pltpu.VMEM(a.shape, a.dtype) for a in arrays],
        scratch_shapes=[pltpu.SemaphoreType.DMA((len(arrays),))],
        compiler_params=pltpu.CompilerParams(vmem_limit_bytes=2**20),
        name="load",
    )(*firsts, *arrays)


def tie_kernel(*refs):
    pass


def tie(value, *firsts):
    anywhere = pl.BlockSpec(memory_space=pl.ANY)
    return pl.pallas_call(
        tie_kernel,
        in_specs=[anywhere] * (1 + len(firsts)),
        out_specs=anywhere,
        out_shape=jax.ShapeDtypeStruct(value.shape, value.dtype),
        input_output_aliases={len(firsts): 0},
        compiler_params=pltpu.CompilerParams(vmem_limit_bytes=2**20),
        name="tie",
    )(*firsts, value)


def expert_call(slot, blocks, weights, gate, head, after, held):
    tok, width = blocks[0].shape
    ff = weights[0].shape[1]
    local = tok // PASSAGE
    anywhere = pl.BlockSpec(memory_space=pl.ANY)
    vmem = pl.BlockSpec(memory_space=pltpu.VMEM)
    bf16 = jnp.bfloat16
    return pl.pallas_call(
        functools.partial(expert_kernel, slot),
        in_specs=[anywhere] * 2 + [vmem] * 8 + [anywhere, anywhere],
        out_specs=[vmem, vmem, vmem, anywhere],
        out_shape=[
            pltpu.VMEM((tok, width), bf16),
            pltpu.VMEM((tok, width), bf16),
            jax.ShapeDtypeStruct((2 * local, LANES), jnp.float32),
            jax.ShapeDtypeStruct(held.shape, held.dtype),
        ],
        input_output_aliases={11: 3},
        scratch_shapes=[
            pltpu.VMEM((2 * tok, width), bf16),
            pltpu.VMEM((2, 2 * tok, ff), bf16),
            pltpu.VMEM((2, 2 * tok, 1), jnp.float32),
            pltpu.SemaphoreType.DMA((2,)),
        ],
        compiler_params=pltpu.CompilerParams(vmem_limit_bytes=16 * 2**20),
        cost_estimate=pl.CostEstimate(flops=1, bytes_accessed=1, transcendentals=0),
        name="expert",
    )(*blocks, *weights, gate, head, after, held)


def dense_shards(tokens, routes, gates, w_gate, w_up, w_down, score_head, doc_ids):
    tok_dev, width = tokens.shape
    experts = lax.axis_size("ep")
    groups = lax.axis_size("dp")
    local = tok_dev // PASSAGE
    ring = experts // 4
    me = lax.axis_index("ep")
    places = [*range(0, ring, 2), *reversed(range(1, ring, 2))]
    onward = lambda v: lax.ppermute(
        v,
        "ep",
        [
            (4 * places[n] + i, 4 * places[(n + 1) % ring] + i)
            for n in range(ring)
            for i in range(4)
        ],
    )
    across = lambda v: lax.ppermute(v, "ep", [(i, i ^ 2) for i in range(experts)])
    sibling = lambda v: lax.ppermute(v, "ep", [(i, i ^ 1) for i in range(experts)])

    own = (w_gate[0], w_up[0], w_down[0])

    cores = [[2 * n + core for n in range(experts // 2)] for core in range(2)]
    target = jnp.arange(experts, dtype=jnp.int32)
    wanted = (target // 2 * 2 + me % 2) ^ target % 2
    chosen = routes.T[:, None, :] == wanted[None, :, None]
    sent_gates = jnp.where(chosen, gates.T[:, None, :], jnp.bfloat16(0)).sum(axis=0)
    sent_gates = sent_gates.reshape(experts // 2, 2 * tok_dev)
    gate_rows = lax.all_to_all(
        sent_gates, "ep", split_axis=0, concat_axis=0, tiled=True, axis_index_groups=cores
    )
    row = jnp.arange(2 * ring, dtype=jnp.int32)
    z = me // 4
    at = jnp.where(z % 2 == 0, z // 2, ring - (z + 1) // 2)
    back = lax.rem(at - row // 2 + ring, ring)
    back = jnp.where(back < (ring + 1) // 2, 2 * back, 2 * (ring - back) - 1)
    order = back * 4 + (me % 4 ^ row % 2 * 2)
    position = order[:, None] == jnp.arange(experts, dtype=jnp.int32)[None, :]
    slot_gates = gate_rows.astype(jnp.float32)[order // 2]

    near = [tokens]
    coming = [onward(tokens)]
    far = [across(tokens)]

    def step(*meanwhile):
        near.append(tie(coming[-1], far[-1], *meanwhile))
        if len(near) < ring:
            coming.append(onward(near[-1]))
            far.append(across(near[-1]))
        else:
            far.append(onward(far[-1]))

    head = score_head[None, :]
    scores = [None] * ring
    mine = [None] * ring
    other = [None] * ring

    def work(s, after, held):
        mine[s], other[s], scores[s], passed = expert_call(
            s, (near[s], far[s]), weights, slot_gates, head, after, held
        )
        return passed

    step(slot_gates)
    weights = load(own, slot_gates)
    step(weights[0])
    weights = weights + load([sibling(w) for w in own], slot_gates)
    weights = [pltpu.with_memory_space_constraint(w, pltpu.VMEM) for w in weights]
    held = jnp.zeros((8, LANES), jnp.float32)
    for s in range(1, ring):
        held = work(s, near[-1], held)
        if len(near) < ring:
            step(scores[s])
    carried = None
    sent = []
    for s in [*range(1, ring), 0]:
        total = mine[s].astype(jnp.float32) + across(other[s]).astype(jnp.float32)
        if carried is not None:
            total = total + carried.astype(jnp.float32)
        total = total.astype(jnp.bfloat16)
        if s == ring - 2:
            work(0, total, held)
        if s == ring - 1:
            other[0] = tie(other[0], total)
            total = tie(total, other[0])
        if s > 0:
            carried = onward(total)
            sent.append(total)
    mixed = total

    slot_scores = jnp.stack(scores).sum(axis=2).reshape(2 * ring, local) / math.sqrt(PASSAGE)
    part_score = jnp.where(position[:, :, None], slot_scores[:, None, :], 0.0).sum(axis=0)
    told = jnp.concatenate([part_score.reshape(-1), doc_ids.astype(jnp.float32)])
    told = jnp.pad(told, (0, -told.shape[0] % LANES))[None, :]
    told = tie(told, sent[-1])
    heard = lax.all_to_all(
        jnp.broadcast_to(told, (experts * groups, told.shape[1])),
        ("ep", "dp"),
        split_axis=0,
        concat_axis=0,
        tiled=True,
    )
    count = experts * local
    all_scores = heard[:, :count].reshape(experts, groups, experts, local).sum(axis=0)
    all_scores = all_scores.transpose(1, 0, 2).reshape(-1)
    all_docs = heard[:, count : count + local].reshape(-1)
    return (mixed, pool(all_scores, all_docs, count * groups // 4))


def shards(tokens, *rest):
    tok_dev = tokens.shape[0]
    experts = lax.axis_size("ep")
    capacity = min(tok_dev, 3 * tok_dev * TOP // (2 * experts))
    dense = 2 * capacity >= tok_dev and experts % 4 == 0 and tok_dev % PASSAGE == 0
    return (dense_shards if dense else slot_shards)(tokens, *rest)


def solution(mesh):
    return jax.shard_map(
        shards,
        mesh=mesh,
        in_specs=(
            P(("ep", "dp"), None),
            P(("ep", "dp"), None),
            P(("ep", "dp"), None),
            P("ep", None, None),
            P("ep", None, None),
            P("ep", None, None),
            P(),
            P(("ep", "dp")),
        ),
        out_specs=(P(("ep", "dp"), None), P()),
        check_vma=False,
    )
```

```python
import functools
import math

import jax
import jax.numpy as jnp
from jax import lax
from jax.experimental import pallas as pl
from jax.experimental.pallas import tpu as pltpu
from jax.sharding import PartitionSpec as P

TOP = 8
PASSAGE = 128


def expert_rows(rows, gate_rows, wg_single, wu_single, wd_single):
    gate_part = jnp.dot(rows, wg_single, preferred_element_type=jnp.float32)
    up_part = jnp.dot(rows, wu_single, preferred_element_type=jnp.float32)
    hidden = (jax.nn.silu(gate_part) * up_part).astype(jnp.bfloat16)
    result = jnp.dot(hidden, wd_single, preferred_element_type=jnp.float32)
    return (gate_rows.astype(jnp.float32)[:, None] * result).astype(jnp.bfloat16)


def run_expert(slot_rows, slot_gates, wg_single, wu_single, wd_single):
    width = slot_rows.shape[-1]
    rows = slot_rows.reshape(-1, width)
    gate_rows = slot_gates.reshape(-1)
    result = expert_rows(rows, gate_rows, wg_single, wu_single, wd_single)
    return result.reshape(slot_rows.shape)


def slot_shards(tokens, routes, gates, w_gate, w_up, w_down, score_head, doc_ids):
    tok_dev, width = tokens.shape
    experts = lax.axis_size("ep")
    capacity = min(tok_dev, 3 * tok_dev * TOP // (2 * experts))
    flat_routes = routes.reshape(-1)
    onehot = (flat_routes[:, None] == jnp.arange(experts, dtype=jnp.int32)[None, :]).astype(
        jnp.int32
    )
    ranked = jnp.cumsum(onehot, axis=0)
    slot = jnp.sum(ranked * onehot, axis=1) - 1
    destination = flat_routes * capacity + slot
    repeated = jnp.repeat(tokens, TOP, axis=0)
    send_rows = jnp.zeros((experts * capacity, width), jnp.bfloat16).at[destination].set(repeated)
    send_gates = (
        jnp.zeros((experts * capacity,), jnp.bfloat16).at[destination].set(gates.reshape(-1))
    )
    recv_rows, recv_gates = (
        lax.all_to_all(
            send_rows.reshape(experts, capacity, width),
            "ep",
            split_axis=0,
            concat_axis=0,
            tiled=True,
        ),
        lax.all_to_all(
            send_gates.reshape(experts, capacity), "ep", split_axis=0, concat_axis=0, tiled=True
        ),
    )
    wg_single = w_gate[0]
    wu_single = w_up[0]
    wd_single = w_down[0]
    results = run_expert(recv_rows, recv_gates, wg_single, wu_single, wd_single)
    returned = lax.all_to_all(results, "ep", split_axis=0, concat_axis=0, tiled=True)
    returned_flat = returned.reshape(experts * capacity, width)
    gathered = returned_flat[destination].astype(jnp.float32).reshape(tok_dev, TOP, width)
    mixed = jnp.sum(gathered, axis=1).astype(jnp.bfloat16)
    token_score = jnp.dot(mixed.astype(jnp.float32), score_head, precision=lax.Precision.HIGHEST)
    passage_score = token_score.reshape(-1, PASSAGE).sum(axis=1) / math.sqrt(PASSAGE)
    doc_count = lax.axis_size("ep") * lax.axis_size("dp") * tok_dev // PASSAGE // 4
    doc_range = jnp.arange(doc_count, dtype=jnp.int32)[None, :]
    all_scores, all_docs = (
        lax.all_gather(passage_score, ("ep", "dp"), axis=0, tiled=True),
        lax.all_gather(doc_ids.astype(jnp.float32), ("ep", "dp"), axis=0, tiled=True),
    )
    member = all_docs[:, None] == doc_range.astype(jnp.float32)
    column = all_scores[:, None]
    passage_index = jnp.arange(all_scores.shape[0], dtype=jnp.int32)[:, None]
    max_score = jnp.where(member, column, -1e30).max(axis=0)
    sum_score = jnp.where(member, column, 0.0).sum(axis=0)
    first_index = jnp.where(member, passage_index, all_scores.shape[0]).min(axis=0)
    first_score = jnp.where(member & (passage_index == first_index[None, :]), column, 0.0).sum(
        axis=0
    )
    return (mixed, jnp.stack([max_score, first_score, sum_score]))


def pool(all_scores, all_docs, doc_count):
    doc_range = jnp.arange(doc_count, dtype=jnp.int32)[None, :]
    member = all_docs[:, None] == doc_range.astype(jnp.float32)
    column = all_scores[:, None]
    passage_index = jnp.arange(all_scores.shape[0], dtype=jnp.int32)[:, None]
    max_score = jnp.where(member, column, -1e30).max(axis=0)
    sum_score = jnp.where(member, column, 0.0).sum(axis=0)
    first_index = jnp.where(member, passage_index, all_scores.shape[0]).min(axis=0)
    first_score = jnp.where(member & (passage_index == first_index[None, :]), column, 0.0).sum(
        axis=0
    )
    return jnp.stack([max_score, first_score, sum_score])


LANES = 128


def tile_of(extent, most):
    return most if extent % most == 0 else extent


def expert_kernel(
    slot, xa, xb, wg0, wu0, wd0, wg1, wu1, wd1, gate, head, after, held,
    outa, outb, score, passed,
    rows, hidden, scale, x_sem,
):
    tok, width = xa.shape
    local = tok // PASSAGE
    out_tile = tile_of(width, 1024)
    blocks = [pl.ds(n * tok, tok) for n in range(2)]
    x_copies = [
        pltpu.make_async_copy(ref, rows.at[blocks[n], :], x_sem.at[n])
        for n, ref in enumerate((xa, xb))
    ]
    for copy in x_copies:
        copy.start()

    diagonal = lax.broadcasted_iota(jnp.int32, (tok, tok), 0) == lax.broadcasted_iota(
        jnp.int32, (tok, tok), 1
    )
    for n in range(2):
        for e in range(2):
            row = gate[pl.ds(2 * slot + n, 1), pl.ds(e * tok, tok)]
            scale[e, blocks[n], :] = jnp.sum(
                jnp.where(diagonal, row, 0.0), axis=1, keepdims=True
            )

    for copy in x_copies:
        copy.wait()
    for e, (wg, wu) in enumerate(((wg0, wu0), (wg1, wu1))):
        ff_tile = tile_of(wg.shape[1], 256)
        for j in range(wg.shape[1] // ff_tile):
            columns = pl.ds(j * ff_tile, ff_tile)
            gate_part = jnp.dot(rows[...], wg[:, columns], preferred_element_type=jnp.float32)
            up_part = jnp.dot(rows[...], wu[:, columns], preferred_element_type=jnp.float32)
            value = gate_part / (1.0 + jnp.exp(-gate_part)) * up_part
            hidden[e, :, columns] = value.astype(jnp.bfloat16)

    totals = [jnp.zeros((1, LANES), jnp.float32) for _ in range(2 * local)]
    for j in range(width // out_tile):
        columns = pl.ds(j * out_tile, out_tile)
        weighted = sum(
            scale[e] * jnp.dot(hidden[e], wd[:, columns], preferred_element_type=jnp.float32)
            for e, wd in enumerate((wd0, wd1))
        )
        rounded = weighted.astype(jnp.bfloat16)
        outa[:, columns] = rounded[:tok]
        outb[:, columns] = rounded[tok:]
        scored = weighted * head[:, columns]
        lanes = sum(
            scored[:, k * LANES : (k + 1) * LANES] for k in range(out_tile // LANES)
        )
        for p in range(2 * local):
            totals[p] += jnp.sum(lanes[p * PASSAGE : (p + 1) * PASSAGE], axis=0, keepdims=True)
    for p in range(2 * local):
        score[pl.ds(p, 1), :] = totals[p]


def load_kernel(count, *refs):
    refs = refs[-2 * count - 1 :]
    copies = [
        pltpu.make_async_copy(src, dst, refs[-1].at[n])
        for n, (src, dst) in enumerate(zip(refs[:count], refs[count:-1]))
    ]
    for copy in copies:
        copy.start()
    for copy in copies:
        copy.wait()


def load(arrays, *firsts):
    arrays = [pltpu.with_memory_space_constraint(a, pltpu.HBM) for a in arrays]
    return pl.pallas_call(
        functools.partial(load_kernel, len(arrays)),
        in_specs=[pl.BlockSpec(memory_space=pl.ANY)] * (len(firsts) + len(arrays)),
        out_specs=[pl.BlockSpec(memory_space=pltpu.VMEM)] * len(arrays),
        out_shape=[pltpu.VMEM(a.shape, a.dtype) for a in arrays],
        scratch_shapes=[pltpu.SemaphoreType.DMA((len(arrays),))],
        compiler_params=pltpu.CompilerParams(vmem_limit_bytes=2**20),
        name="load",
    )(*firsts, *arrays)


def tie_kernel(*refs):
    pass


def tie(value, *firsts):
    anywhere = pl.BlockSpec(memory_space=pl.ANY)
    return pl.pallas_call(
        tie_kernel,
        in_specs=[anywhere] * (1 + len(firsts)),
        out_specs=anywhere,
        out_shape=jax.ShapeDtypeStruct(value.shape, value.dtype),
        input_output_aliases={len(firsts): 0},
        compiler_params=pltpu.CompilerParams(vmem_limit_bytes=2**20),
        name="tie",
    )(*firsts, value)


def expert_call(slot, blocks, weights, gate, head, after, held):
    tok, width = blocks[0].shape
    ff = weights[0].shape[1]
    local = tok // PASSAGE
    anywhere = pl.BlockSpec(memory_space=pl.ANY)
    vmem = pl.BlockSpec(memory_space=pltpu.VMEM)
    bf16 = jnp.bfloat16
    return pl.pallas_call(
        functools.partial(expert_kernel, slot),
        in_specs=[anywhere] * 2 + [vmem] * 8 + [anywhere, anywhere],
        out_specs=[vmem, vmem, vmem, anywhere],
        out_shape=[
            pltpu.VMEM((tok, width), bf16),
            pltpu.VMEM((tok, width), bf16),
            jax.ShapeDtypeStruct((2 * local, LANES), jnp.float32),
            jax.ShapeDtypeStruct(held.shape, held.dtype),
        ],
        input_output_aliases={11: 3},
        scratch_shapes=[
            pltpu.VMEM((2 * tok, width), bf16),
            pltpu.VMEM((2, 2 * tok, ff), bf16),
            pltpu.VMEM((2, 2 * tok, 1), jnp.float32),
            pltpu.SemaphoreType.DMA((2,)),
        ],
        compiler_params=pltpu.CompilerParams(vmem_limit_bytes=16 * 2**20),
        cost_estimate=pl.CostEstimate(flops=1, bytes_accessed=1, transcendentals=0),
        name="expert",
    )(*blocks, *weights, gate, head, after, held)


def dense_shards(tokens, routes, gates, w_gate, w_up, w_down, score_head, doc_ids):
    tok_dev, width = tokens.shape
    experts = lax.axis_size("ep")
    groups = lax.axis_size("dp")
    local = tok_dev // PASSAGE
    ring = experts // 4
    me = lax.axis_index("ep")
    places = [*range(0, ring, 2), *reversed(range(1, ring, 2))]
    onward = lambda v: lax.ppermute(
        v,
        "ep",
        [
            (4 * places[n] + i, 4 * places[(n + 1) % ring] + i)
            for n in range(ring)
            for i in range(4)
        ],
    )
    across = lambda v: lax.ppermute(v, "ep", [(i, i ^ 2) for i in range(experts)])
    sibling = lambda v: lax.ppermute(v, "ep", [(i, i ^ 1) for i in range(experts)])

    own = (w_gate[0], w_up[0], w_down[0])

    cores = [[2 * n + core for n in range(experts // 2)] for core in range(2)]
    target = jnp.arange(experts, dtype=jnp.int32)
    wanted = (target // 2 * 2 + me % 2) ^ target % 2
    chosen = routes.T[:, None, :] == wanted[None, :, None]
    sent_gates = jnp.where(chosen, gates.T[:, None, :], jnp.bfloat16(0)).sum(axis=0)
    sent_gates = sent_gates.reshape(experts // 2, 2 * tok_dev)
    gate_rows = lax.all_to_all(
        sent_gates, "ep", split_axis=0, concat_axis=0, tiled=True, axis_index_groups=cores
    )
    row = jnp.arange(2 * ring, dtype=jnp.int32)
    z = me // 4
    at = jnp.where(z % 2 == 0, z // 2, ring - (z + 1) // 2)
    back = lax.rem(at - row // 2 + ring, ring)
    back = jnp.where(back < (ring + 1) // 2, 2 * back, 2 * (ring - back) - 1)
    order = back * 4 + (me % 4 ^ row % 2 * 2)
    position = order[:, None] == jnp.arange(experts, dtype=jnp.int32)[None, :]
    slot_gates = gate_rows.astype(jnp.float32)[order // 2]

    near = [tokens]
    coming = [onward(tokens)]
    far = [across(tokens)]

    def step(*meanwhile):
        near.append(tie(coming[-1], far[-1], *meanwhile))
        if len(near) < ring:
            coming.append(onward(near[-1]))
            far.append(across(near[-1]))
        else:
            far.append(onward(far[-1]))

    head = score_head[None, :]
    scores = [None] * ring
    mine = [None] * ring
    other = [None] * ring

    def work(s, after, held):
        mine[s], other[s], scores[s], passed = expert_call(
            s, (near[s], far[s]), weights, slot_gates, head, after, held
        )
        return passed

    step(slot_gates)
    weights = load(own, slot_gates)
    step(weights[0])
    weights = weights + load([sibling(w) for w in own], slot_gates)
    weights = [pltpu.with_memory_space_constraint(w, pltpu.VMEM) for w in weights]
    held = jnp.zeros((8, LANES), jnp.float32)
    turns = [1, 0, *range(2, ring)]
    for n, s in enumerate(turns):
        if n == ring - 1:
            other[0] = work(s, held, other[0])
        else:
            held = work(s, near[-1], held)
        if len(near) < ring:
            step(scores[s])
    carried = None
    sent = []
    for s in [*range(1, ring), 0]:
        total = mine[s].astype(jnp.float32) + across(other[s]).astype(jnp.float32)
        if carried is not None:
            total = total + carried.astype(jnp.float32)
        total = total.astype(jnp.bfloat16)
        if s == ring - 1:
            other[0] = tie(other[0], total)
            total = tie(total, other[0])
        if s > 0:
            carried = onward(total)
            sent.append(total)
    mixed = total

    slot_scores = jnp.stack(scores).sum(axis=2).reshape(2 * ring, local) / math.sqrt(PASSAGE)
    part_score = jnp.where(position[:, :, None], slot_scores[:, None, :], 0.0).sum(axis=0)
    told = jnp.concatenate([part_score.reshape(-1), doc_ids.astype(jnp.float32)])
    told = jnp.pad(told, (0, -told.shape[0] % LANES))[None, :]
    told = tie(told, sent[-2])
    heard = lax.all_to_all(
        jnp.broadcast_to(told, (experts * groups, told.shape[1])),
        ("ep", "dp"),
        split_axis=0,
        concat_axis=0,
        tiled=True,
    )
    count = experts * local
    all_scores = heard[:, :count].reshape(experts, groups, experts, local).sum(axis=0)
    all_scores = all_scores.transpose(1, 0, 2).reshape(-1)
    all_docs = heard[:, count : count + local].reshape(-1)
    return (mixed, pool(all_scores, all_docs, count * groups // 4))


def shards(tokens, *rest):
    tok_dev = tokens.shape[0]
    experts = lax.axis_size("ep")
    capacity = min(tok_dev, 3 * tok_dev * TOP // (2 * experts))
    dense = 2 * capacity >= tok_dev and experts % 4 == 0 and tok_dev % PASSAGE == 0
    return (dense_shards if dense else slot_shards)(tokens, *rest)


def solution(mesh):
    return jax.shard_map(
        shards,
        mesh=mesh,
        in_specs=(
            P(("ep", "dp"), None),
            P(("ep", "dp"), None),
            P(("ep", "dp"), None),
            P("ep", None, None),
            P("ep", None, None),
            P("ep", None, None),
            P(),
            P(("ep", "dp")),
        ),
        out_specs=(P(("ep", "dp"), None), P()),
        check_vma=False,
    )
```
